32 devices in a mesh: mat: 4 (over y, x), shard: 8 (over z, core).
Axes of the slice: x: 2, y: 2, z: 4, core: 2. Of those that a mesh axis runs over, the one named last changes fastest.
Arguments:
- iterate: bfloat16 [4, 2560, 2560], P('mat', 'shard')
Outputs:
- next_iterate: bfloat16 [4, 2560, 2560], P(None, 'shard')
All inputs are finite; a program needn't handle non-finite values.
Results may differ from the reference program's by a relative error of at most 0.0077.
Values may be sent and summed in bfloat16 or wider, within the bound.
No kernel may reach another device: no remote copies, remote signals or barrier semaphores. Data moves between devices by JAX's collectives and lax.ppermute only.
A program may use at most 128 MiB of HBM per device.

```python
import math
import jax
import jax.numpy as jnp
from jax import lax

ROWS = 2560
COLS = 2560
MATS = 4


def draw_iterate(key, part):
    key = jax.random.fold_in(key, 7)
    key_diag, key_noise = jax.random.split(key)
    diagonal = jax.random.uniform(key_diag, (MATS, ROWS), jnp.float32, 0.4, 0.9)
    noise = jax.random.truncated_normal(key_noise, -4.0, 4.0, (MATS, ROWS, COLS), jnp.float32)
    identity = (jnp.arange(ROWS)[:, None] == jnp.arange(COLS)[None, :]).astype(jnp.float32)
    matrices = diagonal[:, :, None] * identity[None, :, :] + 0.35 / math.sqrt(COLS) * noise
    return matrices.astype(jnp.bfloat16)


def setup_inputs(seed: int = 0) -> dict:
    arg_keys = jax.random.split(jax.random.key(seed), 2)
    return {
        "iterate": draw_iterate(jax.random.fold_in(arg_keys[1], 71), 0),
    }


coef_a = 3.4445
coef_b = -4.7750
coef_c = 2.0315


def iterate_once(matrix):
    gram_matrix = jnp.dot(matrix, matrix.T, preferred_element_type=jnp.float32).astype(jnp.bfloat16)
    squared = jnp.dot(gram_matrix, gram_matrix, preferred_element_type=jnp.float32)
    polynomial = (coef_b * gram_matrix.astype(jnp.float32) + coef_c * squared).astype(jnp.bfloat16)
    product = jnp.dot(polynomial, matrix, preferred_element_type=jnp.float32)
    return (coef_a * matrix.astype(jnp.float32) + product).astype(jnp.bfloat16)


def reference(iterate):
    return lax.map(iterate_once, iterate)
```

```python
import jax
import jax.numpy as jnp
from jax import lax
from jax.sharding import PartitionSpec as P

coef_a = 3.4445
coef_b = -4.775
coef_c = 2.0315


def dot_t(left, right):
    return lax.dot_general(
        left, right, (((1,), (1,)), ((), ())), preferred_element_type=jnp.float32
    )


def dot(left, right):
    return jnp.dot(left, right, preferred_element_type=jnp.float32)


def general_shards(iterate):
    own = iterate[0]
    gathered = lax.all_gather(own, "shard", axis=0, tiled=True)
    gram = dot_t(own, gathered).astype(jnp.bfloat16)
    cubic = dot(gram, gathered).astype(jnp.bfloat16)
    squared = dot_t(cubic, gathered)
    polynomial = (coef_b * gram.astype(jnp.float32) + coef_c * squared).astype(jnp.bfloat16)
    product = dot(polynomial, gathered)
    next_rows = (coef_a * own.astype(jnp.float32) + product).astype(jnp.bfloat16)
    return lax.all_gather(next_rows[None], "mat", axis=0, tiled=True)


def line_shards(iterate, row_cuts, column_cuts):
    own = iterate[0]
    rows, columns = own.shape
    place = lax.axis_index("shard") // 2
    outer = (place == 0) | (place == 3)
    mat = lax.axis_index("mat")

    other_core = [(d, d ^ 1) for d in range(8)]
    inwards = [(0, 2), (1, 3), (6, 4), (7, 5)]
    outwards = [(b, a) for a, b in inwards]
    middle = [(2, 4), (3, 5), (4, 2), (5, 3)]
    along_x = [(m, m ^ 1) for m in range(4)]
    along_y = [(m, m ^ 2) for m in range(4)]

    def send(value, axis, pairs):
        return lax.ppermute(value, axis, pairs)

    cut = rows // row_cuts
    own_cuts = [own[k * cut : (k + 1) * cut] for k in range(row_cuts)]
    from_outer = [send(part, "shard", inwards) for part in own_cuts]
    from_inner = [send(part, "shard", middle) for part in own_cuts]
    from_far = [send(part, "shard", middle) for part in from_outer]

    groups = []
    groups.append(own_cuts + [send(own, "shard", other_core)])
    for parts in (from_outer, from_inner, from_far):
        for part in parts:
            groups.append([part, send(part, "shard", other_core)])

    left = jnp.concatenate([own] + from_outer, axis=0)
    whole = jnp.zeros((8 * rows, columns), own.dtype)
    grams = []
    cubic = jnp.zeros(left.shape, jnp.float32)
    start = 0
    for group in groups:
        block = jnp.concatenate(group, axis=0)
        whole = lax.dynamic_update_slice_in_dim(whole, block, start, 0)
        start += block.shape[0]
        gram = dot_t(left, block).astype(jnp.bfloat16)
        cubic = cubic + dot(gram, block)
        grams.append(gram)
    gram = jnp.concatenate(grams, axis=1)
    cubic = cubic.astype(jnp.bfloat16)
    squared = dot_t(cubic, whole)
    polynomial = (coef_b * gram.astype(jnp.float32) + coef_c * squared).astype(jnp.bfloat16)

    width = columns // column_cuts

    def new_columns(first, k):
        part = lax.slice_in_dim(polynomial, first, first + rows, axis=0)
        base = lax.slice(left, (first, k * width), (first + rows, (k + 1) * width))
        product = dot(part, lax.slice_in_dim(whole, k * width, (k + 1) * width, axis=1))
        return (coef_a * base.astype(jnp.float32) + product).astype(jnp.bfloat16)

    for_outer = [new_columns(rows, k) for k in range(column_cuts)]
    returned = [send(part, "shard", outwards) for part in for_outer]
    result = jnp.zeros((4, rows, columns), jnp.bfloat16)

    def place_in(result, index, k, part):
        return lax.dynamic_update_slice(result, part[None], (index, 0, k * width))

    for k in range(column_cuts):
        mine = jnp.where(outer, returned[k], new_columns(0, k))
        by_x = send(mine, "mat", along_x)
        by_y = send(mine, "mat", along_y)
        if k % 2 == 0:
            across = send(by_x, "mat", along_y)
        else:
            across = send(by_y, "mat", along_x)
        result = place_in(result, mat, k, mine)
        result = place_in(result, mat ^ 1, k, by_x)
        result = place_in(result, mat ^ 2, k, by_y)
        result = place_in(result, mat ^ 3, k, across)
    return result


def solution(mesh):
    if (mesh.shape["mat"], mesh.shape["shard"]) == (4, 8):
        def shards(iterate):
            return line_shards(iterate, row_cuts=2, column_cuts=4)
    else:
        shards = general_shards
    return jax.shard_map(
        shards,
        mesh=mesh,
        in_specs=(P("mat", "shard", None),),
        out_specs=P(None, "shard", None),
        check_vma=False,
    )
```

```python
import functools

import jax
import jax.numpy as jnp
from jax import lax
from jax.experimental import pallas as pl
from jax.experimental.pallas import tpu as pltpu
from jax.sharding import PartitionSpec as P

coef_a = 3.4445
coef_b = -4.775
coef_c = 2.0315

TILE = 256
VMEM_LIMIT = 48 * 1024 * 1024


def dot_t(left, right):
    return lax.dot_general(
        left, right, (((1,), (1,)), ((), ())), preferred_element_type=jnp.float32
    )


def dot(left, right):
    return jnp.dot(left, right, preferred_element_type=jnp.float32)


def general_shards(iterate):
    own = iterate[0]
    gathered = lax.all_gather(own, "shard", axis=0, tiled=True)
    gram = dot_t(own, gathered).astype(jnp.bfloat16)
    cubic = dot(gram, gathered).astype(jnp.bfloat16)
    squared = dot_t(cubic, gathered)
    polynomial = (coef_b * gram.astype(jnp.float32) + coef_c * squared).astype(jnp.bfloat16)
    product = dot(polynomial, gathered)
    next_rows = (coef_a * own.astype(jnp.float32) + product).astype(jnp.bfloat16)
    return lax.all_gather(next_rows[None], "mat", axis=0, tiled=True)


def tiles(total):
    return [(s, min(TILE, total - s)) for s in range(0, total, TILE)]


def early_kernel(count, *refs):
    blocks, (gram, cubic, whole, sems) = refs[:count], refs[count:]
    rows = blocks[0].shape[0]
    copies = []
    for k, block in enumerate(blocks):
        copy = pltpu.make_async_copy(block, whole.at[pl.ds(k * rows, rows), :], sems.at[k])
        copy.start()
        copies.append(copy)
    for copy in copies:
        copy.wait()

    def gram_tile(start, width):
        gram[:, pl.ds(start, width)] = dot_t(
            whole[: 2 * rows, :], whole[pl.ds(start, width), :]
        ).astype(jnp.bfloat16)

    full = (count * rows) // TILE

    @pl.loop(0, full)
    def _(n):
        gram_tile(pl.multiple_of(n * TILE, TILE), TILE)

    if full * TILE < count * rows:
        gram_tile(full * TILE, count * rows - full * TILE)

    @pl.loop(0, whole.shape[1] // TILE)
    def _(n):
        at = pl.ds(pl.multiple_of(n * TILE, TILE), TILE)
        cubic[:, at] = dot(gram[...], whole[:, at])


def early_products(blocks):
    count = len(blocks)
    rows, columns = blocks[0].shape
    known = count * rows
    return pl.pallas_call(
        functools.partial(early_kernel, count),
        out_shape=(
            jax.ShapeDtypeStruct((2 * rows, known), jnp.bfloat16),
            jax.ShapeDtypeStruct((2 * rows, columns), jnp.float32),
        ),
        in_specs=[pl.BlockSpec(memory_space=pl.ANY)] * count,
        out_specs=(pl.BlockSpec(memory_space=pltpu.VMEM),) * 2,
        scratch_shapes=[
            pltpu.VMEM((known, columns), jnp.bfloat16),
            pltpu.SemaphoreType.DMA((count,)),
        ],
        compiler_params=pltpu.CompilerParams(vmem_limit_bytes=VMEM_LIMIT),
        cost_estimate=pl.CostEstimate(
            flops=8 * rows * known * columns, bytes_accessed=2 * known * columns, transcendentals=0
        ),
    )(*blocks)


def late_kernel(count, first, widths, *refs):
    blocks, gram_in, cubic_in = refs[:count], refs[count], refs[count + 1]
    outs = refs[count + 2 : count + 2 + len(widths)]
    whole, gram, cubic_sum, cubic, poly, sems = refs[count + 2 + len(widths) :]
    rows, columns = blocks[0].shape
    known = (count - 2) * rows
    mine = pl.ds(first * rows, rows)

    copies = {}

    def fetch(name, source, target):
        copies[name] = pltpu.make_async_copy(source, target, sems.at[len(copies)])
        copies[name].start()

    def fetch_block(k):
        if k not in copies:
            fetch(k, blocks[k], whole.at[pl.ds(k * rows, rows), :])

    fetch_block(count - 2)
    fetch_block(count - 1)
    fetch_block(first)
    fetch("gram", gram_in.at[mine, :], gram.at[:, pl.ds(0, known)])
    fetch("cubic", cubic_in.at[mine, :], cubic_sum)
    for k in range(count):
        fetch_block(k)

    for name in (count - 2, count - 1, first, "gram"):
        copies[name].wait()
    late = dot_t(whole[mine, :], whole[known:, :]).astype(jnp.bfloat16)
    gram[:, pl.ds(known, 2 * rows)] = late
    copies["cubic"].wait()

    @pl.loop(0, columns // TILE)
    def _(n):
        at = pl.ds(pl.multiple_of(n * TILE, TILE), TILE)
        add = dot(gram[:, pl.ds(known, 2 * rows)], whole[pl.ds(known, 2 * rows), at])
        cubic[:, at] = (cubic_sum[:, at] + add).astype(jnp.bfloat16)

    for k in range(count - 2):
        if k != first:
            copies[k].wait()

    @pl.loop(0, count * rows // TILE)
    def _(n):
        at = pl.ds(pl.multiple_of(n * TILE, TILE), TILE)
        squared = dot_t(cubic[...], whole[at, :])
        poly[:, at] = (coef_b * gram[:, at].astype(jnp.float32) + coef_c * squared).astype(
            jnp.bfloat16
        )

    begin = 0
    for out, width in zip(outs, widths):

        @pl.loop(0, width // TILE)
        def _(n, out=out, begin=begin):
            local = pl.ds(pl.multiple_of(n * TILE, TILE), TILE)
            at = pl.ds(pl.multiple_of(begin + n * TILE, TILE), TILE)
            product = dot(poly[...], whole[:, at])
            base = whole[mine, at].astype(jnp.float32)
            out[:, local] = (coef_a * base + product).astype(jnp.bfloat16)

        begin += width


def late_products(blocks, gram, cubic, first, widths):
    count = len(blocks)
    rows, columns = blocks[0].shape
    total = count * rows
    return pl.pallas_call(
        functools.partial(late_kernel, count, first, widths),
        out_shape=tuple(jax.ShapeDtypeStruct((rows, w), jnp.bfloat16) for w in widths),
        in_specs=[pl.BlockSpec(memory_space=pl.ANY)] * (count + 2),
        out_specs=tuple(pl.BlockSpec(memory_space=pltpu.VMEM) for _ in widths),
        scratch_shapes=[
            pltpu.VMEM((total, columns), jnp.bfloat16),
            pltpu.VMEM((rows, total), jnp.bfloat16),
            pltpu.VMEM((rows, columns), jnp.float32),
            pltpu.VMEM((rows, columns), jnp.bfloat16),
            pltpu.VMEM((rows, total), jnp.bfloat16),
            pltpu.SemaphoreType.DMA((count + 2,)),
        ],
        compiler_params=pltpu.CompilerParams(vmem_limit_bytes=VMEM_LIMIT),
        cost_estimate=pl.CostEstimate(
            flops=5 * rows * total * columns, bytes_accessed=2 * total * columns, transcendentals=0
        ),
    )(*blocks, gram, cubic)


def line_shards(iterate, widths):
    own = iterate[0]
    rows, columns = own.shape
    place = lax.axis_index("shard") // 2
    outer = (place == 0) | (place == 3)
    mat = lax.axis_index("mat")

    other_core = [(d, d ^ 1) for d in range(8)]
    inwards = [(0, 2), (1, 3), (6, 4), (7, 5)]
    outwards = [(b, a) for a, b in inwards]
    middle = [(2, 4), (3, 5), (4, 2), (5, 3)]
    along_x = [(m, m ^ 1) for m in range(4)]
    along_y = [(m, m ^ 2) for m in range(4)]

    from_outer = lax.ppermute(own, "shard", inwards)
    from_inner = lax.ppermute(own, "shard", middle)
    from_far = lax.ppermute(from_outer, "shard", middle)

    def swap(block):
        return lax.ppermute(block, "shard", other_core)

    early = [from_outer, own, swap(from_outer), swap(own), from_inner, swap(from_inner)]
    gram, cubic = early_products(early)
    blocks = early + [from_far, swap(from_far)]
    for_outer = late_products(blocks, gram, cubic, 0, widths)
    for_own = late_products(blocks, gram, cubic, 1, widths)

    result = jnp.zeros((4, rows, columns), jnp.bfloat16)
    begin = 0
    onward, onward_axis, onward_at = None, None, None

    def place(result, flip, at, part):
        return lax.dynamic_update_slice(result, part[None], (mat ^ flip, 0, at))

    for k, width in enumerate(widths):
        returned = lax.ppermute(for_outer[k], "shard", outwards)
        mine = jnp.where(outer, returned, for_own[k])
        if onward is not None:
            mine, onward = lax.optimization_barrier((mine, onward))
        by_x = lax.ppermute(mine, "mat", along_x)
        by_y = lax.ppermute(mine, "mat", along_y)
        if onward is not None:
            across = lax.ppermute(onward, "mat", onward_axis)
            result = place(result, 3, onward_at, across)
        for flip, part in enumerate((mine, by_x, by_y)):
            result = place(result, flip, begin, part)
        onward, onward_axis = (by_x, along_y) if k % 2 == 0 else (by_y, along_x)
        onward_at = begin
        begin += width
    across = lax.ppermute(onward, "mat", onward_axis)
    result = place(result, 3, onward_at, across)
    return result


def solution(mesh):
    if (mesh.shape["mat"], mesh.shape["shard"]) == (4, 8):
        def shards(iterate):
            return line_shards(iterate, widths=(512, 512, 768, 768))
    else:
        shards = general_shards
    return jax.shard_map(
        shards,
        mesh=mesh,
        in_specs=(P("mat", "shard", None),),
        out_specs=P(None, "shard", None),
        check_vma=False,
    )
```

```python
import functools

import jax
import jax.numpy as jnp
from jax import lax
from jax.experimental import pallas as pl
from jax.experimental.pallas import tpu as pltpu
from jax.sharding import PartitionSpec as P

coef_a = 3.4445
coef_b = -4.775
coef_c = 2.0315

TILE = 1280
VMEM_LIMIT = 48 * 1024 * 1024


def dot_t(left, right):
    return lax.dot_general(
        left, right, (((1,), (1,)), ((), ())), preferred_element_type=jnp.float32
    )


def dot(left, right):
    return jnp.dot(left, right, preferred_element_type=jnp.float32)


def general_shards(iterate):
    own = iterate[0]
    gathered = lax.all_gather(own, "shard", axis=0, tiled=True)
    gram = dot_t(own, gathered).astype(jnp.bfloat16)
    cubic = dot(gram, gathered).astype(jnp.bfloat16)
    squared = dot_t(cubic, gathered)
    polynomial = (coef_b * gram.astype(jnp.float32) + coef_c * squared).astype(jnp.bfloat16)
    product = dot(polynomial, gathered)
    next_rows = (coef_a * own.astype(jnp.float32) + product).astype(jnp.bfloat16)
    return lax.all_gather(next_rows[None], "mat", axis=0, tiled=True)


def tiles(start, stop):
    return [pl.ds(at, min(TILE, stop - at)) for at in range(start, stop, TILE)]


def early_kernel(count, *refs):
    inner, blocks, (gram, cubic, whole, sems) = refs[0], refs[1 : count + 1], refs[count + 1 :]
    rows, columns = blocks[0].shape

    @pl.when(inner[0] != 0)
    def _():
        copies = []
        for k, block in enumerate(blocks):
            target = whole.at[pl.ds(k * rows, rows), :]
            copy = pltpu.make_async_copy(block, target, sems.at[k])
            copy.start()
            copies.append(copy)
        for copy in copies:
            copy.wait()
        for at in tiles(0, count * rows):
            gram[:, at] = dot_t(whole[: 2 * rows, :], whole[at, :]).astype(jnp.bfloat16)
        for at in tiles(0, columns):
            cubic[:, at] = dot(gram[...], whole[:, at])


def early_products(inner, blocks):
    count = len(blocks)
    rows, columns = blocks[0].shape
    known = count * rows
    return pl.pallas_call(
        functools.partial(early_kernel, count),
        out_shape=(
            jax.ShapeDtypeStruct((2 * rows, known), jnp.bfloat16),
            jax.ShapeDtypeStruct((2 * rows, columns), jnp.float32),
        ),
        in_specs=[pl.BlockSpec(memory_space=pltpu.SMEM)]
        + [pl.BlockSpec(memory_space=pl.ANY)] * count,
        out_specs=(pl.BlockSpec(memory_space=pltpu.VMEM),) * 2,
        scratch_shapes=[
            pltpu.VMEM((known, columns), jnp.bfloat16),
            pltpu.SemaphoreType.DMA((count,)),
        ],
        compiler_params=pltpu.CompilerParams(vmem_limit_bytes=VMEM_LIMIT),
        cost_estimate=pl.CostEstimate(
            flops=8 * rows * known * columns, bytes_accessed=2 * known * columns, transcendentals=0
        ),
    )(inner, *blocks)


def late_kernel(count, first, widths, *refs):
    inner, refs = refs[0], refs[1:]
    blocks, gram_in, cubic_in = refs[:count], refs[count], refs[count + 1]
    outs = refs[count + 2 : count + 2 + len(widths)]
    whole, gram, cubic_sum, cubic, poly, sems = refs[count + 2 + len(widths) :]
    rows, columns = blocks[0].shape
    known = (count - 2) * rows
    mine = pl.ds(first * rows, rows)
    late = pl.ds(known, 2 * rows)

    @pl.when(inner[0] != 0)
    def _():
        copies = {}

        def fetch(name, source, target):
            copies[name] = pltpu.make_async_copy(source, target, sems.at[len(copies)])
            copies[name].start()

        def fetch_block(k):
            if k not in copies:
                fetch(k, blocks[k], whole.at[pl.ds(k * rows, rows), :])

        fetch_block(count - 2)
        fetch_block(count - 1)
        fetch_block(first)
        fetch("gram", gram_in.at[mine, :], gram.at[:, pl.ds(0, known)])
        fetch("cubic", cubic_in.at[mine, :], cubic_sum)
        for k in range(count):
            fetch_block(k)

        for name in (count - 2, count - 1, first, "gram"):
            copies[name].wait()
        gram[:, late] = dot_t(whole[mine, :], whole[late, :]).astype(jnp.bfloat16)
        copies["cubic"].wait()
        for at in tiles(0, columns):
            add = dot(gram[:, late], whole[late, at])
            cubic[:, at] = (cubic_sum[:, at] + add).astype(jnp.bfloat16)

        for k in range(count - 2):
            if k != first:
                copies[k].wait()
        for at in tiles(0, count * rows):
            squared = dot_t(cubic[...], whole[at, :])
            poly[:, at] = (coef_b * gram[:, at].astype(jnp.float32) + coef_c * squared).astype(
                jnp.bfloat16
            )

        begin = 0
        for out, width in zip(outs, widths):
            at = pl.ds(begin, width)
            product = dot(poly[...], whole[:, at])
            base = whole[mine, at].astype(jnp.float32)
            out[...] = (coef_a * base + product).astype(jnp.bfloat16)
            begin += width


def late_products(inner, blocks, gram, cubic, first, widths):
    count = len(blocks)
    rows, columns = blocks[0].shape
    total = count * rows
    return pl.pallas_call(
        functools.partial(late_kernel, count, first, widths),
        out_shape=tuple(jax.ShapeDtypeStruct((rows, w), jnp.bfloat16) for w in widths),
        in_specs=[pl.BlockSpec(memory_space=pltpu.SMEM)]
        + [pl.BlockSpec(memory_space=pl.ANY)] * (count + 2),
        out_specs=tuple(pl.BlockSpec(memory_space=pltpu.VMEM) for _ in widths),
        scratch_shapes=[
            pltpu.VMEM((total, columns), jnp.bfloat16),
            pltpu.VMEM((rows, total), jnp.bfloat16),
            pltpu.VMEM((rows, columns), jnp.float32),
            pltpu.VMEM((rows, columns), jnp.bfloat16),
            pltpu.VMEM((rows, total), jnp.bfloat16),
            pltpu.SemaphoreType.DMA((count + 2,)),
        ],
        compiler_params=pltpu.CompilerParams(vmem_limit_bytes=VMEM_LIMIT),
        cost_estimate=pl.CostEstimate(
            flops=5 * rows * total * columns, bytes_accessed=2 * total * columns, transcendentals=0
        ),
    )(inner, *blocks, gram, cubic)


def line_shards(iterate, widths):
    own = iterate[0]
    rows, columns = own.shape
    place = lax.axis_index("shard") // 2
    outer = (place == 0) | (place == 3)
    mat = lax.axis_index("mat")

    inner = jnp.where(outer, 0, 1).astype(jnp.int32)[None]
    tie = lax.optimization_barrier

    other_core = [(2, 3), (3, 2), (4, 5), (5, 4)]
    inwards = [(0, 2), (1, 3), (6, 4), (7, 5)]
    outwards = [(b, a) for a, b in inwards]
    middle = [(2, 4), (3, 5), (4, 2), (5, 3)]
    along_x = [(m, m ^ 1) for m in range(4)]
    along_y = [(m, m ^ 2) for m in range(4)]

    from_outer = lax.ppermute(own, "shard", inwards)
    from_inner = lax.ppermute(own, "shard", middle)
    from_far = lax.ppermute(from_outer, "shard", middle)

    def swap(block):
        return lax.ppermute(block, "shard", other_core)

    early = [from_outer, own, swap(from_outer), swap(own), from_inner, swap(from_inner)]
    gram, cubic = early_products(inner, early)
    from_far, gram, cubic = tie((from_far, gram, cubic))
    blocks = early + [from_far, swap(from_far)]
    for_outer = list(late_products(inner, blocks, gram, cubic, 0, widths))
    for_own = list(late_products(inner, blocks, gram, cubic, 1, widths))
    for_outer[2], for_outer[3], for_own[0] = tie((for_outer[2], for_outer[3], for_own[0]))

    result = jnp.zeros((4, rows, columns), jnp.bfloat16)

    def place_in(result, flip, at, part):
        return lax.dynamic_update_slice(result, part[None], (mat ^ flip, 0, at))

    begins = [sum(widths[:k]) for k in range(len(widths))]
    first_hop = []

    def send_corner(k):
        by_x, by_y = first_hop[k]
        return lax.ppermute(*((by_x, "mat", along_y) if k % 2 == 0 else (by_y, "mat", along_x)))

    for k in range(len(widths)):
        returned = lax.ppermute(for_outer[k], "shard", outwards)
        here, returned = tie((outer, returned))
        mine = jnp.where(here, returned, for_own[k])
        if k >= 2:
            by_x, by_y = first_hop[k - 2]
            if k % 2 == 0:
                mine, by_x = tie((mine, by_x))
            else:
                mine, by_y = tie((mine, by_y))
            first_hop[k - 2] = (by_x, by_y)
        first_hop.append((lax.ppermute(mine, "mat", along_x), lax.ppermute(mine, "mat", along_y)))
        result = place_in(result, 0, begins[k], mine)
    corners = [send_corner(k) for k in range(len(widths))]
    for k in range(len(widths)):
        by_x, by_y = first_hop[k]
        for flip, part in ((1, by_x), (2, by_y), (3, corners[k])):
            result = place_in(result, flip, begins[k], part)
    return result


def solution(mesh):
    if (mesh.shape["mat"], mesh.shape["shard"]) == (4, 8):
        def shards(iterate):
            return line_shards(iterate, widths=(512, 512, 768, 768))
    else:
        shards = general_shards
    return jax.shard_map(
        shards,
        mesh=mesh,
        in_specs=(P("mat", "shard", None),),
        out_specs=P(None, "shard", None),
        check_vma=False,
    )
```

```python
import functools

import jax
import jax.numpy as jnp
from jax import lax
from jax.experimental import pallas as pl
from jax.experimental.pallas import tpu as pltpu
from jax.sharding import PartitionSpec as P

coef_a = 3.4445
coef_b = -4.775
coef_c = 2.0315

TILE = 1280
VMEM_LIMIT = 48 * 1024 * 1024


def dot_t(left, right):
    return lax.dot_general(
        left, right, (((1,), (1,)), ((), ())), preferred_element_type=jnp.float32
    )


def dot(left, right):
    return jnp.dot(left, right, preferred_element_type=jnp.float32)


def general_shards(iterate):
    own = iterate[0]
    gathered = lax.all_gather(own, "shard", axis=0, tiled=True)
    gram = dot_t(own, gathered).astype(jnp.bfloat16)
    cubic = dot(gram, gathered).astype(jnp.bfloat16)
    squared = dot_t(cubic, gathered)
    polynomial = (coef_b * gram.astype(jnp.float32) + coef_c * squared).astype(jnp.bfloat16)
    product = dot(polynomial, gathered)
    next_rows = (coef_a * own.astype(jnp.float32) + product).astype(jnp.bfloat16)
    return lax.all_gather(next_rows[None], "mat", axis=0, tiled=True)


def tiles(start, stop):
    return [pl.ds(at, min(TILE, stop - at)) for at in range(start, stop, TILE)]


def early_kernel(count, *refs):
    inner, blocks, (gram, cubic, whole, sems) = refs[0], refs[1 : count + 1], refs[count + 1 :]
    rows, columns = blocks[0].shape

    @pl.when(inner[0] != 0)
    def _():
        copies = []
        for k, block in enumerate(blocks):
            target = whole.at[pl.ds(k * rows, rows), :]
            copy = pltpu.make_async_copy(block, target, sems.at[k])
            copy.start()
            copies.append(copy)
        for copy in copies:
            copy.wait()
        for at in tiles(0, count * rows):
            gram[:, at] = dot_t(whole[: 2 * rows, :], whole[at, :]).astype(jnp.bfloat16)
        for at in tiles(0, columns):
            cubic[:, at] = dot(gram[...], whole[:, at])


def early_products(inner, blocks):
    count = len(blocks)
    rows, columns = blocks[0].shape
    known = count * rows
    return pl.pallas_call(
        functools.partial(early_kernel, count),
        out_shape=(
            jax.ShapeDtypeStruct((2 * rows, known), jnp.bfloat16),
            jax.ShapeDtypeStruct((2 * rows, columns), jnp.float32),
        ),
        in_specs=[pl.BlockSpec(memory_space=pltpu.SMEM)]
        + [pl.BlockSpec(memory_space=pl.ANY)] * count,
        out_specs=(pl.BlockSpec(memory_space=pltpu.VMEM),) * 2,
        scratch_shapes=[
            pltpu.VMEM((known, columns), jnp.bfloat16),
            pltpu.SemaphoreType.DMA((count,)),
        ],
        compiler_params=pltpu.CompilerParams(vmem_limit_bytes=VMEM_LIMIT),
        cost_estimate=pl.CostEstimate(
            flops=rows * known, bytes_accessed=2 * rows, transcendentals=0
        ),
    )(inner, *blocks)


def late_kernel(count, first, widths, *refs):
    inner, refs = refs[0], refs[1:]
    blocks, gram_in, cubic_in = refs[:count], refs[count], refs[count + 1]
    outs = refs[count + 2 : count + 2 + len(widths)]
    whole, gram, cubic_sum, cubic, poly, sems = refs[count + 2 + len(widths) :]
    rows, columns = blocks[0].shape
    known = (count - 2) * rows
    mine = pl.ds(first * rows, rows)
    late = pl.ds(known, 2 * rows)

    @pl.when(inner[0] != 0)
    def _():
        copies = {}

        def fetch(name, source, target):
            copies[name] = pltpu.make_async_copy(source, target, sems.at[len(copies)])
            copies[name].start()

        def fetch_block(k):
            if k not in copies:
                fetch(k, blocks[k], whole.at[pl.ds(k * rows, rows), :])

        fetch_block(count - 2)
        fetch_block(count - 1)
        fetch_block(first)
        fetch("gram", gram_in.at[mine, :], gram.at[:, pl.ds(0, known)])
        fetch("cubic", cubic_in.at[mine, :], cubic_sum)
        for k in range(count):
            fetch_block(k)

        for name in (count - 2, count - 1, first, "gram"):
            copies[name].wait()
        gram[:, late] = dot_t(whole[mine, :], whole[late, :]).astype(jnp.bfloat16)
        copies["cubic"].wait()
        for at in tiles(0, columns):
            add = dot(gram[:, late], whole[late, at])
            cubic[:, at] = (cubic_sum[:, at] + add).astype(jnp.bfloat16)

        for k in range(count - 2):
            if k != first:
                copies[k].wait()
        for at in tiles(0, count * rows):
            squared = dot_t(cubic[...], whole[at, :])
            poly[:, at] = (coef_b * gram[:, at].astype(jnp.float32) + coef_c * squared).astype(
                jnp.bfloat16
            )

        begin = 0
        for out, width in zip(outs, widths):
            at = pl.ds(begin, width)
            product = dot(poly[...], whole[:, at])
            base = whole[mine, at].astype(jnp.float32)
            out[...] = (coef_a * base + product).astype(jnp.bfloat16)
            begin += width


def late_products(inner, blocks, gram, cubic, first, widths):
    count = len(blocks)
    rows, columns = blocks[0].shape
    total = count * rows
    return pl.pallas_call(
        functools.partial(late_kernel, count, first, widths),
        out_shape=tuple(jax.ShapeDtypeStruct((rows, w), jnp.bfloat16) for w in widths),
        in_specs=[pl.BlockSpec(memory_space=pltpu.SMEM)]
        + [pl.BlockSpec(memory_space=pl.ANY)] * (count + 2),
        out_specs=tuple(pl.BlockSpec(memory_space=pltpu.VMEM) for _ in widths),
        scratch_shapes=[
            pltpu.VMEM((total, columns), jnp.bfloat16),
            pltpu.VMEM((rows, total), jnp.bfloat16),
            pltpu.VMEM((rows, columns), jnp.float32),
            pltpu.VMEM((rows, columns), jnp.bfloat16),
            pltpu.VMEM((rows, total), jnp.bfloat16),
            pltpu.SemaphoreType.DMA((count + 2,)),
        ],
        compiler_params=pltpu.CompilerParams(vmem_limit_bytes=VMEM_LIMIT),
        cost_estimate=pl.CostEstimate(
            flops=5 * rows * total * columns, bytes_accessed=2 * total * columns, transcendentals=0
        ),
    )(inner, *blocks, gram, cubic)


def put_kernel(places, aliased, *refs):
    matrices, parts = refs[0], refs[1 : 1 + len(places)]
    out, sems = refs[1 + len(places) + aliased :]
    copies = []
    for k, ((flip, at), part) in enumerate(zip(places, parts)):
        target = out.at[matrices[flip], :, pl.ds(at, part.shape[1])]
        copies.append(pltpu.make_async_copy(part, target, sems.at[k]))
        copies[k].start()
    for copy in copies:
        copy.wait()


def put(result, matrices, stage, shape):
    places = [(flip, at) for flip, at, _ in stage]
    parts = [part for _, _, part in stage]
    aliased = result is not None
    return pl.pallas_call(
        functools.partial(put_kernel, places, aliased),
        out_shape=jax.ShapeDtypeStruct(shape, parts[0].dtype),
        in_specs=[pl.BlockSpec(memory_space=pltpu.SMEM)]
        + [pl.BlockSpec(memory_space=pl.ANY)] * len(parts)
        + [pl.BlockSpec(memory_space=pltpu.HBM)] * aliased,
        out_specs=pl.BlockSpec(memory_space=pltpu.HBM),
        scratch_shapes=[pltpu.SemaphoreType.DMA((len(parts),))],
        input_output_aliases={1 + len(parts): 0} if aliased else {},
        compiler_params=pltpu.CompilerParams(vmem_limit_bytes=1024 * 1024),
        cost_estimate=pl.CostEstimate(flops=0, bytes_accessed=1024, transcendentals=0),
    )(matrices, *parts, *([result] if aliased else []))


def line_shards(iterate, widths):
    own = iterate[0]
    rows, columns = own.shape
    place = lax.axis_index("shard") // 2
    outer = (place == 0) | (place == 3)
    mat = lax.axis_index("mat")

    inner = jnp.where(outer, 0, 1).astype(jnp.int32)[None]
    tie = lax.optimization_barrier

    other_core = [(2, 3), (3, 2), (4, 5), (5, 4)]
    inwards = [(0, 2), (1, 3), (6, 4), (7, 5)]
    outwards = [(b, a) for a, b in inwards]
    middle = [(2, 4), (3, 5), (4, 2), (5, 3)]
    along_x = [(m, m ^ 1) for m in range(4)]
    along_y = [(m, m ^ 2) for m in range(4)]

    from_outer = lax.ppermute(own, "shard", inwards)
    from_inner = lax.ppermute(own, "shard", middle)
    from_far = lax.ppermute(from_outer, "shard", middle)

    def swap(block):
        return lax.ppermute(block, "shard", other_core)

    early = [from_outer, own, swap(from_outer), swap(own), from_inner, swap(from_inner)]
    gram, cubic = early_products(inner, early)
    from_far, gram, cubic = tie((from_far, gram, cubic))
    blocks = early + [from_far, swap(from_far)]
    for_outer = list(late_products(inner, blocks, gram, cubic, 0, widths))
    for_own = list(late_products(inner, blocks, gram, cubic, 1, widths))
    result = None
    begin = 0
    stages = []
    for k, width in enumerate(widths):
        half = width // 2
        returned = lax.ppermute(for_outer[k], "shard", outwards)
        mine = tie(jnp.where(outer, returned, for_own[k]))
        by_x = lax.ppermute(mine, "mat", along_x)
        by_y = lax.ppermute(mine, "mat", along_y)
        by_x, by_y = tie((by_x, by_y))
        left_half = lax.ppermute(by_x[:, :half], "mat", along_y)
        right_half = lax.ppermute(by_y[:, half:], "mat", along_x)
        stages.append([(0, begin, mine), (1, begin, by_x), (2, begin, by_y)])
        stages.append([(3, begin, left_half), (3, begin + half, right_half)])
        begin += width
    matrices = mat[None] ^ jnp.arange(4, dtype=jnp.int32)
    order = stages[:1] + [stages[1] + stages[2]] + stages[3:] if len(stages) == 4 else stages
    for stage in order:
        result = put(result, matrices, stage, (4, rows, columns))
    return result


def solution(mesh):
    if (mesh.shape["mat"], mesh.shape["shard"]) == (4, 8):
        def shards(iterate):
            return line_shards(iterate, widths=(1280, 1280))
    else:
        shards = general_shards
    return jax.shard_map(
        shards,
        mesh=mesh,
        in_specs=(P("mat", "shard", None),),
        out_specs=P(None, "shard", None),
        check_vma=False,
    )
```

```python
import functools

import jax
import jax.numpy as jnp
from jax import lax
from jax.experimental import pallas as pl
from jax.experimental.pallas import tpu as pltpu
from jax.sharding import PartitionSpec as P

coef_a = 3.4445
coef_b = -4.775
coef_c = 2.0315

TILE = 1280
LANES = 128
VMEM_LIMIT = 48 * 1024 * 1024


def dot_t(left, right):
    return lax.dot_general(
        left, right, (((1,), (1,)), ((), ())), preferred_element_type=jnp.float32
    )


def dot(left, right):
    return jnp.dot(left, right, preferred_element_type=jnp.float32)


def general_shards(iterate):
    own = iterate[0]
    gathered = lax.all_gather(own, "shard", axis=0, tiled=True)
    gram = dot_t(own, gathered).astype(jnp.bfloat16)
    cubic = dot(gram, gathered).astype(jnp.bfloat16)
    squared = dot_t(cubic, gathered)
    polynomial = (coef_b * gram.astype(jnp.float32) + coef_c * squared).astype(jnp.bfloat16)
    product = dot(polynomial, gathered)
    next_rows = (coef_a * own.astype(jnp.float32) + product).astype(jnp.bfloat16)
    return lax.all_gather(next_rows[None], "mat", axis=0, tiled=True)


def tiles(start, stop):
    return [pl.ds(at, min(TILE, stop - at)) for at in range(start, stop, TILE)]


def starts(blocks):
    return [sum(b.shape[0] for b in blocks[:k]) for k in range(len(blocks) + 1)]


def early_kernel(rows, first, count, *refs):
    inner, blocks, refs = refs[0], refs[1 : count + 1], refs[count + 1 :]
    *cubic_in, gram, cubic, whole, sems = refs
    columns = blocks[0].shape[1]
    begin = starts(blocks)
    base = begin[first]

    @pl.when(inner[0] != 0)
    def _():
        copies = []
        for k, block in enumerate(blocks):
            target = whole.at[pl.ds(begin[k], block.shape[0]), :]
            copies.append(pltpu.make_async_copy(block, target, sems.at[k]))
        if cubic_in:
            copies.append(pltpu.make_async_copy(cubic_in[0], cubic, sems.at[count]))
        for copy in copies:
            copy.start()
        for copy in copies:
            copy.wait()
        for at in tiles(base, begin[-1]):
            out = pl.ds(at.start - base, at.size)
            gram[:, out] = dot_t(whole[: 2 * rows, :], whole[at, :]).astype(jnp.bfloat16)
        for at in tiles(0, columns):
            add = dot(gram[:, : begin[-1] - base], whole[pl.ds(base, begin[-1] - base), at])
            cubic[:, at] = (cubic[:, at] + add) if cubic_in else add


def early_products(inner, rows, left, blocks, cubic=None):
    blocks, first = left + blocks, len(left)
    count = len(blocks)
    columns = blocks[0].shape[1]
    begin = starts(blocks)
    known = begin[-1] - begin[first]
    more = [] if cubic is None else [cubic]
    return pl.pallas_call(
        functools.partial(early_kernel, rows, first, count),
        out_shape=(
            jax.ShapeDtypeStruct((2 * rows, pl.cdiv(known, LANES) * LANES), jnp.bfloat16),
            jax.ShapeDtypeStruct((2 * rows, columns), jnp.float32),
        ),
        in_specs=[pl.BlockSpec(memory_space=pltpu.SMEM)]
        + [pl.BlockSpec(memory_space=pl.ANY)] * (count + len(more)),
        out_specs=(pl.BlockSpec(memory_space=pltpu.VMEM),) * 2,
        scratch_shapes=[
            pltpu.VMEM((begin[-1], columns), jnp.bfloat16),
            pltpu.SemaphoreType.DMA((count + len(more),)),
        ],
        compiler_params=pltpu.CompilerParams(vmem_limit_bytes=VMEM_LIMIT),
        cost_estimate=pl.CostEstimate(
            flops=8 * rows * known * columns, bytes_accessed=4 * known * columns, transcendentals=0
        ),
    )(inner, *blocks, *more)


def late_kernel(first, early_count, count, gram_count, widths, *refs):
    inner, refs = refs[0], refs[1:]
    blocks, grams_in = refs[:count], refs[count : count + gram_count]
    cubic_in, refs = refs[count + gram_count], refs[count + gram_count + 1 :]
    outs = refs[: len(widths)]
    whole, gram, cubic_sum, cubic, poly, sems = refs[len(widths) :]
    rows, total = gram.shape
    columns = blocks[0].shape[1]
    begin = starts(blocks)
    known = begin[early_count]
    mine = pl.ds(first, rows)
    late = pl.ds(known, total - known)

    @pl.when(inner[0] != 0)
    def _():
        copies = {}

        def fetch(name, source, target):
            copies[name] = pltpu.make_async_copy(source, target, sems.at[len(copies)])
            copies[name].start()

        def fetch_block(k):
            fetch(k, blocks[k], whole.at[pl.ds(begin[k], blocks[k].shape[0]), :])

        own = [k for k in range(early_count) if first <= begin[k] < first + rows]
        others = [k for k in range(early_count) if k not in own]
        for k in own + list(range(early_count, count)):
            fetch_block(k)
        at = 0
        for k, gram_in in enumerate(grams_in):
            width = gram_in.shape[1]
            fetch("gram%d" % k, gram_in.at[mine, :], gram.at[:, pl.ds(at, width)])
            at += width
        fetch("cubic", cubic_in.at[mine, :], cubic_sum)
        for k in others:
            fetch_block(k)

        for k in own + list(range(early_count, count)):
            copies[k].wait()
        for k in range(gram_count):
            copies["gram%d" % k].wait()
        gram[:, late] = dot_t(whole[mine, :], whole[late, :]).astype(jnp.bfloat16)
        copies["cubic"].wait()
        for at in tiles(0, columns):
            add = dot(gram[:, late], whole[late, at])
            cubic[:, at] = (cubic_sum[:, at] + add).astype(jnp.bfloat16)

        for k in others:
            copies[k].wait()
        for at in tiles(0, total):
            squared = dot_t(cubic[...], whole[at, :])
            poly[:, at] = (coef_b * gram[:, at].astype(jnp.float32) + coef_c * squared).astype(
                jnp.bfloat16
            )

        left = 0
        for out, width in zip(outs, widths):
            at = pl.ds(left, width)
            product = dot(poly[...], whole[:, at])
            base = whole[mine, at].astype(jnp.float32)
            out[...] = (coef_a * base + product).astype(jnp.bfloat16)
            left += width


def late_products(inner, first, rows, early, late, grams, cubic, widths):
    blocks = early + late
    count = len(blocks)
    columns = blocks[0].shape[1]
    total = starts(blocks)[-1]
    return pl.pallas_call(
        functools.partial(late_kernel, first, len(early), count, len(grams), widths),
        out_shape=tuple(jax.ShapeDtypeStruct((rows, w), jnp.bfloat16) for w in widths),
        in_specs=[pl.BlockSpec(memory_space=pltpu.SMEM)]
        + [pl.BlockSpec(memory_space=pl.ANY)] * (count + len(grams) + 1),
        out_specs=tuple(pl.BlockSpec(memory_space=pltpu.VMEM) for _ in widths),
        scratch_shapes=[
            pltpu.VMEM((total, columns), jnp.bfloat16),
            pltpu.VMEM((rows, total), jnp.bfloat16),
            pltpu.VMEM((rows, columns), jnp.float32),
            pltpu.VMEM((rows, columns), jnp.bfloat16),
            pltpu.VMEM((rows, total), jnp.bfloat16),
            pltpu.SemaphoreType.DMA((count + len(grams) + 1,)),
        ],
        compiler_params=pltpu.CompilerParams(vmem_limit_bytes=VMEM_LIMIT),
        cost_estimate=pl.CostEstimate(
            flops=5 * rows * total * columns, bytes_accessed=2 * total * columns, transcendentals=0
        ),
    )(inner, *blocks, *grams, cubic)


def line_shards(iterate, widths):
    own = iterate[0]
    rows, columns = own.shape
    place = lax.axis_index("shard") // 2
    outer = (place == 0) | (place == 3)
    mat = lax.axis_index("mat")

    inner = jnp.where(outer, 0, 1).astype(jnp.int32)[None]
    tie = lax.optimization_barrier

    other_core = [(2, 3), (3, 2), (4, 5), (5, 4)]
    inwards = [(0, 2), (1, 3), (6, 4), (7, 5)]
    outwards = [(b, a) for a, b in inwards]
    middle = [(2, 4), (3, 5), (4, 2), (5, 3)]
    along_x = [(m, m ^ 1) for m in range(4)]
    along_y = [(m, m ^ 2) for m in range(4)]

    def swap(block):
        return lax.ppermute(block, "shard", other_core)

    from_outer = lax.ppermute(own, "shard", inwards)
    from_inner = lax.ppermute(own, "shard", middle)
    from_far = lax.ppermute(from_outer, "shard", middle)

    left = [from_outer, own]
    first = left + [swap(own), from_inner]
    first_gram, cubic = early_products(inner, rows, [], first)
    from_far, first_gram, cubic = tie((from_far, first_gram, cubic))
    then = [swap(from_outer), swap(from_inner), from_far]
    then_gram, cubic = early_products(inner, rows, left, then, cubic)
    early, grams, late = first + then, [first_gram, then_gram], [swap(from_far)]
    for_outer = late_products(inner, 0, rows, early, late, grams, cubic, widths)
    for_own = late_products(inner, rows, rows, early, late, grams, cubic, widths)

    result = jnp.zeros((4, rows, columns), jnp.bfloat16)

    def place_in(result, flip, at, part):
        return lax.dynamic_update_slice(result, part[None], (mat ^ flip, 0, at))

    begin = 0
    for k, width in enumerate(widths):
        returned = lax.ppermute(for_outer[k], "shard", outwards)
        mine = tie(jnp.where(outer, returned, for_own[k]))
        by_x = lax.ppermute(mine, "mat", along_x)
        by_y = lax.ppermute(mine, "mat", along_y)
        by_x, by_y = tie((by_x, by_y))
        if k % 2 == 0:
            across = lax.ppermute(by_x, "mat", along_y)
        else:
            across = lax.ppermute(by_y, "mat", along_x)
        for flip, part in enumerate((mine, by_x, by_y, across)):
            result = place_in(result, flip, begin, part)
        begin += width
    return result


def solution(mesh):
    if (mesh.shape["mat"], mesh.shape["shard"]) == (4, 8):
        def shards(iterate):
            return line_shards(iterate, widths=(1280, 1280))
    else:
        shards = general_shards
    return jax.shard_map(
        shards,
        mesh=mesh,
        in_specs=(P("mat", "shard", None),),
        out_specs=P(None, "shard", None),
        check_vma=False,
    )
```

```python
import functools

import jax
import jax.numpy as jnp
from jax import lax
from jax.experimental import pallas as pl
from jax.experimental.pallas import tpu as pltpu
from jax.sharding import PartitionSpec as P

coef_a = 3.4445
coef_b = -4.775
coef_c = 2.0315

TILE = 1280
VMEM_LIMIT = 48 * 1024 * 1024


def dot_t(left, right):
    return lax.dot_general(
        left, right, (((1,), (1,)), ((), ())), preferred_element_type=jnp.float32
    )


def dot(left, right):
    return jnp.dot(left, right, preferred_element_type=jnp.float32)


def general_shards(iterate):
    own = iterate[0]
    gathered = lax.all_gather(own, "shard", axis=0, tiled=True)
    gram = dot_t(own, gathered).astype(jnp.bfloat16)
    cubic = dot(gram, gathered).astype(jnp.bfloat16)
    squared = dot_t(cubic, gathered)
    polynomial = (coef_b * gram.astype(jnp.float32) + coef_c * squared).astype(jnp.bfloat16)
    product = dot(polynomial, gathered)
    next_rows = (coef_a * own.astype(jnp.float32) + product).astype(jnp.bfloat16)
    return lax.all_gather(next_rows[None], "mat", axis=0, tiled=True)


def tiles(start, stop):
    return [pl.ds(at, min(TILE, stop - at)) for at in range(start, stop, TILE)]


def starts(blocks):
    return [sum(b.shape[0] for b in blocks[:k]) for k in range(len(blocks) + 1)]


def fetch_blocks(blocks, whole, sems):
    copies = []
    for k, (block, at) in enumerate(zip(blocks, starts(blocks))):
        target = whole.at[pl.ds(at, block.shape[0]), :]
        copies.append(pltpu.make_async_copy(block, target, sems.at[k]))
        copies[k].start()
    return copies


def gram_kernel(count, *refs):
    inner, blocks, (gram, whole, sems) = refs[0], refs[1 : count + 1], refs[count + 1 :]
    left = pl.ds(0, gram.shape[0])

    @pl.when(inner[0] != 0)
    def _():
        for copy in fetch_blocks(blocks, whole, sems):
            copy.wait()
        for at in tiles(0, whole.shape[0]):
            gram[:, at] = dot_t(whole[left, :], whole[at, :]).astype(jnp.bfloat16)


def cubic_kernel(count, *refs):
    inner, blocks, refs = refs[0], refs[1 : count + 1], refs[count + 1 :]
    gram_in, gram, cubic, whole, sems = refs
    left = pl.ds(0, gram.shape[0])
    known = gram_in.shape[1]

    @pl.when(inner[0] != 0)
    def _():
        copies = fetch_blocks(blocks, whole, sems)
        copies.append(
            pltpu.make_async_copy(gram_in, gram.at[:, pl.ds(0, known)], sems.at[count])
        )
        copies[count].start()
        for copy in copies:
            copy.wait()
        for at in tiles(known, whole.shape[0]):
            gram[:, at] = dot_t(whole[left, :], whole[at, :]).astype(jnp.bfloat16)
        for at in tiles(0, whole.shape[1]):
            cubic[:, at] = dot(gram[...], whole[:, at])


def early_products(kernel, inner, blocks, more, out_shape, flops):
    count = len(blocks)
    return pl.pallas_call(
        functools.partial(kernel, count),
        out_shape=out_shape,
        in_specs=[pl.BlockSpec(memory_space=pltpu.SMEM)]
        + [pl.BlockSpec(memory_space=pl.ANY)] * (count + len(more)),
        out_specs=tuple(pl.BlockSpec(memory_space=pltpu.VMEM) for _ in out_shape),
        scratch_shapes=[
            pltpu.VMEM((starts(blocks)[-1], blocks[0].shape[1]), jnp.bfloat16),
            pltpu.SemaphoreType.DMA((count + len(more),)),
        ],
        compiler_params=pltpu.CompilerParams(vmem_limit_bytes=VMEM_LIMIT),
        cost_estimate=pl.CostEstimate(flops=flops, bytes_accessed=flops // 1024, transcendentals=0),
    )(inner, *blocks, *more)


def first_grams(inner, blocks, rows):
    columns = blocks[0].shape[1]
    known = starts(blocks)[-1]
    shape = (jax.ShapeDtypeStruct((2 * rows, known), jnp.bfloat16),)
    return early_products(gram_kernel, inner, blocks, [], shape, 4 * rows * known * columns)[0]


def early_cubic(inner, blocks, rows, gram):
    columns = blocks[0].shape[1]
    known = starts(blocks)[-1]
    shape = (
        jax.ShapeDtypeStruct((2 * rows, known), jnp.bfloat16),
        jax.ShapeDtypeStruct((2 * rows, columns), jnp.float32),
    )
    return early_products(cubic_kernel, inner, blocks, [gram], shape, 6 * rows * known * columns)


def late_kernel(first, early_count, count, gram_count, widths, *refs):
    inner, refs = refs[0], refs[1:]
    blocks, grams_in = refs[:count], refs[count : count + gram_count]
    cubic_in, refs = refs[count + gram_count], refs[count + gram_count + 1 :]
    outs = refs[: len(widths)]
    whole, gram, cubic_sum, cubic, poly, sems = refs[len(widths) :]
    rows, total = gram.shape
    columns = blocks[0].shape[1]
    begin = starts(blocks)
    known = begin[early_count]
    mine = pl.ds(first, rows)
    late = pl.ds(known, total - known)

    @pl.when(inner[0] != 0)
    def _():
        copies = {}

        def fetch(name, source, target):
            copies[name] = pltpu.make_async_copy(source, target, sems.at[len(copies)])
            copies[name].start()

        def fetch_block(k):
            fetch(k, blocks[k], whole.at[pl.ds(begin[k], blocks[k].shape[0]), :])

        own = [k for k in range(early_count) if first <= begin[k] < first + rows]
        others = [k for k in range(early_count) if k not in own]
        for k in own + list(range(early_count, count)):
            fetch_block(k)
        at = 0
        for k, gram_in in enumerate(grams_in):
            width = gram_in.shape[1]
            fetch("gram%d" % k, gram_in.at[mine, :], gram.at[:, pl.ds(at, width)])
            at += width
        fetch("cubic", cubic_in.at[mine, :], cubic_sum)
        for k in others:
            fetch_block(k)

        for k in own + list(range(early_count, count)):
            copies[k].wait()
        for k in range(gram_count):
            copies["gram%d" % k].wait()
        gram[:, late] = dot_t(whole[mine, :], whole[late, :]).astype(jnp.bfloat16)
        copies["cubic"].wait()
        for at in tiles(0, columns):
            add = dot(gram[:, late], whole[late, at])
            cubic[:, at] = (cubic_sum[:, at] + add).astype(jnp.bfloat16)

        for k in others:
            copies[k].wait()
        for at in tiles(0, total):
            squared = dot_t(cubic[...], whole[at, :])
            poly[:, at] = (coef_b * gram[:, at].astype(jnp.float32) + coef_c * squared).astype(
                jnp.bfloat16
            )

        left = 0
        for out, width in zip(outs, widths):
            at = pl.ds(left, width)
            product = dot(poly[...], whole[:, at])
            base = whole[mine, at].astype(jnp.float32)
            out[...] = (coef_a * base + product).astype(jnp.bfloat16)
            left += width


def late_products(inner, first, rows, early, late, grams, cubic, widths):
    blocks = early + late
    count = len(blocks)
    columns = blocks[0].shape[1]
    total = starts(blocks)[-1]
    return pl.pallas_call(
        functools.partial(late_kernel, first, len(early), count, len(grams), widths),
        out_shape=tuple(jax.ShapeDtypeStruct((rows, w), jnp.bfloat16) for w in widths),
        in_specs=[pl.BlockSpec(memory_space=pltpu.SMEM)]
        + [pl.BlockSpec(memory_space=pl.ANY)] * (count + len(grams) + 1),
        out_specs=tuple(pl.BlockSpec(memory_space=pltpu.VMEM) for _ in widths),
        scratch_shapes=[
            pltpu.VMEM((total, columns), jnp.bfloat16),
            pltpu.VMEM((rows, total), jnp.bfloat16),
            pltpu.VMEM((rows, columns), jnp.float32),
            pltpu.VMEM((rows, columns), jnp.bfloat16),
            pltpu.VMEM((rows, total), jnp.bfloat16),
            pltpu.SemaphoreType.DMA((count + len(grams) + 1,)),
        ],
        compiler_params=pltpu.CompilerParams(vmem_limit_bytes=VMEM_LIMIT),
        cost_estimate=pl.CostEstimate(
            flops=5 * rows * total * columns, bytes_accessed=2 * total * columns, transcendentals=0
        ),
    )(inner, *blocks, *grams, cubic)


def line_shards(iterate, widths):
    own = iterate[0]
    rows, columns = own.shape
    place = lax.axis_index("shard") // 2
    outer = (place == 0) | (place == 3)
    mat = lax.axis_index("mat")

    inner = jnp.where(outer, 0, 1).astype(jnp.int32)[None]
    tie = lax.optimization_barrier

    other_core = [(2, 3), (3, 2), (4, 5), (5, 4)]
    inwards = [(0, 2), (1, 3), (6, 4), (7, 5)]
    outwards = [(b, a) for a, b in inwards]
    middle = [(2, 4), (3, 5), (4, 2), (5, 3)]
    along_x = [(m, m ^ 1) for m in range(4)]
    along_y = [(m, m ^ 2) for m in range(4)]

    def move(name, block, axis, pairs):
        with jax.named_scope(name):
            return lax.ppermute(block, axis, pairs)

    def swap(name, block):
        return move("swap_" + name, block, "shard", other_core)

    cut = rows // 2
    halves = [own[:cut], own[cut:]]
    outer_rows = [move("rows_in", half, "shard", inwards) for half in halves]
    inner_rows = move("middle_own", own, "shard", middle)
    far_rows = [move("middle_far", half, "shard", middle) for half in outer_rows]

    inner_rows, _ = tie((inner_rows, outer_rows[1]))
    first = outer_rows + [own, swap("own", own), inner_rows]
    gram = first_grams(inner, first, rows)
    far_rows[0], gram = tie((far_rows[0], gram))
    then = [swap("outer", half) for half in outer_rows] + [swap("inner", inner_rows)]
    early = first + then
    gram, cubic = early_cubic(inner, early, rows, gram)
    far_rows[1], gram, cubic = tie((far_rows[1], gram, cubic))
    late = far_rows + [swap("far", half) for half in far_rows]
    for_outer = late_products(inner, 0, rows, early, late, [gram], cubic, widths)
    for_own = late_products(inner, rows, rows, early, late, [gram], cubic, widths)

    result = jnp.zeros((4, rows, columns), jnp.bfloat16)

    def place_in(result, flip, at, part):
        return lax.dynamic_update_slice(result, part[None], (mat ^ flip, 0, at))

    begin = 0
    for k, width in enumerate(widths):
        returned = move("rows_out", for_outer[k], "shard", outwards)
        mine = tie(jnp.where(outer, returned, for_own[k]))
        by_x = move("along_x", mine, "mat", along_x)
        by_y = move("along_y", mine, "mat", along_y)
        by_x, by_y = tie((by_x, by_y))
        if k % 2 == 0:
            across = move("across_y", by_x, "mat", along_y)
        else:
            across = move("across_x", by_y, "mat", along_x)
        for flip, part in enumerate((mine, by_x, by_y, across)):
            result = place_in(result, flip, begin, part)
        begin += width
    return result


def solution(mesh):
    if (mesh.shape["mat"], mesh.shape["shard"]) == (4, 8):
        def shards(iterate):
            return line_shards(iterate, widths=(1280, 1280))
    else:
        shards = general_shards
    return jax.shard_map(
        shards,
        mesh=mesh,
        in_specs=(P("mat", "shard", None),),
        out_specs=P(None, "shard", None),
        check_vma=False,
    )
```

```python
import functools

import jax
import jax.numpy as jnp
from jax import lax
from jax.experimental import pallas as pl
from jax.experimental.pallas import tpu as pltpu
from jax.sharding import PartitionSpec as P

coef_a = 3.4445
coef_b = -4.775
coef_c = 2.0315

TILE = 1024
VMEM_LIMIT = 30 * 1024 * 1024


def dot_t(left, right):
    return lax.dot_general(
        left, right, (((1,), (1,)), ((), ())), preferred_element_type=jnp.float32
    )


def dot(left, right):
    return jnp.dot(left, right, preferred_element_type=jnp.float32)


def general_shards(iterate):
    own = iterate[0]
    gathered = lax.all_gather(own, "shard", axis=0, tiled=True)
    gram = dot_t(own, gathered).astype(jnp.bfloat16)
    cubic = dot(gram, gathered).astype(jnp.bfloat16)
    squared = dot_t(cubic, gathered)
    polynomial = (coef_b * gram.astype(jnp.float32) + coef_c * squared).astype(jnp.bfloat16)
    product = dot(polynomial, gathered)
    next_rows = (coef_a * own.astype(jnp.float32) + product).astype(jnp.bfloat16)
    return lax.all_gather(next_rows[None], "mat", axis=0, tiled=True)


def tiles(start, stop):
    return [pl.ds(at, min(TILE, stop - at)) for at in range(start, stop, TILE)]


def starts(blocks):
    return [sum(b.shape[0] for b in blocks[:k]) for k in range(len(blocks) + 1)]


def fetch_blocks(blocks, whole, sems):
    copies = []
    for k, (block, at) in enumerate(zip(blocks, starts(blocks))):
        target = whole.at[pl.ds(at, block.shape[0]), :]
        copies.append(pltpu.make_async_copy(block, target, sems.at[k]))
        copies[k].start()
    return copies


def gram_kernel(count, *refs):
    inner, blocks, (gram, whole, sems) = refs[0], refs[1 : count + 1], refs[count + 1 :]
    left = pl.ds(0, gram.shape[0])

    @pl.when(inner[0] != 0)
    def _():
        for copy in fetch_blocks(blocks, whole, sems):
            copy.wait()
        for at in tiles(0, whole.shape[0]):
            gram[:, at] = dot_t(whole[left, :], whole[at, :]).astype(jnp.bfloat16)


def cubic_kernel(count, *refs):
    inner, blocks, refs = refs[0], refs[1 : count + 1], refs[count + 1 :]
    gram_in, gram, cubic, whole, sems = refs
    left = pl.ds(0, gram.shape[0])
    known = gram_in.shape[1]

    @pl.when(inner[0] != 0)
    def _():
        copies = fetch_blocks(blocks, whole, sems)
        copies.append(
            pltpu.make_async_copy(gram_in, gram.at[:, pl.ds(0, known)], sems.at[count])
        )
        copies[count].start()
        for copy in copies:
            copy.wait()
        for at in tiles(known, whole.shape[0]):
            gram[:, at] = dot_t(whole[left, :], whole[at, :]).astype(jnp.bfloat16)
        for at in tiles(0, whole.shape[1]):
            cubic[:, at] = dot(gram[...], whole[:, at])


def early_products(kernel, inner, blocks, more, out_shape, flops):
    count = len(blocks)
    return pl.pallas_call(
        functools.partial(kernel, count),
        out_shape=out_shape,
        in_specs=[pl.BlockSpec(memory_space=pltpu.SMEM)]
        + [pl.BlockSpec(memory_space=pltpu.HBM)] * count
        + [pl.BlockSpec(memory_space=pl.ANY)] * len(more),
        out_specs=tuple(pl.BlockSpec(memory_space=pltpu.VMEM) for _ in out_shape),
        scratch_shapes=[
            pltpu.VMEM((starts(blocks)[-1], blocks[0].shape[1]), jnp.bfloat16),
            pltpu.SemaphoreType.DMA((count + len(more),)),
        ],
        compiler_params=pltpu.CompilerParams(vmem_limit_bytes=VMEM_LIMIT),
        cost_estimate=pl.CostEstimate(flops=flops, bytes_accessed=flops // 1024, transcendentals=0),
    )(inner, *blocks, *more)


def first_grams(inner, blocks, rows):
    columns = blocks[0].shape[1]
    known = starts(blocks)[-1]
    shape = (jax.ShapeDtypeStruct((2 * rows, known), jnp.bfloat16),)
    return early_products(gram_kernel, inner, blocks, [], shape, 4 * rows * known * columns)[0]


def early_cubic(inner, blocks, rows, gram):
    columns = blocks[0].shape[1]
    known = starts(blocks)[-1]
    shape = (
        jax.ShapeDtypeStruct((2 * rows, known), jnp.bfloat16),
        jax.ShapeDtypeStruct((2 * rows, columns), jnp.float32),
    )
    return early_products(cubic_kernel, inner, blocks, [gram], shape, 6 * rows * known * columns)


def late_kernel(first, early_count, count, gram_count, widths, *refs):
    inner, refs = refs[0], refs[1:]
    blocks, grams_in = refs[:count], refs[count : count + gram_count]
    cubic_in, refs = refs[count + gram_count], refs[count + gram_count + 1 :]
    outs = refs[: len(widths)]
    whole, gram, cubic_sum, cubic, poly, sems = refs[len(widths) :]
    rows, total = gram.shape
    columns = blocks[0].shape[1]
    begin = starts(blocks)
    known = begin[early_count]
    mine = pl.ds(first, rows)
    late = pl.ds(known, total - known)

    @pl.when(inner[0] != 0)
    def _():
        copies = {}

        def fetch(name, source, target):
            copies[name] = pltpu.make_async_copy(source, target, sems.at[len(copies)])
            copies[name].start()

        def fetch_block(k):
            fetch(k, blocks[k], whole.at[pl.ds(begin[k], blocks[k].shape[0]), :])

        own = [k for k in range(early_count) if first <= begin[k] < first + rows]
        others = [k for k in range(early_count) if k not in own]
        for k in own + list(range(early_count, count)):
            fetch_block(k)
        at = 0
        for k, gram_in in enumerate(grams_in):
            width = gram_in.shape[1]
            fetch("gram%d" % k, gram_in.at[mine, :], gram.at[:, pl.ds(at, width)])
            at += width
        fetch("cubic", cubic_in.at[mine, :], cubic_sum)
        for k in others:
            fetch_block(k)

        for k in own + list(range(early_count, count)):
            copies[k].wait()
        for k in range(gram_count):
            copies["gram%d" % k].wait()
        gram[:, late] = dot_t(whole[mine, :], whole[late, :]).astype(jnp.bfloat16)
        copies["cubic"].wait()
        for at in tiles(0, columns):
            add = dot(gram[:, late], whole[late, at])
            cubic[:, at] = (cubic_sum[:, at] + add).astype(jnp.bfloat16)

        for k in others:
            copies[k].wait()
        for at in tiles(0, total):
            squared = dot_t(cubic[...], whole[at, :])
            poly[:, at] = (coef_b * gram[:, at].astype(jnp.float32) + coef_c * squared).astype(
                jnp.bfloat16
            )

        for at in tiles(0, columns):
            product = dot(poly[...], whole[:, at])
            base = whole[mine, at].astype(jnp.float32)
            new = (coef_a * base + product).astype(jnp.bfloat16)
            left = 0
            for out, width in zip(outs, widths):
                low, high = max(at.start, left), min(at.start + at.size, left + width)
                if low < high:
                    out[:, low - left : high - left] = new[:, low - at.start : high - at.start]
                left += width


def late_products(inner, first, rows, early, late, grams, cubic, widths):
    blocks = early + late
    count = len(blocks)
    columns = blocks[0].shape[1]
    total = starts(blocks)[-1]
    return pl.pallas_call(
        functools.partial(late_kernel, first, len(early), count, len(grams), widths),
        out_shape=tuple(jax.ShapeDtypeStruct((rows, w), jnp.bfloat16) for w in widths),
        in_specs=[pl.BlockSpec(memory_space=pltpu.SMEM)]
        + [pl.BlockSpec(memory_space=pltpu.HBM)] * count
        + [pl.BlockSpec(memory_space=pl.ANY)] * (len(grams) + 1),
        out_specs=tuple(pl.BlockSpec(memory_space=pltpu.VMEM) for _ in widths),
        scratch_shapes=[
            pltpu.VMEM((total, columns), jnp.bfloat16),
            pltpu.VMEM((rows, total), jnp.bfloat16),
            pltpu.VMEM((rows, columns), jnp.float32),
            pltpu.VMEM((rows, columns), jnp.bfloat16),
            pltpu.VMEM((rows, total), jnp.bfloat16),
            pltpu.SemaphoreType.DMA((count + len(grams) + 1,)),
        ],
        compiler_params=pltpu.CompilerParams(vmem_limit_bytes=VMEM_LIMIT),
        cost_estimate=pl.CostEstimate(
            flops=5 * rows * total * columns, bytes_accessed=2 * total * columns, transcendentals=0
        ),
    )(inner, *blocks, *grams, cubic)


def line_shards(iterate, widths):
    own = iterate[0]
    rows, columns = own.shape
    place = lax.axis_index("shard") // 2
    outer = (place == 0) | (place == 3)
    mat = lax.axis_index("mat")

    inner = jnp.where(outer, 0, 1).astype(jnp.int32)[None]
    tie = lax.optimization_barrier

    other_core = [(2, 3), (3, 2), (4, 5), (5, 4)]
    inwards = [(0, 2), (1, 3), (6, 4), (7, 5)]
    outwards = [(b, a) for a, b in inwards]
    middle = [(2, 4), (3, 5), (4, 2), (5, 3)]
    along_x = [(m, m ^ 1) for m in range(4)]
    along_y = [(m, m ^ 2) for m in range(4)]

    def move(name, block, axis, pairs):
        with jax.named_scope(name):
            return lax.ppermute(block, axis, pairs)

    def swap(name, block):
        return move("swap_" + name, block, "shard", other_core)

    cut = rows // 2
    halves = [own[:cut], own[cut:]]
    outer_rows = [move("rows_in", half, "shard", inwards) for half in halves]
    inner_rows = move("middle_own", own, "shard", middle)
    far_rows = [move("middle_far", half, "shard", middle) for half in outer_rows]

    inner_rows, _ = tie((inner_rows, outer_rows[1]))
    first = outer_rows + [own, swap("own", own), inner_rows]
    gram = first_grams(inner, first, rows)
    far_rows[0], gram = tie((far_rows[0], gram))
    then = [swap("outer", half) for half in outer_rows] + [swap("inner", inner_rows)]
    early = first + then
    gram, cubic = early_cubic(inner, early, rows, gram)
    far_rows[1], gram, cubic = tie((far_rows[1], gram, cubic))
    late = far_rows + [swap("far", half) for half in far_rows]
    for_outer = late_products(inner, 0, rows, early, late, [gram], cubic, widths)
    for_own = late_products(inner, rows, rows, early, late, [gram], cubic, widths)

    result = jnp.zeros((4, rows, columns), jnp.bfloat16)

    def place_in(result, flip, at, part):
        return lax.dynamic_update_slice(result, part[None], (mat ^ flip, 0, at))

    begin = 0
    for k, width in enumerate(widths):
        returned = move("rows_out", for_outer[k], "shard", outwards)
        mine = tie(jnp.where(outer, returned, for_own[k]))
        by_x = move("along_x", mine, "mat", along_x)
        by_y = move("along_y", mine, "mat", along_y)
        by_x, by_y = tie((by_x, by_y))
        if k % 2 == 0:
            across = move("across_y", by_x, "mat", along_y)
        else:
            across = move("across_x", by_y, "mat", along_x)
        for flip, part in enumerate((mine, by_x, by_y, across)):
            result = place_in(result, flip, begin, part)
        begin += width
    return result


def solution(mesh):
    if (mesh.shape["mat"], mesh.shape["shard"]) == (4, 8):
        def shards(iterate):
            return line_shards(iterate, widths=(1280, 1280))
    else:
        shards = general_shards
    return jax.shard_map(
        shards,
        mesh=mesh,
        in_specs=(P("mat", "shard", None),),
        out_specs=P(None, "shard", None),
        check_vma=False,
    )
```

```python
import functools

import jax
import jax.numpy as jnp
from jax import lax
from jax.experimental import pallas as pl
from jax.experimental.pallas import tpu as pltpu
from jax.sharding import PartitionSpec as P

coef_a = 3.4445
coef_b = -4.775
coef_c = 2.0315

TILE = 1024
VMEM_LIMIT = 30 * 1024 * 1024


def dot_t(left, right):
    return lax.dot_general(
        left, right, (((1,), (1,)), ((), ())), preferred_element_type=jnp.float32
    )


def dot(left, right):
    return jnp.dot(left, right, preferred_element_type=jnp.float32)


def general_shards(iterate):
    own = iterate[0]
    gathered = lax.all_gather(own, "shard", axis=0, tiled=True)
    gram = dot_t(own, gathered).astype(jnp.bfloat16)
    cubic = dot(gram, gathered).astype(jnp.bfloat16)
    squared = dot_t(cubic, gathered)
    polynomial = (coef_b * gram.astype(jnp.float32) + coef_c * squared).astype(jnp.bfloat16)
    product = dot(polynomial, gathered)
    next_rows = (coef_a * own.astype(jnp.float32) + product).astype(jnp.bfloat16)
    return lax.all_gather(next_rows[None], "mat", axis=0, tiled=True)


def tiles(start, stop):
    return [pl.ds(at, min(TILE, stop - at)) for at in range(start, stop, TILE)]


def starts(blocks):
    return [sum(b.shape[0] for b in blocks[:k]) for k in range(len(blocks) + 1)]


def fetch_blocks(blocks, whole, sems):
    copies = []
    for k, (block, at) in enumerate(zip(blocks, starts(blocks))):
        target = whole.at[pl.ds(at, block.shape[0]), :]
        copies.append(pltpu.make_async_copy(block, target, sems.at[k]))
        copies[k].start()
    return copies


def early_kernel(count, *refs):
    inner, blocks, (gram, cubic, whole, sems) = refs[0], refs[1 : count + 1], refs[count + 1 :]
    left = pl.ds(0, gram.shape[0])

    @pl.when(inner[0] != 0)
    def _():
        for copy in fetch_blocks(blocks, whole, sems):
            copy.wait()
        for at in tiles(0, whole.shape[0]):
            gram[:, at] = dot_t(whole[left, :], whole[at, :]).astype(jnp.bfloat16)
        for at in tiles(0, whole.shape[1]):
            cubic[:, at] = dot(gram[...], whole[:, at])


def early_products(inner, rows, blocks):
    count = len(blocks)
    columns = blocks[0].shape[1]
    known = starts(blocks)[-1]
    return pl.pallas_call(
        functools.partial(early_kernel, count),
        out_shape=(
            jax.ShapeDtypeStruct((2 * rows, known), jnp.bfloat16),
            jax.ShapeDtypeStruct((2 * rows, columns), jnp.float32),
        ),
        in_specs=[pl.BlockSpec(memory_space=pltpu.SMEM)]
        + [pl.BlockSpec(memory_space=pltpu.HBM)] * count,
        out_specs=(pl.BlockSpec(memory_space=pltpu.VMEM),) * 2,
        scratch_shapes=[
            pltpu.VMEM((known, columns), jnp.bfloat16),
            pltpu.SemaphoreType.DMA((count,)),
        ],
        compiler_params=pltpu.CompilerParams(vmem_limit_bytes=VMEM_LIMIT),
        cost_estimate=pl.CostEstimate(
            flops=rows * known, bytes_accessed=2 * rows, transcendentals=0
        ),
    )(inner, *blocks)


def late_kernel(first, early_count, count, gram_count, widths, *refs):
    inner, refs = refs[0], refs[1:]
    blocks, grams_in = refs[:count], refs[count : count + gram_count]
    cubic_in, refs = refs[count + gram_count], refs[count + gram_count + 1 :]
    outs = refs[: len(widths)]
    whole, gram, cubic_sum, cubic, poly, sems = refs[len(widths) :]
    rows, total = gram.shape
    columns = blocks[0].shape[1]
    begin = starts(blocks)
    known = begin[early_count]
    mine = pl.ds(first, rows)
    late = pl.ds(known, total - known)

    @pl.when(inner[0] != 0)
    def _():
        copies = {}

        def fetch(name, source, target):
            copies[name] = pltpu.make_async_copy(source, target, sems.at[len(copies)])
            copies[name].start()

        def fetch_block(k):
            fetch(k, blocks[k], whole.at[pl.ds(begin[k], blocks[k].shape[0]), :])

        own = [k for k in range(early_count) if first <= begin[k] < first + rows]
        others = [k for k in range(early_count) if k not in own]
        for k in own + list(range(early_count, count)):
            fetch_block(k)
        at = 0
        for k, gram_in in enumerate(grams_in):
            width = gram_in.shape[1]
            fetch("gram%d" % k, gram_in.at[mine, :], gram.at[:, pl.ds(at, width)])
            at += width
        fetch("cubic", cubic_in.at[mine, :], cubic_sum)
        for k in others:
            fetch_block(k)

        for k in own + list(range(early_count, count)):
            copies[k].wait()
        for k in range(gram_count):
            copies["gram%d" % k].wait()
        gram[:, late] = dot_t(whole[mine, :], whole[late, :]).astype(jnp.bfloat16)
        copies["cubic"].wait()
        for at in tiles(0, columns):
            add = dot(gram[:, late], whole[late, at])
            cubic[:, at] = (cubic_sum[:, at] + add).astype(jnp.bfloat16)

        for k in others:
            copies[k].wait()
        for at in tiles(0, total):
            squared = dot_t(cubic[...], whole[at, :])
            poly[:, at] = (coef_b * gram[:, at].astype(jnp.float32) + coef_c * squared).astype(
                jnp.bfloat16
            )

        for at in tiles(0, columns):
            product = dot(poly[...], whole[:, at])
            base = whole[mine, at].astype(jnp.float32)
            new = (coef_a * base + product).astype(jnp.bfloat16)
            left = 0
            for out, width in zip(outs, widths):
                low, high = max(at.start, left), min(at.start + at.size, left + width)
                if low < high:
                    out[:, low - left : high - left] = new[:, low - at.start : high - at.start]
                left += width


def late_products(inner, first, rows, early, late, grams, cubic, widths):
    blocks = early + late
    count = len(blocks)
    columns = blocks[0].shape[1]
    total = starts(blocks)[-1]
    return pl.pallas_call(
        functools.partial(late_kernel, first, len(early), count, len(grams), widths),
        out_shape=tuple(jax.ShapeDtypeStruct((rows, w), jnp.bfloat16) for w in widths),
        in_specs=[pl.BlockSpec(memory_space=pltpu.SMEM)]
        + [pl.BlockSpec(memory_space=pltpu.HBM)] * count
        + [pl.BlockSpec(memory_space=pl.ANY)] * (len(grams) + 1),
        out_specs=tuple(pl.BlockSpec(memory_space=pltpu.VMEM) for _ in widths),
        scratch_shapes=[
            pltpu.VMEM((total, columns), jnp.bfloat16),
            pltpu.VMEM((rows, total), jnp.bfloat16),
            pltpu.VMEM((rows, columns), jnp.float32),
            pltpu.VMEM((rows, columns), jnp.bfloat16),
            pltpu.VMEM((rows, total), jnp.bfloat16),
            pltpu.SemaphoreType.DMA((count + len(grams) + 1,)),
        ],
        compiler_params=pltpu.CompilerParams(vmem_limit_bytes=VMEM_LIMIT),
        cost_estimate=pl.CostEstimate(
            flops=5 * rows * total * columns, bytes_accessed=2 * total * columns, transcendentals=0
        ),
    )(inner, *blocks, *grams, cubic)


def line_shards(iterate, widths):
    own = iterate[0]
    rows, columns = own.shape
    place = lax.axis_index("shard") // 2
    outer = (place == 0) | (place == 3)
    mat = lax.axis_index("mat")

    inner = jnp.where(outer, 0, 1).astype(jnp.int32)[None]
    tie = lax.optimization_barrier

    other_core = [(2, 3), (3, 2), (4, 5), (5, 4)]
    inwards = [(0, 2), (1, 3), (6, 4), (7, 5)]
    outwards = [(b, a) for a, b in inwards]
    middle = [(2, 4), (3, 5), (4, 2), (5, 3)]
    across_middle = [(0, 4), (1, 5), (6, 2), (7, 3)]
    along_x = [(m, m ^ 1) for m in range(4)]
    along_y = [(m, m ^ 2) for m in range(4)]

    def move(name, block, axis, pairs):
        with jax.named_scope(name):
            return lax.ppermute(block, axis, pairs)

    def swap(name, block):
        return move("swap_" + name, block, "shard", other_core)

    cut = rows // 2
    halves = [own[:cut], own[cut:]]
    first_rows = move("rows_in", halves[0], "shard", inwards)
    second_half, first_rows = tie((halves[1], first_rows))
    outer_rows = [first_rows, move("rows_in", second_half, "shard", inwards)]
    inner_rows = [move("middle", half, "shard", middle) for half in halves]
    far_rows = move("rows_far", own, "shard", across_middle)

    early = outer_rows + [own, swap("own", own)] + inner_rows
    early += [swap("rows", half) for half in outer_rows + inner_rows]
    gram, cubic = early_products(inner, rows, early)
    far_rows, gram, cubic = tie((far_rows, gram, cubic))
    late = [far_rows, swap("far", far_rows)]
    for_outer = late_products(inner, 0, rows, early, late, [gram], cubic, widths)
    for_own = late_products(inner, rows, rows, early, late, [gram], cubic, widths)

    result = jnp.zeros((4, rows, columns), jnp.bfloat16)

    def place_in(result, flip, at, part):
        return lax.dynamic_update_slice(result, part[None], (mat ^ flip, 0, at))

    begin = 0
    for k, width in enumerate(widths):
        returned = move("rows_out", for_outer[k], "shard", outwards)
        mine = tie(jnp.where(outer, returned, for_own[k]))
        by_x = move("along_x", mine, "mat", along_x)
        by_y = move("along_y", mine, "mat", along_y)
        by_x, by_y = tie((by_x, by_y))
        if k % 2 == 0:
            across = move("across_y", by_x, "mat", along_y)
        else:
            across = move("across_x", by_y, "mat", along_x)
        for flip, part in enumerate((mine, by_x, by_y, across)):
            result = place_in(result, flip, begin, part)
        begin += width
    return result


def solution(mesh):
    if (mesh.shape["mat"], mesh.shape["shard"]) == (4, 8):
        def shards(iterate):
            return line_shards(iterate, widths=(1280, 1280))
    else:
        shards = general_shards
    return jax.shard_map(
        shards,
        mesh=mesh,
        in_specs=(P("mat", "shard", None),),
        out_specs=P(None, "shard", None),
        check_vma=False,
    )
```

```python
import functools

import jax
import jax.numpy as jnp
from jax import lax
from jax.experimental import pallas as pl
from jax.experimental.pallas import tpu as pltpu
from jax.sharding import PartitionSpec as P

coef_a = 3.4445
coef_b = -4.775
coef_c = 2.0315

TILE = 1024
VMEM_LIMIT = 40 * 1024 * 1024


def dot_t(left, right):
    return lax.dot_general(
        left, right, (((1,), (1,)), ((), ())), preferred_element_type=jnp.float32
    )


def dot(left, right):
    return jnp.dot(left, right, preferred_element_type=jnp.float32)


def general_shards(iterate):
    own = iterate[0]
    gathered = lax.all_gather(own, "shard", axis=0, tiled=True)
    gram = dot_t(own, gathered).astype(jnp.bfloat16)
    cubic = dot(gram, gathered).astype(jnp.bfloat16)
    squared = dot_t(cubic, gathered)
    polynomial = (coef_b * gram.astype(jnp.float32) + coef_c * squared).astype(jnp.bfloat16)
    product = dot(polynomial, gathered)
    next_rows = (coef_a * own.astype(jnp.float32) + product).astype(jnp.bfloat16)
    return lax.all_gather(next_rows[None], "mat", axis=0, tiled=True)


def tiles(start, stop):
    return [pl.ds(at, min(TILE, stop - at)) for at in range(start, stop, TILE)]


def starts(blocks):
    return [sum(b.shape[0] for b in blocks[:k]) for k in range(len(blocks) + 1)]


def fetch_blocks(blocks, whole, sems):
    copies = []
    for k, (block, at) in enumerate(zip(blocks, starts(blocks))):
        target = whole.at[pl.ds(at, block.shape[0]), :]
        copies.append(pltpu.make_async_copy(block, target, sems.at[k]))
        copies[k].start()
    return copies


def early_kernel(count, *refs):
    inner, blocks, (gram, cubic, whole, sems) = refs[0], refs[1 : count + 1], refs[count + 1 :]
    left = pl.ds(0, gram.shape[0])

    @pl.when(inner[0] != 0)
    def _():
        for copy in fetch_blocks(blocks, whole, sems):
            copy.wait()
        for at in tiles(0, whole.shape[0]):
            gram[:, at] = dot_t(whole[left, :], whole[at, :]).astype(jnp.bfloat16)
        for at in tiles(0, whole.shape[1]):
            cubic[:, at] = dot(gram[...], whole[:, at])


def early_products(inner, rows, blocks):
    count = len(blocks)
    columns = blocks[0].shape[1]
    known = starts(blocks)[-1]
    return pl.pallas_call(
        functools.partial(early_kernel, count),
        out_shape=(
            jax.ShapeDtypeStruct((2 * rows, known), jnp.bfloat16),
            jax.ShapeDtypeStruct((2 * rows, columns), jnp.float32),
        ),
        in_specs=[pl.BlockSpec(memory_space=pltpu.SMEM)]
        + [pl.BlockSpec(memory_space=pltpu.HBM)] * count,
        out_specs=(pl.BlockSpec(memory_space=pltpu.VMEM),) * 2,
        scratch_shapes=[
            pltpu.VMEM((known, columns), jnp.bfloat16),
            pltpu.SemaphoreType.DMA((count,)),
        ],
        compiler_params=pltpu.CompilerParams(vmem_limit_bytes=VMEM_LIMIT),
        cost_estimate=pl.CostEstimate(
            flops=rows * known, bytes_accessed=2 * rows, transcendentals=0
        ),
    )(inner, *blocks)


def late_kernel(first, early_count, count, gram_count, widths, *refs):
    inner, refs = refs[0], refs[1:]
    blocks, grams_in = refs[:count], refs[count : count + gram_count]
    cubic_in, refs = refs[count + gram_count], refs[count + gram_count + 1 :]
    outs = refs[: len(widths)]
    whole, gram, cubic_sum, cubic, poly, sems = refs[len(widths) :]
    rows, total = gram.shape
    columns = blocks[0].shape[1]
    begin = starts(blocks)
    known = begin[early_count]
    mine = pl.ds(first, rows)
    late = pl.ds(known, total - known)

    @pl.when(inner[0] != 0)
    def _():
        copies = {}

        def fetch(name, source, target):
            copies[name] = pltpu.make_async_copy(source, target, sems.at[len(copies)])
            copies[name].start()

        def fetch_block(k):
            fetch(k, blocks[k], whole.at[pl.ds(begin[k], blocks[k].shape[0]), :])

        own = [k for k in range(early_count) if first <= begin[k] < first + rows]
        others = [k for k in range(early_count) if k not in own]
        for k in own + list(range(early_count, count)):
            fetch_block(k)
        at = 0
        for k, gram_in in enumerate(grams_in):
            width = gram_in.shape[1]
            fetch("gram%d" % k, gram_in.at[mine, :], gram.at[:, pl.ds(at, width)])
            at += width
        fetch("cubic", cubic_in.at[mine, :], cubic_sum)
        for k in others:
            fetch_block(k)

        for k in own + list(range(early_count, count)):
            copies[k].wait()
        for k in range(gram_count):
            copies["gram%d" % k].wait()
        gram[:, late] = dot_t(whole[mine, :], whole[late, :]).astype(jnp.bfloat16)
        copies["cubic"].wait()
        for at in tiles(0, columns):
            add = dot(gram[:, late], whole[late, at])
            cubic[:, at] = (cubic_sum[:, at] + add).astype(jnp.bfloat16)

        for k in others:
            copies[k].wait()
        for at in tiles(0, total):
            squared = dot_t(cubic[...], whole[at, :])
            poly[:, at] = (coef_b * gram[:, at].astype(jnp.float32) + coef_c * squared).astype(
                jnp.bfloat16
            )

        for at in tiles(0, columns):
            product = dot(poly[...], whole[:, at])
            base = whole[mine, at].astype(jnp.float32)
            new = (coef_a * base + product).astype(jnp.bfloat16)
            left = 0
            for out, width in zip(outs, widths):
                low, high = max(at.start, left), min(at.start + at.size, left + width)
                if low < high:
                    out[:, low - left : high - left] = new[:, low - at.start : high - at.start]
                left += width


def late_products(inner, first, rows, early, late, grams, cubic, widths):
    blocks = early + late
    count = len(blocks)
    columns = blocks[0].shape[1]
    total = starts(blocks)[-1]
    return pl.pallas_call(
        functools.partial(late_kernel, first, len(early), count, len(grams), widths),
        out_shape=tuple(jax.ShapeDtypeStruct((rows, w), jnp.bfloat16) for w in widths),
        in_specs=[pl.BlockSpec(memory_space=pltpu.SMEM)]
        + [pl.BlockSpec(memory_space=pltpu.HBM)] * count
        + [pl.BlockSpec(memory_space=pl.ANY)] * (len(grams) + 1),
        out_specs=tuple(pl.BlockSpec(memory_space=pltpu.VMEM) for _ in widths),
        scratch_shapes=[
            pltpu.VMEM((total, columns), jnp.bfloat16),
            pltpu.VMEM((rows, total), jnp.bfloat16),
            pltpu.VMEM((rows, columns), jnp.float32),
            pltpu.VMEM((rows, columns), jnp.bfloat16),
            pltpu.VMEM((rows, total), jnp.bfloat16),
            pltpu.SemaphoreType.DMA((count + len(grams) + 1,)),
        ],
        compiler_params=pltpu.CompilerParams(vmem_limit_bytes=VMEM_LIMIT),
        cost_estimate=pl.CostEstimate(
            flops=5 * rows * total * columns, bytes_accessed=2 * total * columns, transcendentals=0
        ),
    )(inner, *blocks, *grams, cubic)


def line_shards(iterate, widths):
    own = iterate[0]
    rows, columns = own.shape
    place = lax.axis_index("shard") // 2
    outer = (place == 0) | (place == 3)
    mat = lax.axis_index("mat")

    inner = jnp.where(outer, 0, 1).astype(jnp.int32)[None]
    tie = lax.optimization_barrier

    other_core = [(2, 3), (3, 2), (4, 5), (5, 4)]
    inwards = [(0, 2), (1, 3), (6, 4), (7, 5)]
    outwards = [(b, a) for a, b in inwards]
    middle = [(2, 4), (3, 5), (4, 2), (5, 3)]
    across_middle = [(0, 4), (1, 5), (6, 2), (7, 3)]
    along_x = [(m, m ^ 1) for m in range(4)]
    along_y = [(m, m ^ 2) for m in range(4)]

    def move(name, block, axis, pairs):
        with jax.named_scope(name):
            return lax.ppermute(block, axis, pairs)

    def swap(name, block):
        return move("swap_" + name, block, "shard", other_core)

    cut = rows // 2
    halves = [own[:cut], own[cut:]]
    outer_rows = [move("rows_in", half, "shard", inwards) for half in halves]
    first_rows = move("middle", halves[0], "shard", middle)
    second_half, first_rows = tie((halves[1], first_rows))
    inner_rows = [first_rows, move("middle", second_half, "shard", middle)]
    outer_rows[1], inner_rows[1] = tie((outer_rows[1], inner_rows[1]))
    far_rows = move("rows_far", own, "shard", across_middle)

    early = outer_rows + halves + [swap("own", own)] + inner_rows
    early += [swap("rows", half) for half in outer_rows + inner_rows]
    gram, cubic = early_products(inner, rows, early)
    far_rows, gram, cubic = tie((far_rows, gram, cubic))
    late = [far_rows, swap("far", far_rows)]
    for_outer = late_products(inner, 0, rows, early, late, [gram], cubic, widths)
    for_own = late_products(inner, rows, rows, early, late, [gram], cubic, widths)

    result = jnp.zeros((4, rows, columns), jnp.bfloat16)

    def place_in(result, flip, at, part):
        return lax.dynamic_update_slice(result, part[None], (mat ^ flip, 0, at))

    begin, corner = 0, []
    for k, width in enumerate(widths):
        returned = move("rows_out", for_outer[k], "shard", outwards)
        mine = tie(jnp.where(outer, returned, for_own[k]))
        by_x = move("along_x", mine, "mat", along_x)
        by_y = move("along_y", mine, "mat", along_y)
        by_x, by_y = tie((by_x, by_y))
        if k % 2 == 0:
            corner.append(move("across_y", by_x, "mat", along_y))
        else:
            corner.append(move("across_x", by_y, "mat", along_x))
        for flip, part in enumerate((mine, by_x, by_y)):
            result = place_in(result, flip, begin, part)
        begin += width
    result = place_in(result, 3, 0, jnp.concatenate(corner, axis=1))
    return result


def solution(mesh):
    if (mesh.shape["mat"], mesh.shape["shard"]) == (4, 8):
        def shards(iterate):
            return line_shards(iterate, widths=(1280, 1280))
    else:
        shards = general_shards
    return jax.shard_map(
        shards,
        mesh=mesh,
        in_specs=(P("mat", "shard", None),),
        out_specs=P(None, "shard", None),
        check_vma=False,
    )
```

```python
import functools

import jax
import jax.numpy as jnp
from jax import lax
from jax.experimental import pallas as pl
from jax.experimental.pallas import tpu as pltpu
from jax.sharding import PartitionSpec as P

coef_a = 3.4445
coef_b = -4.775
coef_c = 2.0315

TILE = 1024
VMEM_LIMIT = 30 * 1024 * 1024


def dot_t(left, right):
    return lax.dot_general(
        left, right, (((1,), (1,)), ((), ())), preferred_element_type=jnp.float32
    )


def dot(left, right):
    return jnp.dot(left, right, preferred_element_type=jnp.float32)


def general_shards(iterate):
    own = iterate[0]
    gathered = lax.all_gather(own, "shard", axis=0, tiled=True)
    gram = dot_t(own, gathered).astype(jnp.bfloat16)
    cubic = dot(gram, gathered).astype(jnp.bfloat16)
    squared = dot_t(cubic, gathered)
    polynomial = (coef_b * gram.astype(jnp.float32) + coef_c * squared).astype(jnp.bfloat16)
    product = dot(polynomial, gathered)
    next_rows = (coef_a * own.astype(jnp.float32) + product).astype(jnp.bfloat16)
    return lax.all_gather(next_rows[None], "mat", axis=0, tiled=True)


def tiles(start, stop):
    return [pl.ds(at, min(TILE, stop - at)) for at in range(start, stop, TILE)]


def starts(blocks):
    return [sum(b.shape[0] for b in blocks[:k]) for k in range(len(blocks) + 1)]


def fetch_blocks(blocks, whole, sems):
    copies = []
    for k, (block, at) in enumerate(zip(blocks, starts(blocks))):
        target = whole.at[pl.ds(at, block.shape[0]), :]
        copies.append(pltpu.make_async_copy(block, target, sems.at[k]))
        copies[k].start()
    return copies


def early_kernel(count, *refs):
    inner, blocks, (gram, cubic, whole, sems) = refs[0], refs[1 : count + 1], refs[count + 1 :]
    left = pl.ds(0, gram.shape[0])

    @pl.when(inner[0] != 0)
    def _():
        for copy in fetch_blocks(blocks, whole, sems):
            copy.wait()
        for at in tiles(0, whole.shape[0]):
            gram[:, at] = dot_t(whole[left, :], whole[at, :]).astype(jnp.bfloat16)
        for at in tiles(0, whole.shape[1]):
            cubic[:, at] = dot(gram[...], whole[:, at])


def early_products(inner, rows, blocks):
    count = len(blocks)
    columns = blocks[0].shape[1]
    known = starts(blocks)[-1]
    return pl.pallas_call(
        functools.partial(early_kernel, count),
        out_shape=(
            jax.ShapeDtypeStruct((2 * rows, known), jnp.bfloat16),
            jax.ShapeDtypeStruct((2 * rows, columns), jnp.float32),
        ),
        in_specs=[pl.BlockSpec(memory_space=pltpu.SMEM)]
        + [pl.BlockSpec(memory_space=pltpu.HBM)] * count,
        out_specs=(pl.BlockSpec(memory_space=pltpu.VMEM),) * 2,
        scratch_shapes=[
            pltpu.VMEM((known, columns), jnp.bfloat16),
            pltpu.SemaphoreType.DMA((count,)),
        ],
        compiler_params=pltpu.CompilerParams(vmem_limit_bytes=VMEM_LIMIT),
        cost_estimate=pl.CostEstimate(
            flops=rows * known, bytes_accessed=2 * rows, transcendentals=0
        ),
    )(inner, *blocks)


def late_kernel(first, early_count, count, gram_count, widths, *refs):
    inner, refs = refs[0], refs[1:]
    blocks, grams_in = refs[:count], refs[count : count + gram_count]
    cubic_in, refs = refs[count + gram_count], refs[count + gram_count + 1 :]
    outs = refs[: len(widths)]
    whole, gram, cubic_sum, cubic, poly, sems = refs[len(widths) :]
    rows, total = gram.shape
    columns = blocks[0].shape[1]
    begin = starts(blocks)
    known = begin[early_count]
    mine = pl.ds(first, rows)
    late = pl.ds(known, total - known)

    @pl.when(inner[0] != 0)
    def _():
        copies = {}

        def fetch(name, source, target):
            copies[name] = pltpu.make_async_copy(source, target, sems.at[len(copies)])
            copies[name].start()

        def fetch_block(k):
            fetch(k, blocks[k], whole.at[pl.ds(begin[k], blocks[k].shape[0]), :])

        own = [k for k in range(early_count) if first <= begin[k] < first + rows]
        others = [k for k in range(early_count) if k not in own]
        for k in own + list(range(early_count, count)):
            fetch_block(k)
        at = 0
        for k, gram_in in enumerate(grams_in):
            width = gram_in.shape[1]
            fetch("gram%d" % k, gram_in.at[mine, :], gram.at[:, pl.ds(at, width)])
            at += width
        fetch("cubic", cubic_in.at[mine, :], cubic_sum)
        for k in others:
            fetch_block(k)

        for k in own + list(range(early_count, count)):
            copies[k].wait()
        for k in range(gram_count):
            copies["gram%d" % k].wait()
        gram[:, late] = dot_t(whole[mine, :], whole[late, :]).astype(jnp.bfloat16)
        copies["cubic"].wait()
        for at in tiles(0, columns):
            add = dot(gram[:, late], whole[late, at])
            cubic[:, at] = (cubic_sum[:, at] + add).astype(jnp.bfloat16)

        for k in others:
            copies[k].wait()
        for at in tiles(0, total):
            squared = dot_t(cubic[...], whole[at, :])
            poly[:, at] = (coef_b * gram[:, at].astype(jnp.float32) + coef_c * squared).astype(
                jnp.bfloat16
            )

        for at in tiles(0, columns):
            product = dot(poly[...], whole[:, at])
            base = whole[mine, at].astype(jnp.float32)
            new = (coef_a * base + product).astype(jnp.bfloat16)
            left = 0
            for out, width in zip(outs, widths):
                low, high = max(at.start, left), min(at.start + at.size, left + width)
                if low < high:
                    out[:, low - left : high - left] = new[:, low - at.start : high - at.start]
                left += width


def late_products(inner, first, rows, early, late, grams, cubic, widths):
    blocks = early + late
    count = len(blocks)
    columns = blocks[0].shape[1]
    total = starts(blocks)[-1]
    return pl.pallas_call(
        functools.partial(late_kernel, first, len(early), count, len(grams), widths),
        out_shape=tuple(jax.ShapeDtypeStruct((rows, w), jnp.bfloat16) for w in widths),
        in_specs=[pl.BlockSpec(memory_space=pltpu.SMEM)]
        + [pl.BlockSpec(memory_space=pltpu.HBM)] * count
        + [pl.BlockSpec(memory_space=pl.ANY)] * (len(grams) + 1),
        out_specs=tuple(pl.BlockSpec(memory_space=pltpu.VMEM) for _ in widths),
        scratch_shapes=[
            pltpu.VMEM((total, columns), jnp.bfloat16),
            pltpu.VMEM((rows, total), jnp.bfloat16),
            pltpu.VMEM((rows, columns), jnp.float32),
            pltpu.VMEM((rows, columns), jnp.bfloat16),
            pltpu.VMEM((rows, total), jnp.bfloat16),
            pltpu.SemaphoreType.DMA((count + len(grams) + 1,)),
        ],
        compiler_params=pltpu.CompilerParams(vmem_limit_bytes=VMEM_LIMIT),
        cost_estimate=pl.CostEstimate(
            flops=5 * rows * total * columns, bytes_accessed=2 * total * columns, transcendentals=0
        ),
    )(inner, *blocks, *grams, cubic)


def line_shards(iterate, widths):
    own = iterate[0]
    rows, columns = own.shape
    place = lax.axis_index("shard") // 2
    outer = (place == 0) | (place == 3)
    mat = lax.axis_index("mat")

    inner = jnp.where(outer, 0, 1).astype(jnp.int32)[None]
    tie = lax.optimization_barrier

    other_core = [(2, 3), (3, 2), (4, 5), (5, 4)]
    inwards = [(0, 2), (1, 3), (6, 4), (7, 5)]
    outwards = [(b, a) for a, b in inwards]
    middle = [(2, 4), (3, 5), (4, 2), (5, 3)]
    across_middle = [(0, 4), (1, 5), (6, 2), (7, 3)]
    along_x = [(m, m ^ 1) for m in range(4)]
    along_y = [(m, m ^ 2) for m in range(4)]

    def move(name, block, axis, pairs):
        with jax.named_scope(name):
            return lax.ppermute(block, axis, pairs)

    def swap(name, block):
        return move("swap_" + name, block, "shard", other_core)

    cut = rows // 2
    halves = [own[:cut], own[cut:]]
    inner_rows = move("middle", own, "shard", middle)
    outer_rows = [move("rows_in", half, "shard", inwards) for half in halves]
    own_swapped = swap("own", own)
    outer_rows[0], own_swapped = tie((outer_rows[0], own_swapped))
    far_rows = move("rows_far", own, "shard", across_middle)

    early = outer_rows + halves + [own_swapped, inner_rows]
    early += [swap("rows", block) for block in outer_rows + [inner_rows]]
    gram, cubic = early_products(inner, rows, early)
    far_rows, gram, cubic = tie((far_rows, gram, cubic))
    late = [far_rows, swap("far", far_rows)]
    for_outer = late_products(inner, 0, rows, early, late, [gram], cubic, widths)
    for_own = late_products(inner, rows, rows, early, late, [gram], cubic, widths)

    result = jnp.zeros((4, rows, columns), jnp.bfloat16)

    def place_in(result, flip, at, part):
        return lax.dynamic_update_slice(result, part[None], (mat ^ flip, 0, at))

    begin, corner = 0, []
    for k, width in enumerate(widths):
        returned = move("rows_out", for_outer[k], "shard", outwards)
        mine = tie(jnp.where(outer, returned, for_own[k]))
        by_x = move("along_x", mine, "mat", along_x)
        by_y = move("along_y", mine, "mat", along_y)
        by_x, by_y = tie((by_x, by_y))
        corner.append((by_x, by_y)[k % 2])
        for flip, part in enumerate((mine, by_x, by_y)):
            result = place_in(result, flip, begin, part)
        begin += width
    corner = tie(corner)
    for k, part in enumerate(corner):
        name, pairs = ("across_y", along_y) if k % 2 == 0 else ("across_x", along_x)
        corner[k] = move(name, part, "mat", pairs)
    result = place_in(result, 3, 0, jnp.concatenate(corner, axis=1))
    return result


def solution(mesh):
    if (mesh.shape["mat"], mesh.shape["shard"]) == (4, 8):
        def shards(iterate):
            return line_shards(iterate, widths=(1280, 1280))
    else:
        shards = general_shards
    return jax.shard_map(
        shards,
        mesh=mesh,
        in_specs=(P("mat", "shard", None),),
        out_specs=P(None, "shard", None),
        check_vma=False,
    )
```

```python
import functools

import jax
import jax.numpy as jnp
from jax import lax
from jax.experimental import pallas as pl
from jax.experimental.pallas import tpu as pltpu
from jax.sharding import PartitionSpec as P

coef_a = 3.4445
coef_b = -4.775
coef_c = 2.0315

TILE = 1024
VMEM_LIMIT = 30 * 1024 * 1024


def dot_t(left, right):
    return lax.dot_general(
        left, right, (((1,), (1,)), ((), ())), preferred_element_type=jnp.float32
    )


def dot(left, right):
    return jnp.dot(left, right, preferred_element_type=jnp.float32)


def general_shards(iterate):
    own = iterate[0]
    gathered = lax.all_gather(own, "shard", axis=0, tiled=True)
    gram = dot_t(own, gathered).astype(jnp.bfloat16)
    cubic = dot(gram, gathered).astype(jnp.bfloat16)
    squared = dot_t(cubic, gathered)
    polynomial = (coef_b * gram.astype(jnp.float32) + coef_c * squared).astype(jnp.bfloat16)
    product = dot(polynomial, gathered)
    next_rows = (coef_a * own.astype(jnp.float32) + product).astype(jnp.bfloat16)
    return lax.all_gather(next_rows[None], "mat", axis=0, tiled=True)


def tiles(start, stop):
    return [pl.ds(at, min(TILE, stop - at)) for at in range(start, stop, TILE)]


def starts(blocks):
    return [sum(b.shape[0] for b in blocks[:k]) for k in range(len(blocks) + 1)]


def fetch_blocks(blocks, whole, sems):
    copies = []
    for k, (block, at) in enumerate(zip(blocks, starts(blocks))):
        target = whole.at[pl.ds(at, block.shape[0]), :]
        copies.append(pltpu.make_async_copy(block, target, sems.at[k]))
        copies[k].start()
    return copies


def early_kernel(count, *refs):
    inner, blocks, (gram, cubic, whole, sems) = refs[0], refs[1 : count + 1], refs[count + 1 :]
    left = pl.ds(0, gram.shape[0])

    @pl.when(inner[0] != 0)
    def _():
        for copy in fetch_blocks(blocks, whole, sems):
            copy.wait()
        for at in tiles(0, whole.shape[0]):
            gram[:, at] = dot_t(whole[left, :], whole[at, :]).astype(jnp.bfloat16)
        for at in tiles(0, whole.shape[1]):
            cubic[:, at] = dot(gram[...], whole[:, at])


def early_products(inner, rows, blocks):
    count = len(blocks)
    columns = blocks[0].shape[1]
    known = starts(blocks)[-1]
    return pl.pallas_call(
        functools.partial(early_kernel, count),
        out_shape=(
            jax.ShapeDtypeStruct((2 * rows, known), jnp.bfloat16),
            jax.ShapeDtypeStruct((2 * rows, columns), jnp.float32),
        ),
        in_specs=[pl.BlockSpec(memory_space=pltpu.SMEM)]
        + [pl.BlockSpec(memory_space=pltpu.HBM)] * count,
        out_specs=(pl.BlockSpec(memory_space=pltpu.VMEM),) * 2,
        scratch_shapes=[
            pltpu.VMEM((known, columns), jnp.bfloat16),
            pltpu.SemaphoreType.DMA((count,)),
        ],
        compiler_params=pltpu.CompilerParams(vmem_limit_bytes=VMEM_LIMIT),
        cost_estimate=pl.CostEstimate(
            flops=rows * known, bytes_accessed=2 * rows, transcendentals=0
        ),
    )(inner, *blocks)


def late_kernel(first, early_count, count, gram_count, widths, *refs):
    inner, refs = refs[0], refs[1:]
    blocks, grams_in = refs[:count], refs[count : count + gram_count]
    cubic_in, refs = refs[count + gram_count], refs[count + gram_count + 1 :]
    outs = refs[: len(widths)]
    whole, gram, cubic_sum, cubic, poly, sems = refs[len(widths) :]
    rows, total = gram.shape
    columns = blocks[0].shape[1]
    begin = starts(blocks)
    known = begin[early_count]
    mine = pl.ds(first, rows)
    late = pl.ds(known, total - known)

    @pl.when(inner[0] != 0)
    def _():
        copies = {}

        def fetch(name, source, target):
            copies[name] = pltpu.make_async_copy(source, target, sems.at[len(copies)])
            copies[name].start()

        def fetch_block(k):
            fetch(k, blocks[k], whole.at[pl.ds(begin[k], blocks[k].shape[0]), :])

        own = [k for k in range(early_count) if first <= begin[k] < first + rows]
        others = [k for k in range(early_count) if k not in own]
        for k in own + list(range(early_count, count)):
            fetch_block(k)
        at = 0
        for k, gram_in in enumerate(grams_in):
            width = gram_in.shape[1]
            fetch("gram%d" % k, gram_in.at[mine, :], gram.at[:, pl.ds(at, width)])
            at += width
        fetch("cubic", cubic_in.at[mine, :], cubic_sum)
        for k in others:
            fetch_block(k)

        for k in own + list(range(early_count, count)):
            copies[k].wait()
        for k in range(gram_count):
            copies["gram%d" % k].wait()
        gram[:, late] = dot_t(whole[mine, :], whole[late, :]).astype(jnp.bfloat16)
        copies["cubic"].wait()
        for at in tiles(0, columns):
            add = dot(gram[:, late], whole[late, at])
            cubic[:, at] = (cubic_sum[:, at] + add).astype(jnp.bfloat16)

        for k in others:
            copies[k].wait()
        for at in tiles(0, total):
            squared = dot_t(cubic[...], whole[at, :])
            poly[:, at] = (coef_b * gram[:, at].astype(jnp.float32) + coef_c * squared).astype(
                jnp.bfloat16
            )

        for at in tiles(0, columns):
            product = dot(poly[...], whole[:, at])
            base = whole[mine, at].astype(jnp.float32)
            new = (coef_a * base + product).astype(jnp.bfloat16)
            left = 0
            for out, width in zip(outs, widths):
                low, high = max(at.start, left), min(at.start + at.size, left + width)
                if low < high:
                    out[:, low - left : high - left] = new[:, low - at.start : high - at.start]
                left += width


def late_products(inner, first, rows, early, late, grams, cubic, widths):
    blocks = early + late
    count = len(blocks)
    columns = blocks[0].shape[1]
    total = starts(blocks)[-1]
    return pl.pallas_call(
        functools.partial(late_kernel, first, len(early), count, len(grams), widths),
        out_shape=tuple(jax.ShapeDtypeStruct((rows, w), jnp.bfloat16) for w in widths),
        in_specs=[pl.BlockSpec(memory_space=pltpu.SMEM)]
        + [pl.BlockSpec(memory_space=pltpu.HBM)] * count
        + [pl.BlockSpec(memory_space=pl.ANY)] * (len(grams) + 1),
        out_specs=tuple(pl.BlockSpec(memory_space=pltpu.VMEM) for _ in widths),
        scratch_shapes=[
            pltpu.VMEM((total, columns), jnp.bfloat16),
            pltpu.VMEM((rows, total), jnp.bfloat16),
            pltpu.VMEM((rows, columns), jnp.float32),
            pltpu.VMEM((rows, columns), jnp.bfloat16),
            pltpu.VMEM((rows, total), jnp.bfloat16),
            pltpu.SemaphoreType.DMA((count + len(grams) + 1,)),
        ],
        compiler_params=pltpu.CompilerParams(vmem_limit_bytes=VMEM_LIMIT),
        cost_estimate=pl.CostEstimate(
            flops=5 * rows * total * columns, bytes_accessed=2 * total * columns, transcendentals=0
        ),
    )(inner, *blocks, *grams, cubic)


def line_shards(iterate, widths):
    own = iterate[0]
    rows, columns = own.shape
    place = lax.axis_index("shard") // 2
    outer = (place == 0) | (place == 3)
    mat = lax.axis_index("mat")

    inner = jnp.where(outer, 0, 1).astype(jnp.int32)[None]
    tie = lax.optimization_barrier

    other_core = [(2, 3), (3, 2), (4, 5), (5, 4)]
    inwards = [(0, 2), (1, 3), (6, 4), (7, 5)]
    outwards = [(b, a) for a, b in inwards]
    middle = [(2, 4), (3, 5), (4, 2), (5, 3)]
    across_middle = [(0, 4), (1, 5), (6, 2), (7, 3)]
    along_x = [(m, m ^ 1) for m in range(4)]
    along_y = [(m, m ^ 2) for m in range(4)]

    def move(name, block, axis, pairs):
        with jax.named_scope(name):
            return lax.ppermute(block, axis, pairs)

    def swap(name, block):
        return move("swap_" + name, block, "shard", other_core)

    cut = rows // 2
    halves = [own[:cut], own[cut:]]
    outer_rows = [move("rows_in", half, "shard", inwards) for half in halves]
    inner_rows = [move("middle", half, "shard", middle) for half in halves]
    far_rows = move("rows_far", own, "shard", across_middle)
    own_swapped = swap("own", own)
    outer_rows[0], own_swapped = tie((outer_rows[0], own_swapped))
    swapped = swap("rows", outer_rows[0])
    outer_rows[1], inner_rows[0], inner_rows[1], swapped = tie(
        (outer_rows[1], inner_rows[0], inner_rows[1], swapped)
    )
    early = outer_rows + halves + [own_swapped] + inner_rows
    early += [swapped] + [swap("rows", half) for half in outer_rows[1:] + inner_rows]
    gram, cubic = early_products(inner, rows, early)
    far_rows, gram, cubic = tie((far_rows, gram, cubic))
    late = [far_rows, swap("far", far_rows)]
    for_outer = late_products(inner, 0, rows, early, late, [gram], cubic, widths)
    for_own = late_products(inner, rows, rows, early, late, [gram], cubic, widths)

    result = jnp.zeros((4, rows, columns), jnp.bfloat16)

    def place_in(result, flip, at, part):
        return lax.dynamic_update_slice(result, part[None], (mat ^ flip, 0, at))

    begin, corner = 0, []
    for k, width in enumerate(widths):
        returned = move("rows_out", for_outer[k], "shard", outwards)
        mine = tie(jnp.where(outer, returned, for_own[k]))
        by_x = move("along_x", mine, "mat", along_x)
        by_y = move("along_y", mine, "mat", along_y)
        by_x, by_y = tie((by_x, by_y))
        corner.append((by_x, by_y)[k % 2])
        for flip, part in enumerate((mine, by_x, by_y)):
            result = place_in(result, flip, begin, part)
        begin += width
    corner = tie(corner)
    for k, part in enumerate(corner):
        name, pairs = ("across_y", along_y) if k % 2 == 0 else ("across_x", along_x)
        corner[k] = move(name, part, "mat", pairs)
    result = place_in(result, 3, 0, jnp.concatenate(corner, axis=1))
    return result


def solution(mesh):
    if (mesh.shape["mat"], mesh.shape["shard"]) == (4, 8):
        def shards(iterate):
            return line_shards(iterate, widths=(1280, 1280))
    else:
        shards = general_shards
    return jax.shard_map(
        shards,
        mesh=mesh,
        in_specs=(P("mat", "shard", None),),
        out_specs=P(None, "shard", None),
        check_vma=False,
    )
```

```python
import functools

import jax
import jax.numpy as jnp
from jax import lax
from jax.experimental import pallas as pl
from jax.experimental.pallas import tpu as pltpu
from jax.sharding import PartitionSpec as P

coef_a = 3.4445
coef_b = -4.775
coef_c = 2.0315

TILE = 1024
VMEM_LIMIT = 30 * 1024 * 1024


def dot_t(left, right):
    return lax.dot_general(
        left, right, (((1,), (1,)), ((), ())), preferred_element_type=jnp.float32
    )


def dot(left, right):
    return jnp.dot(left, right, preferred_element_type=jnp.float32)


def general_shards(iterate):
    own = iterate[0]
    gathered = lax.all_gather(own, "shard", axis=0, tiled=True)
    gram = dot_t(own, gathered).astype(jnp.bfloat16)
    cubic = dot(gram, gathered).astype(jnp.bfloat16)
    squared = dot_t(cubic, gathered)
    polynomial = (coef_b * gram.astype(jnp.float32) + coef_c * squared).astype(jnp.bfloat16)
    product = dot(polynomial, gathered)
    next_rows = (coef_a * own.astype(jnp.float32) + product).astype(jnp.bfloat16)
    return lax.all_gather(next_rows[None], "mat", axis=0, tiled=True)


def tiles(start, stop):
    return [pl.ds(at, min(TILE, stop - at)) for at in range(start, stop, TILE)]


def starts(blocks):
    return [sum(b.shape[0] for b in blocks[:k]) for k in range(len(blocks) + 1)]


def fetch_blocks(blocks, whole, sems):
    copies = []
    for k, (block, at) in enumerate(zip(blocks, starts(blocks))):
        target = whole.at[pl.ds(at, block.shape[0]), :]
        copies.append(pltpu.make_async_copy(block, target, sems.at[k]))
        copies[k].start()
    return copies


def early_kernel(count, *refs):
    inner, blocks, (gram, cubic, whole, sems) = refs[0], refs[1 : count + 1], refs[count + 1 :]
    left = pl.ds(0, gram.shape[0])

    @pl.when(inner[0] != 0)
    def _():
        for copy in fetch_blocks(blocks, whole, sems):
            copy.wait()
        for at in tiles(0, whole.shape[0]):
            gram[:, at] = dot_t(whole[left, :], whole[at, :]).astype(jnp.bfloat16)
        for at in tiles(0, whole.shape[1]):
            cubic[:, at] = dot(gram[...], whole[:, at])


def early_products(inner, rows, blocks):
    count = len(blocks)
    columns = blocks[0].shape[1]
    known = starts(blocks)[-1]
    return pl.pallas_call(
        functools.partial(early_kernel, count),
        out_shape=(
            jax.ShapeDtypeStruct((2 * rows, known), jnp.bfloat16),
            jax.ShapeDtypeStruct((2 * rows, columns), jnp.float32),
        ),
        in_specs=[pl.BlockSpec(memory_space=pltpu.SMEM)]
        + [pl.BlockSpec(memory_space=pltpu.HBM)] * count,
        out_specs=(pl.BlockSpec(memory_space=pltpu.VMEM),) * 2,
        scratch_shapes=[
            pltpu.VMEM((known, columns), jnp.bfloat16),
            pltpu.SemaphoreType.DMA((count,)),
        ],
        compiler_params=pltpu.CompilerParams(vmem_limit_bytes=VMEM_LIMIT),
        cost_estimate=pl.CostEstimate(
            flops=rows * known, bytes_accessed=2 * rows, transcendentals=0
        ),
    )(inner, *blocks)


def late_kernel(first, early_count, count, gram_count, widths, *refs):
    inner, refs = refs[0], refs[1:]
    blocks, grams_in = refs[:count], refs[count : count + gram_count]
    cubic_in, refs = refs[count + gram_count], refs[count + gram_count + 1 :]
    outs = refs[: len(widths)]
    whole, gram, cubic_sum, cubic, poly, sems = refs[len(widths) :]
    rows, total = gram.shape
    columns = blocks[0].shape[1]
    begin = starts(blocks)
    known = begin[early_count]
    mine = pl.ds(first, rows)
    late = pl.ds(known, total - known)

    @pl.when(inner[0] != 0)
    def _():
        copies = {}

        def fetch(name, source, target):
            copies[name] = pltpu.make_async_copy(source, target, sems.at[len(copies)])
            copies[name].start()

        def fetch_block(k):
            fetch(k, blocks[k], whole.at[pl.ds(begin[k], blocks[k].shape[0]), :])

        own = [k for k in range(early_count) if first <= begin[k] < first + rows]
        others = [k for k in range(early_count) if k not in own]
        for k in own + list(range(early_count, count)):
            fetch_block(k)
        at = 0
        for k, gram_in in enumerate(grams_in):
            width = gram_in.shape[1]
            fetch("gram%d" % k, gram_in.at[mine, :], gram.at[:, pl.ds(at, width)])
            at += width
        fetch("cubic", cubic_in.at[mine, :], cubic_sum)
        for k in others:
            fetch_block(k)

        for k in own + list(range(early_count, count)):
            copies[k].wait()
        for k in range(gram_count):
            copies["gram%d" % k].wait()
        gram[:, late] = dot_t(whole[mine, :], whole[late, :]).astype(jnp.bfloat16)
        copies["cubic"].wait()
        for at in tiles(0, columns):
            add = dot(gram[:, late], whole[late, at])
            cubic[:, at] = (cubic_sum[:, at] + add).astype(jnp.bfloat16)

        for k in others:
            copies[k].wait()
        for at in tiles(0, total):
            squared = dot_t(cubic[...], whole[at, :])
            poly[:, at] = (coef_b * gram[:, at].astype(jnp.float32) + coef_c * squared).astype(
                jnp.bfloat16
            )

        for at in tiles(0, columns):
            product = dot(poly[...], whole[:, at])
            base = whole[mine, at].astype(jnp.float32)
            new = (coef_a * base + product).astype(jnp.bfloat16)
            left = 0
            for out, width in zip(outs, widths):
                low, high = max(at.start, left), min(at.start + at.size, left + width)
                if low < high:
                    out[:, low - left : high - left] = new[:, low - at.start : high - at.start]
                left += width


def late_products(inner, first, rows, early, late, grams, cubic, widths):
    blocks = early + late
    count = len(blocks)
    columns = blocks[0].shape[1]
    total = starts(blocks)[-1]
    return pl.pallas_call(
        functools.partial(late_kernel, first, len(early), count, len(grams), widths),
        out_shape=tuple(jax.ShapeDtypeStruct((rows, w), jnp.bfloat16) for w in widths),
        in_specs=[pl.BlockSpec(memory_space=pltpu.SMEM)]
        + [pl.BlockSpec(memory_space=pltpu.HBM)] * count
        + [pl.BlockSpec(memory_space=pl.ANY)] * (len(grams) + 1),
        out_specs=tuple(pl.BlockSpec(memory_space=pltpu.VMEM) for _ in widths),
        scratch_shapes=[
            pltpu.VMEM((total, columns), jnp.bfloat16),
            pltpu.VMEM((rows, total), jnp.bfloat16),
            pltpu.VMEM((rows, columns), jnp.float32),
            pltpu.VMEM((rows, columns), jnp.bfloat16),
            pltpu.VMEM((rows, total), jnp.bfloat16),
            pltpu.SemaphoreType.DMA((count + len(grams) + 1,)),
        ],
        compiler_params=pltpu.CompilerParams(vmem_limit_bytes=VMEM_LIMIT),
        cost_estimate=pl.CostEstimate(
            flops=5 * rows * total * columns, bytes_accessed=2 * total * columns, transcendentals=0
        ),
    )(inner, *blocks, *grams, cubic)


def line_shards(iterate, widths, own_widths):
    own = iterate[0]
    rows, columns = own.shape
    place = lax.axis_index("shard") // 2
    outer = (place == 0) | (place == 3)
    mat = lax.axis_index("mat")

    inner = jnp.where(outer, 0, 1).astype(jnp.int32)[None]
    tie = lax.optimization_barrier

    other_core = [(2, 3), (3, 2), (4, 5), (5, 4)]
    inwards = [(0, 2), (1, 3), (6, 4), (7, 5)]
    outwards = [(b, a) for a, b in inwards]
    middle = [(2, 4), (3, 5), (4, 2), (5, 3)]
    across_middle = [(0, 4), (1, 5), (6, 2), (7, 3)]
    along_x = [(m, m ^ 1) for m in range(4)]
    along_y = [(m, m ^ 2) for m in range(4)]

    def move(name, block, axis, pairs):
        with jax.named_scope(name):
            return lax.ppermute(block, axis, pairs)

    def swap(name, block):
        return move("swap_" + name, block, "shard", other_core)

    outer_rows = move("rows_in", own, "shard", inwards)
    inner_rows = move("middle", own, "shard", middle)
    outer_rows = move("rows_in", own, "shard", inwards)
    inner_rows = move("middle", own, "shard", middle)
    far_rows = move("rows_far", own, "shard", across_middle)
    early = [outer_rows, own, swap("own", own), inner_rows]
    early += [swap("rows", outer_rows), swap("rows", inner_rows)]
    gram, cubic = early_products(inner, rows, early)
    far_rows, gram, cubic = tie((far_rows, gram, cubic))
    late = [far_rows, swap("far", far_rows)]
    for_outer = late_products(inner, 0, rows, early, late, [gram], cubic, widths)
    for_own = late_products(inner, rows, rows, early, late, [gram], cubic, own_widths)

    result = jnp.zeros((4, rows, columns), jnp.bfloat16)

    def place_in(result, flip, at, part):
        return lax.dynamic_update_slice(result, part[None], (mat ^ flip, 0, at))

    returned = [move("rows_out", part, "shard", outwards) for part in for_outer]
    begin, corner = 0, []
    for k, width in enumerate(own_widths):
        n = min(k, len(widths) - 1)
        at = begin - sum(widths[:n])
        mine = tie(jnp.where(outer, returned[n][:, at : at + width], for_own[k]))
        by_x = move("along_x", mine, "mat", along_x)
        by_y = move("along_y", mine, "mat", along_y)
        by_x, by_y = tie((by_x, by_y))
        if k % 2 == 0:
            corner.append(move("across_y", by_x, "mat", along_y))
        else:
            corner.append(move("across_x", by_y, "mat", along_x))
        for flip, part in enumerate((mine, by_x, by_y)):
            result = place_in(result, flip, begin, part)
        begin += width
    result = place_in(result, 3, 0, jnp.concatenate(corner, axis=1))
    return result


def solution(mesh):
    if (mesh.shape["mat"], mesh.shape["shard"]) == (4, 8):
        def shards(iterate):
            return line_shards(iterate, widths=(640, 640, 1280), own_widths=(640,) * 4)
    else:
        shards = general_shards
    return jax.shard_map(
        shards,
        mesh=mesh,
        in_specs=(P("mat", "shard", None),),
        out_specs=P(None, "shard", None),
        check_vma=False,
    )
```

```python
import functools

import jax
import jax.numpy as jnp
from jax import lax
from jax.experimental import pallas as pl
from jax.experimental.pallas import tpu as pltpu
from jax.sharding import PartitionSpec as P

coef_a = 3.4445
coef_b = -4.775
coef_c = 2.0315

TILE = 1024
VMEM_LIMIT = 30 * 1024 * 1024


def dot_t(left, right):
    return lax.dot_general(
        left, right, (((1,), (1,)), ((), ())), preferred_element_type=jnp.float32
    )


def dot(left, right):
    return jnp.dot(left, right, preferred_element_type=jnp.float32)


def general_shards(iterate):
    own = iterate[0]
    gathered = lax.all_gather(own, "shard", axis=0, tiled=True)
    gram = dot_t(own, gathered).astype(jnp.bfloat16)
    cubic = dot(gram, gathered).astype(jnp.bfloat16)
    squared = dot_t(cubic, gathered)
    polynomial = (coef_b * gram.astype(jnp.float32) + coef_c * squared).astype(jnp.bfloat16)
    product = dot(polynomial, gathered)
    next_rows = (coef_a * own.astype(jnp.float32) + product).astype(jnp.bfloat16)
    return lax.all_gather(next_rows[None], "mat", axis=0, tiled=True)


def tiles(start, stop):
    return [pl.ds(at, min(TILE, stop - at)) for at in range(start, stop, TILE)]


def starts(blocks):
    return [sum(b.shape[0] for b in blocks[:k]) for k in range(len(blocks) + 1)]


def fetch_blocks(blocks, whole, sems):
    copies = []
    for k, (block, at) in enumerate(zip(blocks, starts(blocks))):
        target = whole.at[pl.ds(at, block.shape[0]), :]
        copies.append(pltpu.make_async_copy(block, target, sems.at[k]))
        copies[k].start()
    return copies


def early_kernel(count, *refs):
    inner, blocks, (gram, cubic, whole, sems) = refs[0], refs[1 : count + 1], refs[count + 1 :]
    left = pl.ds(0, gram.shape[0])

    @pl.when(inner[0] != 0)
    def _():
        for copy in fetch_blocks(blocks, whole, sems):
            copy.wait()
        for at in tiles(0, whole.shape[0]):
            gram[:, at] = dot_t(whole[left, :], whole[at, :]).astype(jnp.bfloat16)
        for at in tiles(0, whole.shape[1]):
            cubic[:, at] = dot(gram[...], whole[:, at])


def early_products(inner, rows, blocks):
    count = len(blocks)
    columns = blocks[0].shape[1]
    known = starts(blocks)[-1]
    return pl.pallas_call(
        functools.partial(early_kernel, count),
        out_shape=(
            jax.ShapeDtypeStruct((2 * rows, known), jnp.bfloat16),
            jax.ShapeDtypeStruct((2 * rows, columns), jnp.float32),
        ),
        in_specs=[pl.BlockSpec(memory_space=pltpu.SMEM)]
        + [pl.BlockSpec(memory_space=pltpu.HBM)] * count,
        out_specs=(pl.BlockSpec(memory_space=pltpu.VMEM),) * 2,
        scratch_shapes=[
            pltpu.VMEM((known, columns), jnp.bfloat16),
            pltpu.SemaphoreType.DMA((count,)),
        ],
        compiler_params=pltpu.CompilerParams(vmem_limit_bytes=VMEM_LIMIT),
        cost_estimate=pl.CostEstimate(
            flops=rows * known, bytes_accessed=2 * rows, transcendentals=0
        ),
    )(inner, *blocks)


def late_kernel(first, early_count, count, gram_count, widths, *refs):
    inner, refs = refs[0], refs[1:]
    blocks, grams_in = refs[:count], refs[count : count + gram_count]
    cubic_in, refs = refs[count + gram_count], refs[count + gram_count + 1 :]
    outs = refs[: len(widths)]
    whole, gram, cubic_sum, cubic, poly, sems = refs[len(widths) :]
    rows, total = gram.shape
    columns = blocks[0].shape[1]
    begin = starts(blocks)
    known = begin[early_count]
    mine = pl.ds(first, rows)
    late = pl.ds(known, total - known)

    @pl.when(inner[0] != 0)
    def _():
        copies = {}

        def fetch(name, source, target):
            copies[name] = pltpu.make_async_copy(source, target, sems.at[len(copies)])
            copies[name].start()

        def fetch_block(k):
            fetch(k, blocks[k], whole.at[pl.ds(begin[k], blocks[k].shape[0]), :])

        own = [k for k in range(early_count) if first <= begin[k] < first + rows]
        others = [k for k in range(early_count) if k not in own]
        for k in own + list(range(early_count, count)):
            fetch_block(k)
        at = 0
        for k, gram_in in enumerate(grams_in):
            width = gram_in.shape[1]
            fetch("gram%d" % k, gram_in.at[mine, :], gram.at[:, pl.ds(at, width)])
            at += width
        fetch("cubic", cubic_in.at[mine, :], cubic_sum)
        for k in others:
            fetch_block(k)

        for k in own + list(range(early_count, count)):
            copies[k].wait()
        for k in range(gram_count):
            copies["gram%d" % k].wait()
        gram[:, late] = dot_t(whole[mine, :], whole[late, :]).astype(jnp.bfloat16)
        copies["cubic"].wait()
        for at in tiles(0, columns):
            add = dot(gram[:, late], whole[late, at])
            cubic[:, at] = (cubic_sum[:, at] + add).astype(jnp.bfloat16)

        for k in others:
            copies[k].wait()
        for at in tiles(0, total):
            squared = dot_t(cubic[...], whole[at, :])
            poly[:, at] = (coef_b * gram[:, at].astype(jnp.float32) + coef_c * squared).astype(
                jnp.bfloat16
            )

        for at in tiles(0, columns):
            product = dot(poly[...], whole[:, at])
            base = whole[mine, at].astype(jnp.float32)
            new = (coef_a * base + product).astype(jnp.bfloat16)
            left = 0
            for out, width in zip(outs, widths):
                low, high = max(at.start, left), min(at.start + at.size, left + width)
                if low < high:
                    out[:, low - left : high - left] = new[:, low - at.start : high - at.start]
                left += width


def late_products(inner, first, rows, early, late, grams, cubic, widths):
    blocks = early + late
    count = len(blocks)
    columns = blocks[0].shape[1]
    total = starts(blocks)[-1]
    return pl.pallas_call(
        functools.partial(late_kernel, first, len(early), count, len(grams), widths),
        out_shape=tuple(jax.ShapeDtypeStruct((rows, w), jnp.bfloat16) for w in widths),
        in_specs=[pl.BlockSpec(memory_space=pltpu.SMEM)]
        + [pl.BlockSpec(memory_space=pltpu.HBM)] * count
        + [pl.BlockSpec(memory_space=pl.ANY)] * (len(grams) + 1),
        out_specs=tuple(pl.BlockSpec(memory_space=pltpu.VMEM) for _ in widths),
        scratch_shapes=[
            pltpu.VMEM((total, columns), jnp.bfloat16),
            pltpu.VMEM((rows, total), jnp.bfloat16),
            pltpu.VMEM((rows, columns), jnp.float32),
            pltpu.VMEM((rows, columns), jnp.bfloat16),
            pltpu.VMEM((rows, total), jnp.bfloat16),
            pltpu.SemaphoreType.DMA((count + len(grams) + 1,)),
        ],
        compiler_params=pltpu.CompilerParams(vmem_limit_bytes=VMEM_LIMIT),
        cost_estimate=pl.CostEstimate(
            flops=5 * rows * total * columns, bytes_accessed=2 * total * columns, transcendentals=0
        ),
    )(inner, *blocks, *grams, cubic)


def line_shards(iterate, widths):
    own = iterate[0]
    rows, columns = own.shape
    place = lax.axis_index("shard") // 2
    outer = (place == 0) | (place == 3)
    mat = lax.axis_index("mat")

    inner = jnp.where(outer, 0, 1).astype(jnp.int32)[None]
    tie = lax.optimization_barrier

    other_core = [(2, 3), (3, 2), (4, 5), (5, 4)]
    inwards = [(0, 2), (1, 3), (6, 4), (7, 5)]
    outwards = [(b, a) for a, b in inwards]
    middle = [(2, 4), (3, 5), (4, 2), (5, 3)]
    across_middle = [(0, 4), (1, 5), (6, 2), (7, 3)]
    along_x = [(m, m ^ 1) for m in range(4)]
    along_y = [(m, m ^ 2) for m in range(4)]

    def move(name, block, axis, pairs):
        with jax.named_scope(name):
            return lax.ppermute(block, axis, pairs)

    def swap(name, block):
        return move("swap_" + name, block, "shard", other_core)

    cut = rows // 2
    halves = [own[:cut], own[cut:]]
    first_rows = move("rows_in", halves[0], "shard", inwards)
    second_half, first_rows = tie((halves[1], first_rows))
    outer_rows = [first_rows, move("rows_in", second_half, "shard", inwards)]
    inner_rows = [move("middle", half, "shard", middle) for half in halves]
    far_rows = move("rows_far", own, "shard", across_middle)

    early = outer_rows + [own, swap("own", own)] + inner_rows
    early += [swap("rows", half) for half in outer_rows + inner_rows]
    gram, cubic = early_products(inner, rows, early)
    far_rows, gram, cubic = tie((far_rows, gram, cubic))
    late = [far_rows, swap("far", far_rows)]
    for_outer = late_products(inner, 0, rows, early, late, [gram], cubic, widths)
    for_own = late_products(inner, rows, rows, early, late, [gram], cubic, widths)

    result = jnp.zeros((4, rows, columns), jnp.bfloat16)

    def place_in(result, flip, at, part):
        return lax.dynamic_update_slice(result, part[None], (mat ^ flip, 0, at))

    begin, corner = 0, []
    for k, width in enumerate(widths):
        returned = move("rows_out", for_outer[k], "shard", outwards)
        mine = tie(jnp.where(outer, returned, for_own[k]))
        by_x = move("along_x", mine, "mat", along_x)
        by_y = move("along_y", mine, "mat", along_y)
        by_x, by_y = tie((by_x, by_y))
        corner.append((by_x, by_y)[k % 2])
        for flip, part in enumerate((mine, by_x, by_y)):
            result = place_in(result, flip, begin, part)
        begin += width
    corner = tie(corner)
    for k, part in enumerate(corner):
        name, pairs = ("across_y", along_y) if k % 2 == 0 else ("across_x", along_x)
        corner[k] = move(name, part, "mat", pairs)
    result = place_in(result, 3, 0, jnp.concatenate(corner, axis=1))
    return result


def solution(mesh):
    if (mesh.shape["mat"], mesh.shape["shard"]) == (4, 8):
        def shards(iterate):
            return line_shards(iterate, widths=(1280, 1280))
    else:
        shards = general_shards
    return jax.shard_map(
        shards,
        mesh=mesh,
        in_specs=(P("mat", "shard", None),),
        out_specs=P(None, "shard", None),
        check_vma=False,
    )
```

```python
import functools

import jax
import jax.numpy as jnp
from jax import lax
from jax.experimental import pallas as pl
from jax.experimental.pallas import tpu as pltpu
from jax.sharding import PartitionSpec as P

coef_a = 3.4445
coef_b = -4.775
coef_c = 2.0315

TILE = 512
VMEM_LIMIT = 30 * 1024 * 1024


def dot_t(left, right):
    return lax.dot_general(
        left, right, (((1,), (1,)), ((), ())), preferred_element_type=jnp.float32
    )


def dot(left, right):
    return jnp.dot(left, right, preferred_element_type=jnp.float32)


def general_shards(iterate):
    own = iterate[0]
    gathered = lax.all_gather(own, "shard", axis=0, tiled=True)
    gram = dot_t(own, gathered).astype(jnp.bfloat16)
    cubic = dot(gram, gathered).astype(jnp.bfloat16)
    squared = dot_t(cubic, gathered)
    polynomial = (coef_b * gram.astype(jnp.float32) + coef_c * squared).astype(jnp.bfloat16)
    product = dot(polynomial, gathered)
    next_rows = (coef_a * own.astype(jnp.float32) + product).astype(jnp.bfloat16)
    return lax.all_gather(next_rows[None], "mat", axis=0, tiled=True)


def tiles(start, stop):
    return [pl.ds(at, min(TILE, stop - at)) for at in range(start, stop, TILE)]


def starts(blocks):
    return [sum(b.shape[0] for b in blocks[:k]) for k in range(len(blocks) + 1)]


def fetch_blocks(blocks, whole, sems):
    copies = []
    for k, (block, at) in enumerate(zip(blocks, starts(blocks))):
        target = whole.at[pl.ds(at, block.shape[0]), :]
        copies.append(pltpu.make_async_copy(block, target, sems.at[k]))
        copies[k].start()
    return copies


def early_kernel(count, *refs):
    inner, blocks, (gram, cubic, whole, sems) = refs[0], refs[1 : count + 1], refs[count + 1 :]
    left = pl.ds(0, gram.shape[0])

    @pl.when(inner[0] != 0)
    def _():
        for copy in fetch_blocks(blocks, whole, sems):
            copy.wait()
        for at in tiles(0, whole.shape[0]):
            gram[:, at] = dot_t(whole[left, :], whole[at, :]).astype(jnp.bfloat16)
        for at in tiles(0, whole.shape[1]):
            cubic[:, at] = dot(gram[...], whole[:, at])


def early_products(inner, rows, blocks):
    count = len(blocks)
    columns = blocks[0].shape[1]
    known = starts(blocks)[-1]
    return pl.pallas_call(
        functools.partial(early_kernel, count),
        out_shape=(
            jax.ShapeDtypeStruct((2 * rows, known), jnp.bfloat16),
            jax.ShapeDtypeStruct((2 * rows, columns), jnp.float32),
        ),
        in_specs=[pl.BlockSpec(memory_space=pltpu.SMEM)]
        + [pl.BlockSpec(memory_space=pltpu.HBM)] * count,
        out_specs=(pl.BlockSpec(memory_space=pltpu.VMEM),) * 2,
        scratch_shapes=[
            pltpu.VMEM((known, columns), jnp.bfloat16),
            pltpu.SemaphoreType.DMA((count,)),
        ],
        compiler_params=pltpu.CompilerParams(vmem_limit_bytes=VMEM_LIMIT),
        cost_estimate=pl.CostEstimate(
            flops=rows * known, bytes_accessed=2 * rows, transcendentals=0
        ),
    )(inner, *blocks)


def late_kernel(first, early_count, count, gram_count, widths, *refs):
    inner, refs = refs[0], refs[1:]
    blocks, grams_in = refs[:count], refs[count : count + gram_count]
    cubic_in, refs = refs[count + gram_count], refs[count + gram_count + 1 :]
    outs = refs[: len(widths)]
    whole, gram, cubic_sum, cubic, poly, sems = refs[len(widths) :]
    rows, total = gram.shape
    columns = blocks[0].shape[1]
    begin = starts(blocks)
    known = begin[early_count]
    mine = pl.ds(first, rows)
    late = pl.ds(known, total - known)

    @pl.when(inner[0] != 0)
    def _():
        copies = {}

        def fetch(name, source, target):
            copies[name] = pltpu.make_async_copy(source, target, sems.at[len(copies)])
            copies[name].start()

        def fetch_block(k):
            fetch(k, blocks[k], whole.at[pl.ds(begin[k], blocks[k].shape[0]), :])

        own = [k for k in range(early_count) if first <= begin[k] < first + rows]
        others = [k for k in range(early_count) if k not in own]
        for k in own + [early_count]:
            fetch_block(k)
        for k in range(early_count + 1, count):
            fetch_block(k)
        at = 0
        for k, gram_in in enumerate(grams_in):
            width = gram_in.shape[1]
            fetch("gram%d" % k, gram_in.at[mine, :], gram.at[:, pl.ds(at, width)])
            at += width
        fetch("cubic", cubic_in.at[mine, :], cubic_sum)
        for k in others:
            fetch_block(k)

        for k in own:
            copies[k].wait()
        for k in range(early_count, count):
            copies[k].wait()
            at = pl.ds(begin[k], blocks[k].shape[0])
            gram[:, at] = dot_t(whole[mine, :], whole[at, :]).astype(jnp.bfloat16)
        for k in range(gram_count):
            copies["gram%d" % k].wait()
        copies["cubic"].wait()
        for at in tiles(0, columns):
            add = dot(gram[:, late], whole[late, at])
            cubic[:, at] = (cubic_sum[:, at] + add).astype(jnp.bfloat16)

        for k in others:
            copies[k].wait()
        for at in tiles(0, total):
            squared = dot_t(cubic[...], whole[at, :])
            poly[:, at] = (coef_b * gram[:, at].astype(jnp.float32) + coef_c * squared).astype(
                jnp.bfloat16
            )

        for at in tiles(0, columns):
            product = dot(poly[...], whole[:, at])
            base = whole[mine, at].astype(jnp.float32)
            new = (coef_a * base + product).astype(jnp.bfloat16)
            left = 0
            for out, width in zip(outs, widths):
                low, high = max(at.start, left), min(at.start + at.size, left + width)
                if low < high:
                    out[:, low - left : high - left] = new[:, low - at.start : high - at.start]
                left += width


def late_products(inner, first, rows, early, late, grams, cubic, widths):
    blocks = early + late
    count = len(blocks)
    columns = blocks[0].shape[1]
    total = starts(blocks)[-1]
    return pl.pallas_call(
        functools.partial(late_kernel, first, len(early), count, len(grams), widths),
        out_shape=tuple(jax.ShapeDtypeStruct((rows, w), jnp.bfloat16) for w in widths),
        in_specs=[pl.BlockSpec(memory_space=pltpu.SMEM)]
        + [pl.BlockSpec(memory_space=pltpu.HBM)] * count
        + [pl.BlockSpec(memory_space=pl.ANY)] * (len(grams) + 1),
        out_specs=tuple(pl.BlockSpec(memory_space=pltpu.VMEM) for _ in widths),
        scratch_shapes=[
            pltpu.VMEM((total, columns), jnp.bfloat16),
            pltpu.VMEM((rows, total), jnp.bfloat16),
            pltpu.VMEM((rows, columns), jnp.float32),
            pltpu.VMEM((rows, columns), jnp.bfloat16),
            pltpu.VMEM((rows, total), jnp.bfloat16),
            pltpu.SemaphoreType.DMA((count + len(grams) + 1,)),
        ],
        compiler_params=pltpu.CompilerParams(vmem_limit_bytes=VMEM_LIMIT),
        cost_estimate=pl.CostEstimate(
            flops=5 * rows * total * columns, bytes_accessed=2 * total * columns, transcendentals=0
        ),
    )(inner, *blocks, *grams, cubic)


def line_shards(iterate, widths):
    own = iterate[0]
    rows, columns = own.shape
    place = lax.axis_index("shard") // 2
    outer = (place == 0) | (place == 3)
    mat = lax.axis_index("mat")

    inner = jnp.where(outer, 0, 1).astype(jnp.int32)[None]
    tie = lax.optimization_barrier

    other_core = [(2, 3), (3, 2), (4, 5), (5, 4)]
    inwards = [(0, 2), (1, 3), (6, 4), (7, 5)]
    outwards = [(b, a) for a, b in inwards]
    middle = [(2, 4), (3, 5), (4, 2), (5, 3)]
    across_middle = [(0, 4), (1, 5), (6, 2), (7, 3)]
    along_x = [(m, m ^ 1) for m in range(4)]
    along_y = [(m, m ^ 2) for m in range(4)]

    def move(name, block, axis, pairs):
        with jax.named_scope(name):
            return lax.ppermute(block, axis, pairs)

    def swap(name, block):
        return move("swap_" + name, block, "shard", other_core)

    cut = rows // 2
    halves = [own[:cut], own[cut:]]
    first_rows = move("rows_in", halves[0], "shard", inwards)
    second_half, first_rows = tie((halves[1], first_rows))
    outer_rows = [first_rows, move("rows_in", second_half, "shard", inwards)]
    inner_rows = [move("middle", half, "shard", middle) for half in halves]
    far_rows = move("rows_far", own, "shard", across_middle)

    early = outer_rows + [own, swap("own", own)] + inner_rows
    early += [swap("rows", half) for half in outer_rows + inner_rows]
    gram, cubic = early_products(inner, rows, early)
    far_rows, gram, cubic = tie((far_rows, gram, cubic))
    late = [far_rows, swap("far", far_rows)]
    for_outer = late_products(inner, 0, rows, early, late, [gram], cubic, widths)
    for_own = late_products(inner, rows, rows, early, late, [gram], cubic, widths)

    result = jnp.zeros((4, rows, columns), jnp.bfloat16)

    def place_in(result, flip, at, part):
        return lax.dynamic_update_slice(result, part[None], (mat ^ flip, 0, at))

    begin, corner = 0, []
    for k, width in enumerate(widths):
        returned = move("rows_out", for_outer[k], "shard", outwards)
        mine = tie(jnp.where(outer, returned, for_own[k]))
        by_x = move("along_x", mine, "mat", along_x)
        by_y = move("along_y", mine, "mat", along_y)
        by_x, by_y = tie((by_x, by_y))
        corner.append((by_x, by_y)[k % 2])
        for flip, part in enumerate((mine, by_x, by_y)):
            result = place_in(result, flip, begin, part)
        begin += width
    corner = tie(corner)
    for k, part in enumerate(corner):
        name, pairs = ("across_y", along_y) if k % 2 == 0 else ("across_x", along_x)
        corner[k] = move(name, part, "mat", pairs)
    result = place_in(result, 3, 0, jnp.concatenate(corner, axis=1))
    return result


def solution(mesh):
    if (mesh.shape["mat"], mesh.shape["shard"]) == (4, 8):
        def shards(iterate):
            return line_shards(iterate, widths=(1280, 1280))
    else:
        shards = general_shards
    return jax.shard_map(
        shards,
        mesh=mesh,
        in_specs=(P("mat", "shard", None),),
        out_specs=P(None, "shard", None),
        check_vma=False,
    )
```

```python
import functools

import jax
import jax.numpy as jnp
from jax import lax
from jax.experimental import pallas as pl
from jax.experimental.pallas import tpu as pltpu
from jax.sharding import PartitionSpec as P

coef_a = 3.4445
coef_b = -4.775
coef_c = 2.0315

TILE = 1024
VMEM_LIMIT = 30 * 1024 * 1024


def dot_t(left, right):
    return lax.dot_general(
        left, right, (((1,), (1,)), ((), ())), preferred_element_type=jnp.float32
    )


def dot(left, right):
    return jnp.dot(left, right, preferred_element_type=jnp.float32)


def general_shards(iterate):
    own = iterate[0]
    gathered = lax.all_gather(own, "shard", axis=0, tiled=True)
    gram = dot_t(own, gathered).astype(jnp.bfloat16)
    cubic = dot(gram, gathered).astype(jnp.bfloat16)
    squared = dot_t(cubic, gathered)
    polynomial = (coef_b * gram.astype(jnp.float32) + coef_c * squared).astype(jnp.bfloat16)
    product = dot(polynomial, gathered)
    next_rows = (coef_a * own.astype(jnp.float32) + product).astype(jnp.bfloat16)
    return lax.all_gather(next_rows[None], "mat", axis=0, tiled=True)


def tiles(start, stop):
    return [pl.ds(at, min(TILE, stop - at)) for at in range(start, stop, TILE)]


def starts(blocks):
    return [sum(b.shape[0] for b in blocks[:k]) for k in range(len(blocks) + 1)]


def fetch_blocks(blocks, whole, sems):
    copies = []
    for k, (block, at) in enumerate(zip(blocks, starts(blocks))):
        target = whole.at[pl.ds(at, block.shape[0]), :]
        copies.append(pltpu.make_async_copy(block, target, sems.at[k]))
        copies[k].start()
    return copies


def early_kernel(count, *refs):
    inner, blocks, (gram, cubic, whole, sems) = refs[0], refs[1 : count + 1], refs[count + 1 :]
    left = pl.ds(0, gram.shape[0])

    @pl.when(inner[0] != 0)
    def _():
        for copy in fetch_blocks(blocks, whole, sems):
            copy.wait()
        for at in tiles(0, whole.shape[0]):
            gram[:, at] = dot_t(whole[left, :], whole[at, :]).astype(jnp.bfloat16)
        for at in tiles(0, whole.shape[1]):
            cubic[:, at] = dot(gram[...], whole[:, at])


def early_products(inner, rows, blocks):
    count = len(blocks)
    columns = blocks[0].shape[1]
    known = starts(blocks)[-1]
    return pl.pallas_call(
        functools.partial(early_kernel, count),
        out_shape=(
            jax.ShapeDtypeStruct((2 * rows, known), jnp.bfloat16),
            jax.ShapeDtypeStruct((2 * rows, columns), jnp.float32),
        ),
        in_specs=[pl.BlockSpec(memory_space=pltpu.SMEM)]
        + [pl.BlockSpec(memory_space=pltpu.HBM)] * count,
        out_specs=(pl.BlockSpec(memory_space=pltpu.VMEM),) * 2,
        scratch_shapes=[
            pltpu.VMEM((known, columns), jnp.bfloat16),
            pltpu.SemaphoreType.DMA((count,)),
        ],
        compiler_params=pltpu.CompilerParams(vmem_limit_bytes=VMEM_LIMIT),
        cost_estimate=pl.CostEstimate(
            flops=rows * known, bytes_accessed=2 * rows, transcendentals=0
        ),
    )(inner, *blocks)


def late_kernel(first, early_count, count, gram_count, widths, *refs):
    inner, refs = refs[0], refs[1:]
    blocks, grams_in = refs[:count], refs[count : count + gram_count]
    cubic_in, refs = refs[count + gram_count], refs[count + gram_count + 1 :]
    outs = refs[: len(widths)]
    whole, gram, cubic_sum, cubic, poly, sems = refs[len(widths) :]
    rows, total = gram.shape
    columns = blocks[0].shape[1]
    begin = starts(blocks)
    known = begin[early_count]
    mine = pl.ds(first, rows)
    late = pl.ds(known, total - known)

    @pl.when(inner[0] != 0)
    def _():
        copies = {}

        def fetch(name, source, target):
            copies[name] = pltpu.make_async_copy(source, target, sems.at[len(copies)])
            copies[name].start()

        def fetch_block(k):
            fetch(k, blocks[k], whole.at[pl.ds(begin[k], blocks[k].shape[0]), :])

        own = [k for k in range(early_count) if first <= begin[k] < first + rows]
        others = [k for k in range(early_count) if k not in own]
        for k in own + list(range(early_count, count)):
            fetch_block(k)
        at = 0
        for k, gram_in in enumerate(grams_in):
            width = gram_in.shape[1]
            fetch("gram%d" % k, gram_in.at[mine, :], gram.at[:, pl.ds(at, width)])
            at += width
        fetch("cubic", cubic_in.at[mine, :], cubic_sum)
        for k in others:
            fetch_block(k)

        for k in own + list(range(early_count, count)):
            copies[k].wait()
        for k in range(gram_count):
            copies["gram%d" % k].wait()
        gram[:, late] = dot_t(whole[mine, :], whole[late, :]).astype(jnp.bfloat16)
        copies["cubic"].wait()
        for at in tiles(0, columns):
            add = dot(gram[:, late], whole[late, at])
            cubic[:, at] = (cubic_sum[:, at] + add).astype(jnp.bfloat16)

        for k in others:
            copies[k].wait()
        for at in tiles(0, total):
            squared = dot_t(cubic[...], whole[at, :])
            poly[:, at] = (coef_b * gram[:, at].astype(jnp.float32) + coef_c * squared).astype(
                jnp.bfloat16
            )

        for at in tiles(0, columns):
            product = dot(poly[...], whole[:, at])
            base = whole[mine, at].astype(jnp.float32)
            new = (coef_a * base + product).astype(jnp.bfloat16)
            left = 0
            for out, width in zip(outs, widths):
                low, high = max(at.start, left), min(at.start + at.size, left + width)
                if low < high:
                    out[:, low - left : high - left] = new[:, low - at.start : high - at.start]
                left += width


def late_products(inner, first, rows, early, late, grams, cubic, widths):
    blocks = early + late
    count = len(blocks)
    columns = blocks[0].shape[1]
    total = starts(blocks)[-1]
    return pl.pallas_call(
        functools.partial(late_kernel, first, len(early), count, len(grams), widths),
        out_shape=tuple(jax.ShapeDtypeStruct((rows, w), jnp.bfloat16) for w in widths),
        in_specs=[pl.BlockSpec(memory_space=pltpu.SMEM)]
        + [pl.BlockSpec(memory_space=pltpu.HBM)] * count
        + [pl.BlockSpec(memory_space=pl.ANY)] * (len(grams) + 1),
        out_specs=tuple(pl.BlockSpec(memory_space=pltpu.VMEM) for _ in widths),
        scratch_shapes=[
            pltpu.VMEM((total, columns), jnp.bfloat16),
            pltpu.VMEM((rows, total), jnp.bfloat16),
            pltpu.VMEM((rows, columns), jnp.float32),
            pltpu.VMEM((rows, columns), jnp.bfloat16),
            pltpu.VMEM((rows, total), jnp.bfloat16),
            pltpu.SemaphoreType.DMA((count + len(grams) + 1,)),
        ],
        compiler_params=pltpu.CompilerParams(vmem_limit_bytes=VMEM_LIMIT),
        cost_estimate=pl.CostEstimate(
            flops=5 * rows * total * columns, bytes_accessed=2 * total * columns, transcendentals=0
        ),
    )(inner, *blocks, *grams, cubic)


def line_shards(iterate, widths):
    own = iterate[0]
    rows, columns = own.shape
    place = lax.axis_index("shard") // 2
    outer = (place == 0) | (place == 3)
    mat = lax.axis_index("mat")

    inner = jnp.where(outer, 0, 1).astype(jnp.int32)[None]
    tie = lax.optimization_barrier

    other_core = [(2, 3), (3, 2), (4, 5), (5, 4)]
    inwards = [(0, 2), (1, 3), (6, 4), (7, 5)]
    outwards = [(b, a) for a, b in inwards]
    middle = [(2, 4), (3, 5), (4, 2), (5, 3)]
    across_middle = [(0, 4), (1, 5), (6, 2), (7, 3)]
    along_x = [(m, m ^ 1) for m in range(4)]
    along_y = [(m, m ^ 2) for m in range(4)]

    def move(name, block, axis, pairs):
        with jax.named_scope(name):
            return lax.ppermute(block, axis, pairs)

    def swap(name, block):
        return move("swap_" + name, block, "shard", other_core)

    inner_rows = move("middle", own, "shard", middle)
    outer_rows = move("rows_in", own, "shard", inwards)
    far_rows = move("rows_far", own, "shard", across_middle)

    early = [outer_rows, own, swap("own", own), inner_rows]
    for block, cut in ((outer_rows, rows // 2), (inner_rows, rows * 13 // 20)):
        early += [swap("rows", part) for part in (block[:cut], block[cut:])]
    gram, cubic = early_products(inner, rows, early)
    far_rows, gram, cubic = tie((far_rows, gram, cubic))
    late = [far_rows, swap("far", far_rows)]
    for_outer = late_products(inner, 0, rows, early, late, [gram], cubic, widths)
    for_own = late_products(inner, rows, rows, early, late, [gram], cubic, widths)

    result = jnp.zeros((4, rows, columns), jnp.bfloat16)

    def place_in(result, flip, at, part):
        return lax.dynamic_update_slice(result, part[None], (mat ^ flip, 0, at))

    begin, corner = 0, []
    for k, width in enumerate(widths):
        returned = move("rows_out", for_outer[k], "shard", outwards)
        mine = tie(jnp.where(outer, returned, for_own[k]))
        by_x = move("along_x", mine, "mat", along_x)
        by_y = move("along_y", mine, "mat", along_y)
        by_x, by_y = tie((by_x, by_y))
        corner.append((by_x, by_y)[k % 2])
        for flip, part in enumerate((mine, by_x, by_y)):
            result = place_in(result, flip, begin, part)
        begin += width
    corner = tie(corner)
    for k, part in enumerate(corner):
        name, pairs = ("across_y", along_y) if k % 2 == 0 else ("across_x", along_x)
        corner[k] = move(name, part, "mat", pairs)
    result = place_in(result, 3, 0, jnp.concatenate(corner, axis=1))
    return result


def solution(mesh):
    if (mesh.shape["mat"], mesh.shape["shard"]) == (4, 8):
        def shards(iterate):
            return line_shards(iterate, widths=(1280, 1280))
    else:
        shards = general_shards
    return jax.shard_map(
        shards,
        mesh=mesh,
        in_specs=(P("mat", "shard", None),),
        out_specs=P(None, "shard", None),
        check_vma=False,
    )
```

```python
import functools

import jax
import jax.numpy as jnp
from jax import lax
from jax.experimental import pallas as pl
from jax.experimental.pallas import tpu as pltpu
from jax.sharding import PartitionSpec as P

coef_a = 3.4445
coef_b = -4.775
coef_c = 2.0315

TILE = 1024
VMEM_LIMIT = 30 * 1024 * 1024


def dot_t(left, right):
    return lax.dot_general(
        left, right, (((1,), (1,)), ((), ())), preferred_element_type=jnp.float32
    )


def dot(left, right):
    return jnp.dot(left, right, preferred_element_type=jnp.float32)


def general_shards(iterate):
    own = iterate[0]
    gathered = lax.all_gather(own, "shard", axis=0, tiled=True)
    gram = dot_t(own, gathered).astype(jnp.bfloat16)
    cubic = dot(gram, gathered).astype(jnp.bfloat16)
    squared = dot_t(cubic, gathered)
    polynomial = (coef_b * gram.astype(jnp.float32) + coef_c * squared).astype(jnp.bfloat16)
    product = dot(polynomial, gathered)
    next_rows = (coef_a * own.astype(jnp.float32) + product).astype(jnp.bfloat16)
    return lax.all_gather(next_rows[None], "mat", axis=0, tiled=True)


def tiles(start, stop):
    return [pl.ds(at, min(TILE, stop - at)) for at in range(start, stop, TILE)]


def starts(blocks):
    return [sum(b.shape[0] for b in blocks[:k]) for k in range(len(blocks) + 1)]


def fetch_blocks(blocks, whole, sems):
    copies = []
    for k, (block, at) in enumerate(zip(blocks, starts(blocks))):
        target = whole.at[pl.ds(at, block.shape[0]), :]
        copies.append(pltpu.make_async_copy(block, target, sems.at[k]))
        copies[k].start()
    return copies


def early_kernel(count, *refs):
    inner, blocks, (gram, cubic, whole, sems) = refs[0], refs[1 : count + 1], refs[count + 1 :]
    left = pl.ds(0, gram.shape[0])

    @pl.when(inner[0] != 0)
    def _():
        for copy in fetch_blocks(blocks, whole, sems):
            copy.wait()
        for at in tiles(0, whole.shape[0]):
            gram[:, at] = dot_t(whole[left, :], whole[at, :]).astype(jnp.bfloat16)
        for at in tiles(0, whole.shape[1]):
            cubic[:, at] = dot(gram[...], whole[:, at])


def early_products(inner, rows, blocks):
    count = len(blocks)
    columns = blocks[0].shape[1]
    known = starts(blocks)[-1]
    return pl.pallas_call(
        functools.partial(early_kernel, count),
        out_shape=(
            jax.ShapeDtypeStruct((2 * rows, known), jnp.bfloat16),
            jax.ShapeDtypeStruct((2 * rows, columns), jnp.float32),
        ),
        in_specs=[pl.BlockSpec(memory_space=pltpu.SMEM)]
        + [pl.BlockSpec(memory_space=pltpu.HBM)] * count,
        out_specs=(pl.BlockSpec(memory_space=pltpu.VMEM),) * 2,
        scratch_shapes=[
            pltpu.VMEM((known, columns), jnp.bfloat16),
            pltpu.SemaphoreType.DMA((count,)),
        ],
        compiler_params=pltpu.CompilerParams(vmem_limit_bytes=VMEM_LIMIT),
        cost_estimate=pl.CostEstimate(
            flops=rows * known, bytes_accessed=2 * rows, transcendentals=0
        ),
    )(inner, *blocks)


def late_kernel(early_count, count, own, *refs):
    inner, refs = refs[0], refs[1:]
    blocks, gram_in, cubic_in, refs = refs[:count], refs[count], refs[count + 1], refs[count + 2 :]
    if own:
        outer_poly, out, out_more, outer_more, whole, gram, cubic_sum, cubic, poly, sems = refs
    else:
        out, poly, whole, gram, cubic_sum, cubic, sems = refs
    rows, total = gram.shape
    columns = blocks[0].shape[1]
    begin = starts(blocks)
    known = begin[early_count]
    first = rows if own else 0
    mine = pl.ds(first, rows)
    late = pl.ds(known, total - known)
    mine_poly = pl.ds(first, rows)

    @pl.when(inner[0] != 0)
    def _():
        copies = {}

        def fetch(name, source, target):
            copies[name] = pltpu.make_async_copy(source, target, sems.at[len(copies)])
            copies[name].start()

        def fetch_block(k):
            fetch(k, blocks[k], whole.at[pl.ds(begin[k], blocks[k].shape[0]), :])

        needed = [k for k in range(early_count) if first <= begin[k] < first + rows]
        others = [k for k in range(early_count) if k not in needed]
        for k in needed + list(range(early_count, count)):
            fetch_block(k)
        fetch("gram", gram_in.at[mine, :], gram.at[:, pl.ds(0, known)])
        fetch("cubic", cubic_in.at[mine, :], cubic_sum)
        for k in others:
            fetch_block(k)
        if own:
            fetch("poly", outer_poly, poly.at[pl.ds(0, rows), :])

        for k in needed + list(range(early_count, count)):
            copies[k].wait()
        copies["gram"].wait()
        gram[:, late] = dot_t(whole[mine, :], whole[late, :]).astype(jnp.bfloat16)
        copies["cubic"].wait()
        for at in tiles(0, columns):
            add = dot(gram[:, late], whole[late, at])
            cubic[:, at] = (cubic_sum[:, at] + add).astype(jnp.bfloat16)

        for k in others:
            copies[k].wait()
        for at in tiles(0, total):
            squared = dot_t(cubic[...], whole[at, :])
            poly[mine_poly, at] = (
                coef_b * gram[:, at].astype(jnp.float32) + coef_c * squared
            ).astype(jnp.bfloat16)

        def new(which, at):
            product = dot(poly[which, :], whole[:, at])
            base = whole[which, at].astype(jnp.float32)
            return (coef_a * base + product).astype(jnp.bfloat16)

        half = out.shape[1]
        out[...] = new(mine, pl.ds(0, half))
        if own:
            copies["poly"].wait()
            both = new(pl.ds(0, 2 * rows), pl.ds(half, columns - half))
            outer_more[...] = both[:rows]
            out_more[...] = both[rows:]


def late_products(inner, rows, early, late, gram, cubic, outer_poly=None):
    blocks = early + late
    count = len(blocks)
    columns = blocks[0].shape[1]
    total = starts(blocks)[-1]
    own = outer_poly is not None
    half = jax.ShapeDtypeStruct((rows, columns // 2), jnp.bfloat16)
    poly = jax.ShapeDtypeStruct((rows, total), jnp.bfloat16)
    out_shape = (half,) * 3 if own else (half, poly)
    more = [gram, cubic] + ([outer_poly] if own else [])
    scratch = [
        pltpu.VMEM((total, columns), jnp.bfloat16),
        pltpu.VMEM((rows, total), jnp.bfloat16),
        pltpu.VMEM((rows, columns), jnp.float32),
        pltpu.VMEM((rows, columns), jnp.bfloat16),
    ]
    if own:
        scratch.append(pltpu.VMEM((2 * rows, total), jnp.bfloat16))
    return pl.pallas_call(
        functools.partial(late_kernel, len(early), count, own),
        out_shape=out_shape,
        in_specs=[pl.BlockSpec(memory_space=pltpu.SMEM)]
        + [pl.BlockSpec(memory_space=pltpu.HBM)] * count
        + [pl.BlockSpec(memory_space=pl.ANY)] * len(more),
        out_specs=tuple(pl.BlockSpec(memory_space=pltpu.VMEM) for _ in out_shape),
        scratch_shapes=scratch + [pltpu.SemaphoreType.DMA((count + len(more),))],
        compiler_params=pltpu.CompilerParams(vmem_limit_bytes=VMEM_LIMIT),
        cost_estimate=pl.CostEstimate(
            flops=5 * rows * total * columns, bytes_accessed=2 * total * columns, transcendentals=0
        ),
    )(inner, *blocks, *more)


def line_shards(iterate):
    own = iterate[0]
    rows, columns = own.shape
    place = lax.axis_index("shard") // 2
    outer = (place == 0) | (place == 3)
    mat = lax.axis_index("mat")

    inner = jnp.where(outer, 0, 1).astype(jnp.int32)[None]
    tie = lax.optimization_barrier

    other_core = [(2, 3), (3, 2), (4, 5), (5, 4)]
    inwards = [(0, 2), (1, 3), (6, 4), (7, 5)]
    outwards = [(b, a) for a, b in inwards]
    middle = [(2, 4), (3, 5), (4, 2), (5, 3)]
    across_middle = [(0, 4), (1, 5), (6, 2), (7, 3)]
    along_x = [(m, m ^ 1) for m in range(4)]
    along_y = [(m, m ^ 2) for m in range(4)]

    def move(name, block, axis, pairs):
        with jax.named_scope(name):
            return lax.ppermute(block, axis, pairs)

    def swap(name, block):
        return move("swap_" + name, block, "shard", other_core)

    inner_rows = move("middle", own, "shard", middle)
    outer_rows = move("rows_in", own, "shard", inwards)
    far_rows = move("rows_far", own, "shard", across_middle)

    early = [outer_rows, own, swap("own", own), inner_rows]
    for block, cut in ((outer_rows, rows // 2), (inner_rows, rows * 13 // 20)):
        early += [swap("rows", part) for part in (block[:cut], block[cut:])]
    gram, cubic = early_products(inner, rows, early)
    far_rows, gram, cubic = tie((far_rows, gram, cubic))
    late = [far_rows, swap("far", far_rows)]
    outer_first, outer_poly = late_products(inner, rows, early, late, gram, cubic)
    own_first, own_second, outer_second = late_products(
        inner, rows, early, late, gram, cubic, outer_poly
    )
    for_outer, for_own = (outer_first, outer_second), (own_first, own_second)

    result = jnp.zeros((4, rows, columns), jnp.bfloat16)

    def place_in(result, flip, at, part):
        return lax.dynamic_update_slice(result, part[None], (mat ^ flip, 0, at))

    width, corner = columns // 2, [None, None]
    for k in (1, 0):
        returned = move("rows_out", for_outer[k], "shard", outwards)
        mine = tie(jnp.where(outer, returned, for_own[k]))
        by_x = move("along_x", mine, "mat", along_x)
        by_y = move("along_y", mine, "mat", along_y)
        by_x, by_y = tie((by_x, by_y))
        corner[k] = (by_x, by_y)[k]
        for flip, part in enumerate((mine, by_x, by_y)):
            result = place_in(result, flip, k * width, part)
    corner = tie(corner)
    corner[0] = move("across_y", corner[0], "mat", along_y)
    corner[1] = move("across_x", corner[1], "mat", along_x)
    result = place_in(result, 3, 0, jnp.concatenate(corner, axis=1))
    return result


def solution(mesh):
    if (mesh.shape["mat"], mesh.shape["shard"]) == (4, 8):
        shards = line_shards
    else:
        shards = general_shards
    return jax.shard_map(
        shards,
        mesh=mesh,
        in_specs=(P("mat", "shard", None),),
        out_specs=P(None, "shard", None),
        check_vma=False,
    )
```

```python
import functools

import jax
import jax.numpy as jnp
from jax import lax
from jax.experimental import pallas as pl
from jax.experimental.pallas import tpu as pltpu
from jax.sharding import PartitionSpec as P

coef_a = 3.4445
coef_b = -4.775
coef_c = 2.0315

TILE = 1024
VMEM_LIMIT = 30 * 1024 * 1024


def dot_t(left, right):
    return lax.dot_general(
        left, right, (((1,), (1,)), ((), ())), preferred_element_type=jnp.float32
    )


def dot(left, right):
    return jnp.dot(left, right, preferred_element_type=jnp.float32)


def general_shards(iterate):
    own = iterate[0]
    gathered = lax.all_gather(own, "shard", axis=0, tiled=True)
    gram = dot_t(own, gathered).astype(jnp.bfloat16)
    cubic = dot(gram, gathered).astype(jnp.bfloat16)
    squared = dot_t(cubic, gathered)
    polynomial = (coef_b * gram.astype(jnp.float32) + coef_c * squared).astype(jnp.bfloat16)
    product = dot(polynomial, gathered)
    next_rows = (coef_a * own.astype(jnp.float32) + product).astype(jnp.bfloat16)
    return lax.all_gather(next_rows[None], "mat", axis=0, tiled=True)


def tiles(start, stop):
    return [pl.ds(at, min(TILE, stop - at)) for at in range(start, stop, TILE)]


def starts(blocks):
    return [sum(b.shape[0] for b in blocks[:k]) for k in range(len(blocks) + 1)]


def fetch_blocks(blocks, whole, sems):
    copies = []
    for k, (block, at) in enumerate(zip(blocks, starts(blocks))):
        target = whole.at[pl.ds(at, block.shape[0]), :]
        copies.append(pltpu.make_async_copy(block, target, sems.at[k]))
        copies[k].start()
    return copies


def early_kernel(count, *refs):
    inner, blocks, (gram, cubic, whole, sems) = refs[0], refs[1 : count + 1], refs[count + 1 :]
    left = pl.ds(0, gram.shape[0])

    @pl.when(inner[0] != 0)
    def _():
        for copy in fetch_blocks(blocks, whole, sems):
            copy.wait()
        for at in tiles(0, whole.shape[0]):
            gram[:, at] = dot_t(whole[left, :], whole[at, :]).astype(jnp.bfloat16)
        for at in tiles(0, whole.shape[1]):
            cubic[:, at] = dot(gram[...], whole[:, at])


def early_products(inner, rows, blocks):
    count = len(blocks)
    columns = blocks[0].shape[1]
    known = starts(blocks)[-1]
    return pl.pallas_call(
        functools.partial(early_kernel, count),
        out_shape=(
            jax.ShapeDtypeStruct((2 * rows, known), jnp.bfloat16),
            jax.ShapeDtypeStruct((2 * rows, columns), jnp.float32),
        ),
        in_specs=[pl.BlockSpec(memory_space=pltpu.SMEM)]
        + [pl.BlockSpec(memory_space=pltpu.HBM)] * count,
        out_specs=(pl.BlockSpec(memory_space=pltpu.VMEM),) * 2,
        scratch_shapes=[
            pltpu.VMEM((known, columns), jnp.bfloat16),
            pltpu.SemaphoreType.DMA((count,)),
        ],
        compiler_params=pltpu.CompilerParams(vmem_limit_bytes=VMEM_LIMIT),
        cost_estimate=pl.CostEstimate(
            flops=rows * known, bytes_accessed=2 * rows, transcendentals=0
        ),
    )(inner, *blocks)


def late_kernel(early_count, count, own, *refs):
    inner, refs = refs[0], refs[1:]
    blocks, gram_in, cubic_in, refs = refs[:count], refs[count], refs[count + 1], refs[count + 2 :]
    if own:
        outer_poly, out, out_more, outer_more, whole, gram, cubic_sum, cubic, poly, sems = refs
    else:
        out, poly, whole, gram, cubic_sum, cubic, sems = refs
    rows, total = gram.shape
    columns = blocks[0].shape[1]
    begin = starts(blocks)
    known = begin[early_count]
    first = rows if own else 0
    mine = pl.ds(first, rows)
    late = pl.ds(known, total - known)
    mine_poly = pl.ds(first, rows)

    @pl.when(inner[0] != 0)
    def _():
        copies = {}

        def fetch(name, source, target):
            copies[name] = pltpu.make_async_copy(source, target, sems.at[len(copies)])
            copies[name].start()

        def fetch_block(k):
            fetch(k, blocks[k], whole.at[pl.ds(begin[k], blocks[k].shape[0]), :])

        needed = [k for k in range(early_count) if first <= begin[k] < first + rows]
        others = [k for k in range(early_count) if k not in needed]
        for k in needed + list(range(early_count, count)):
            fetch_block(k)
        fetch("gram", gram_in.at[mine, :], gram.at[:, pl.ds(0, known)])
        fetch("cubic", cubic_in.at[mine, :], cubic_sum)
        for k in others:
            fetch_block(k)
        if own:
            fetch("poly", outer_poly, poly.at[pl.ds(0, rows), :])

        for k in needed + list(range(early_count, count)):
            copies[k].wait()
        copies["gram"].wait()
        gram[:, late] = dot_t(whole[mine, :], whole[late, :]).astype(jnp.bfloat16)
        copies["cubic"].wait()
        for at in tiles(0, columns):
            add = dot(gram[:, late], whole[late, at])
            cubic[:, at] = (cubic_sum[:, at] + add).astype(jnp.bfloat16)

        for k in others:
            copies[k].wait()
        for at in tiles(0, total):
            squared = dot_t(cubic[...], whole[at, :])
            poly[mine_poly, at] = (
                coef_b * gram[:, at].astype(jnp.float32) + coef_c * squared
            ).astype(jnp.bfloat16)

        def new(which, at):
            product = dot(poly[which, :], whole[:, at])
            base = whole[which, at].astype(jnp.float32)
            return (coef_a * base + product).astype(jnp.bfloat16)

        half = out.shape[1]
        out[...] = new(mine, pl.ds(0, half))
        if own:
            copies["poly"].wait()
            both = new(pl.ds(0, 2 * rows), pl.ds(half, columns - half))
            outer_more[...] = both[:rows]
            out_more[...] = both[rows:]


def late_products(inner, rows, early, late, gram, cubic, outer_poly=None):
    blocks = early + late
    count = len(blocks)
    columns = blocks[0].shape[1]
    total = starts(blocks)[-1]
    own = outer_poly is not None
    half = jax.ShapeDtypeStruct((rows, columns // 2), jnp.bfloat16)
    poly = jax.ShapeDtypeStruct((rows, total), jnp.bfloat16)
    out_shape = (half,) * 3 if own else (half, poly)
    more = [gram, cubic] + ([outer_poly] if own else [])
    scratch = [
        pltpu.VMEM((total, columns), jnp.bfloat16),
        pltpu.VMEM((rows, total), jnp.bfloat16),
        pltpu.VMEM((rows, columns), jnp.float32),
        pltpu.VMEM((rows, columns), jnp.bfloat16),
    ]
    if own:
        scratch.append(pltpu.VMEM((2 * rows, total), jnp.bfloat16))
    return pl.pallas_call(
        functools.partial(late_kernel, len(early), count, own),
        out_shape=out_shape,
        in_specs=[pl.BlockSpec(memory_space=pltpu.SMEM)]
        + [pl.BlockSpec(memory_space=pltpu.HBM)] * count
        + [pl.BlockSpec(memory_space=pl.ANY)] * len(more),
        out_specs=tuple(pl.BlockSpec(memory_space=pltpu.VMEM) for _ in out_shape),
        scratch_shapes=scratch + [pltpu.SemaphoreType.DMA((count + len(more),))],
        compiler_params=pltpu.CompilerParams(vmem_limit_bytes=VMEM_LIMIT),
        cost_estimate=pl.CostEstimate(
            flops=5 * rows * total * columns, bytes_accessed=2 * total * columns, transcendentals=0
        ),
    )(inner, *blocks, *more)


def line_shards(iterate):
    own = iterate[0]
    rows, columns = own.shape
    place = lax.axis_index("shard") // 2
    outer = (place == 0) | (place == 3)
    mat = lax.axis_index("mat")

    inner = jnp.where(outer, 0, 1).astype(jnp.int32)[None]
    tie = lax.optimization_barrier

    other_core = [(2, 3), (3, 2), (4, 5), (5, 4)]
    inwards = [(0, 2), (1, 3), (6, 4), (7, 5)]
    outwards = [(b, a) for a, b in inwards]
    middle = [(2, 4), (3, 5), (4, 2), (5, 3)]
    across_middle = [(0, 4), (1, 5), (6, 2), (7, 3)]
    along_x = [(m, m ^ 1) for m in range(4)]
    along_y = [(m, m ^ 2) for m in range(4)]

    def move(name, block, axis, pairs):
        with jax.named_scope(name):
            return lax.ppermute(block, axis, pairs)

    def swap(name, block):
        return move("swap_" + name, block, "shard", other_core)

    inner_rows = move("middle", own, "shard", middle)
    outer_rows = move("rows_in", own, "shard", inwards)
    cut = rows * 13 // 20
    far_rows = [
        move("rows_far", part, "shard", across_middle) for part in (own[:cut], own[cut:])
    ]

    own_kept = pltpu.with_memory_space_constraint(own, pltpu.HBM)
    early = [outer_rows, own_kept, swap("own", own), inner_rows]
    for block, at in ((outer_rows, rows // 2), (inner_rows, rows * 11 // 20)):
        early += [swap("rows", part) for part in (block[:at], block[at:])]
    gram, cubic = early_products(inner, rows, early)
    far_rows[0], gram, cubic = tie((far_rows[0], gram, cubic))
    swapped = swap("far", far_rows[0])
    late = far_rows + [swapped, swap("far_last", far_rows[1])]
    outer_first, outer_poly = late_products(inner, rows, early, late, gram, cubic)
    own_first, own_second, outer_second = late_products(
        inner, rows, early, late, gram, cubic, outer_poly
    )
    for_outer, for_own = (outer_first, outer_second), (own_first, own_second)

    result = jnp.zeros((4, rows, columns), jnp.bfloat16)

    def place_in(result, flip, at, part):
        return lax.dynamic_update_slice(result, part[None], (mat ^ flip, 0, at))

    width, corner = columns // 2, [None, None]
    for k in (1, 0):
        returned = move("rows_out", for_outer[k], "shard", outwards)
        mine = tie(jnp.where(outer, returned, for_own[k]))
        by_x = move("along_x", mine, "mat", along_x)
        by_y = move("along_y", mine, "mat", along_y)
        by_x, by_y = tie((by_x, by_y))
        corner[k] = (by_x, by_y)[k]
        for flip, part in enumerate((mine, by_x, by_y)):
            result = place_in(result, flip, k * width, part)
    corner = tie(corner)
    corner[0] = move("across_y", corner[0], "mat", along_y)
    corner[1] = move("across_x", corner[1], "mat", along_x)
    result = place_in(result, 3, 0, jnp.concatenate(corner, axis=1))
    return result


def solution(mesh):
    if (mesh.shape["mat"], mesh.shape["shard"]) == (4, 8):
        shards = line_shards
    else:
        shards = general_shards
    return jax.shard_map(
        shards,
        mesh=mesh,
        in_specs=(P("mat", "shard", None),),
        out_specs=P(None, "shard", None),
        check_vma=False,
    )
```

```python
import functools

import jax
import jax.numpy as jnp
from jax import lax
from jax.experimental import pallas as pl
from jax.experimental.pallas import tpu as pltpu
from jax.sharding import PartitionSpec as P

coef_a = 3.4445
coef_b = -4.775
coef_c = 2.0315

TILE = 1024
VMEM_LIMIT = 30 * 1024 * 1024


def dot_t(left, right):
    return lax.dot_general(
        left, right, (((1,), (1,)), ((), ())), preferred_element_type=jnp.float32
    )


def dot(left, right):
    return jnp.dot(left, right, preferred_element_type=jnp.float32)


def general_shards(iterate):
    own = iterate[0]
    gathered = lax.all_gather(own, "shard", axis=0, tiled=True)
    gram = dot_t(own, gathered).astype(jnp.bfloat16)
    cubic = dot(gram, gathered).astype(jnp.bfloat16)
    squared = dot_t(cubic, gathered)
    polynomial = (coef_b * gram.astype(jnp.float32) + coef_c * squared).astype(jnp.bfloat16)
    product = dot(polynomial, gathered)
    next_rows = (coef_a * own.astype(jnp.float32) + product).astype(jnp.bfloat16)
    return lax.all_gather(next_rows[None], "mat", axis=0, tiled=True)


def tiles(start, stop):
    return [pl.ds(at, min(TILE, stop - at)) for at in range(start, stop, TILE)]


def starts(blocks):
    return [sum(b.shape[0] for b in blocks[:k]) for k in range(len(blocks) + 1)]


def fetch_blocks(blocks, whole, sems):
    copies = []
    for k, (block, at) in enumerate(zip(blocks, starts(blocks))):
        target = whole.at[pl.ds(at, block.shape[0]), :]
        copies.append(pltpu.make_async_copy(block, target, sems.at[k]))
        copies[k].start()
    return copies


def early_kernel(count, *refs):
    inner, blocks, (gram, cubic, whole, sems) = refs[0], refs[1 : count + 1], refs[count + 1 :]
    left = pl.ds(0, gram.shape[0])

    @pl.when(inner[0] != 0)
    def _():
        for copy in fetch_blocks(blocks, whole, sems):
            copy.wait()
        for at in tiles(0, whole.shape[0]):
            gram[:, at] = dot_t(whole[left, :], whole[at, :]).astype(jnp.bfloat16)
        for at in tiles(0, whole.shape[1]):
            cubic[:, at] = dot(gram[...], whole[:, at])


def early_products(inner, rows, blocks):
    count = len(blocks)
    columns = blocks[0].shape[1]
    known = starts(blocks)[-1]
    return pl.pallas_call(
        functools.partial(early_kernel, count),
        out_shape=(
            jax.ShapeDtypeStruct((2 * rows, known), jnp.bfloat16),
            jax.ShapeDtypeStruct((2 * rows, columns), jnp.float32),
        ),
        in_specs=[pl.BlockSpec(memory_space=pltpu.SMEM)]
        + [pl.BlockSpec(memory_space=pltpu.HBM)] * count,
        out_specs=(pl.BlockSpec(memory_space=pltpu.VMEM),) * 2,
        scratch_shapes=[
            pltpu.VMEM((known, columns), jnp.bfloat16),
            pltpu.SemaphoreType.DMA((count,)),
        ],
        compiler_params=pltpu.CompilerParams(vmem_limit_bytes=VMEM_LIMIT),
        cost_estimate=pl.CostEstimate(
            flops=rows * known, bytes_accessed=2 * rows, transcendentals=0
        ),
    )(inner, *blocks)


def late_kernel(early_count, count, own, *refs):
    inner, refs = refs[0], refs[1:]
    blocks, gram_in, cubic_in, refs = refs[:count], refs[count], refs[count + 1], refs[count + 2 :]
    if own:
        outer_poly, out, out_more, outer_more, whole, gram, cubic_sum, cubic, poly, sems = refs
    else:
        out, poly, whole, gram, cubic_sum, cubic, sems = refs
    rows, total = gram.shape
    columns = blocks[0].shape[1]
    begin = starts(blocks)
    known = begin[early_count]
    first = rows if own else 0
    mine = pl.ds(first, rows)
    late = pl.ds(known, total - known)
    mine_poly = pl.ds(first, rows)

    @pl.when(inner[0] != 0)
    def _():
        copies = {}

        def fetch(name, source, target):
            copies[name] = pltpu.make_async_copy(source, target, sems.at[len(copies)])
            copies[name].start()

        def fetch_block(k):
            fetch(k, blocks[k], whole.at[pl.ds(begin[k], blocks[k].shape[0]), :])

        needed = [k for k in range(early_count) if first <= begin[k] < first + rows]
        others = [k for k in range(early_count) if k not in needed]
        for k in needed + list(range(early_count, count)):
            fetch_block(k)
        fetch("gram", gram_in.at[mine, :], gram.at[:, pl.ds(0, known)])
        fetch("cubic", cubic_in.at[mine, :], cubic_sum)
        for k in others:
            fetch_block(k)
        if own:
            fetch("poly", outer_poly, poly.at[pl.ds(0, rows), :])

        for k in needed + list(range(early_count, count)):
            copies[k].wait()
        copies["gram"].wait()
        gram[:, late] = dot_t(whole[mine, :], whole[late, :]).astype(jnp.bfloat16)
        copies["cubic"].wait()
        for at in tiles(0, columns):
            add = dot(gram[:, late], whole[late, at])
            cubic[:, at] = (cubic_sum[:, at] + add).astype(jnp.bfloat16)

        for k in others:
            copies[k].wait()
        for at in tiles(0, total):
            squared = dot_t(cubic[...], whole[at, :])
            poly[mine_poly, at] = (
                coef_b * gram[:, at].astype(jnp.float32) + coef_c * squared
            ).astype(jnp.bfloat16)

        def new(which, at):
            product = dot(poly[which, :], whole[:, at])
            base = whole[which, at].astype(jnp.float32)
            return (coef_a * base + product).astype(jnp.bfloat16)

        half = out.shape[1]
        out[...] = new(mine, pl.ds(0, half))
        if own:
            copies["poly"].wait()
            both = new(pl.ds(0, 2 * rows), pl.ds(half, columns - half))
            outer_more[...] = both[:rows]
            out_more[...] = both[rows:]


def late_products(inner, rows, first, early, late, gram, cubic, outer_poly=None):
    blocks = early + late
    count = len(blocks)
    columns = blocks[0].shape[1]
    total = starts(blocks)[-1]
    own = outer_poly is not None
    part, rest = (
        jax.ShapeDtypeStruct((rows, width), jnp.bfloat16) for width in (first, columns - first)
    )
    poly = jax.ShapeDtypeStruct((rows, total), jnp.bfloat16)
    out_shape = (part, rest, rest) if own else (part, poly)
    more = [gram, cubic] + ([outer_poly] if own else [])
    scratch = [
        pltpu.VMEM((total, columns), jnp.bfloat16),
        pltpu.VMEM((rows, total), jnp.bfloat16),
        pltpu.VMEM((rows, columns), jnp.float32),
        pltpu.VMEM((rows, columns), jnp.bfloat16),
    ]
    if own:
        scratch.append(pltpu.VMEM((2 * rows, total), jnp.bfloat16))
    return pl.pallas_call(
        functools.partial(late_kernel, len(early), count, own),
        out_shape=out_shape,
        in_specs=[pl.BlockSpec(memory_space=pltpu.SMEM)]
        + [pl.BlockSpec(memory_space=pltpu.HBM)] * count
        + [pl.BlockSpec(memory_space=pl.ANY)] * len(more),
        out_specs=tuple(pl.BlockSpec(memory_space=pltpu.VMEM) for _ in out_shape),
        scratch_shapes=scratch + [pltpu.SemaphoreType.DMA((count + len(more),))],
        compiler_params=pltpu.CompilerParams(vmem_limit_bytes=VMEM_LIMIT),
        cost_estimate=pl.CostEstimate(
            flops=5 * rows * total * columns, bytes_accessed=2 * total * columns, transcendentals=0
        ),
    )(inner, *blocks, *more)


def line_shards(iterate):
    own = iterate[0]
    rows, columns = own.shape
    place = lax.axis_index("shard") // 2
    outer = (place == 0) | (place == 3)
    mat = lax.axis_index("mat")

    inner = jnp.where(outer, 0, 1).astype(jnp.int32)[None]
    tie = lax.optimization_barrier

    other_core = [(2, 3), (3, 2), (4, 5), (5, 4)]
    inwards = [(0, 2), (1, 3), (6, 4), (7, 5)]
    outwards = [(b, a) for a, b in inwards]
    middle = [(2, 4), (3, 5), (4, 2), (5, 3)]
    across_middle = [(0, 4), (1, 5), (6, 2), (7, 3)]
    along_x = [(m, m ^ 1) for m in range(4)]
    along_y = [(m, m ^ 2) for m in range(4)]

    def move(name, block, axis, pairs):
        with jax.named_scope(name):
            return lax.ppermute(block, axis, pairs)

    def swap(name, block):
        return move("swap_" + name, block, "shard", other_core)

    inner_rows = move("middle", own, "shard", middle)
    outer_rows = move("rows_in", own, "shard", inwards)
    cut = rows * 13 // 20
    far_rows = [
        move("rows_far", part, "shard", across_middle) for part in (own[:cut], own[cut:])
    ]

    own_kept = pltpu.with_memory_space_constraint(own, pltpu.HBM)
    early = [outer_rows, own_kept, swap("own", own), inner_rows]
    for block, at in ((outer_rows, rows // 2), (inner_rows, rows * 11 // 20)):
        early += [swap("rows", part) for part in (block[:at], block[at:])]
    gram, cubic = early_products(inner, rows, early)
    far_rows[0], gram, cubic = tie((far_rows[0], gram, cubic))
    swapped = swap("far", far_rows[0])
    late = far_rows + [swapped, swap("far_last", far_rows[1])]
    first = columns * 11 // 20
    outer_first, outer_poly = late_products(inner, rows, first, early, late, gram, cubic)
    own_first, own_second, outer_second = late_products(
        inner, rows, first, early, late, gram, cubic, outer_poly
    )
    for_outer, for_own = (outer_first, outer_second), (own_first, own_second)

    result = jnp.zeros((4, rows, columns), jnp.bfloat16)

    def place_in(result, flip, at, part):
        return lax.dynamic_update_slice(result, part[None], (mat ^ flip, 0, at))

    corner = [None, None]
    for k in (0, 1):
        returned = move("rows_out", for_outer[k], "shard", outwards)
        mine = tie(jnp.where(outer, returned, for_own[k]))
        by_x = move("along_x", mine, "mat", along_x)
        by_y = move("along_y", mine, "mat", along_y)
        by_x, by_y = tie((by_x, by_y))
        corner[k] = (by_x, by_y)[k]
        for flip, part in enumerate((mine, by_x, by_y)):
            result = place_in(result, flip, k * first, part)
    corner = tie(corner)
    corner[0] = move("across_y", corner[0], "mat", along_y)
    corner[1] = move("across_x", corner[1], "mat", along_x)
    result = place_in(result, 3, 0, jnp.concatenate(corner, axis=1))
    return result


def solution(mesh):
    if (mesh.shape["mat"], mesh.shape["shard"]) == (4, 8):
        shards = line_shards
    else:
        shards = general_shards
    return jax.shard_map(
        shards,
        mesh=mesh,
        in_specs=(P("mat", "shard", None),),
        out_specs=P(None, "shard", None),
        check_vma=False,
    )
```

```python
import functools

import jax
import jax.numpy as jnp
from jax import lax
from jax.experimental import pallas as pl
from jax.experimental.pallas import tpu as pltpu
from jax.sharding import PartitionSpec as P

coef_a = 3.4445
coef_b = -4.775
coef_c = 2.0315

TILE = 512
VMEM_LIMIT = 30 * 1024 * 1024


def dot_t(left, right):
    return lax.dot_general(
        left, right, (((1,), (1,)), ((), ())), preferred_element_type=jnp.float32
    )


def dot(left, right):
    return jnp.dot(left, right, preferred_element_type=jnp.float32)


def general_shards(iterate):
    own = iterate[0]
    gathered = lax.all_gather(own, "shard", axis=0, tiled=True)
    gram = dot_t(own, gathered).astype(jnp.bfloat16)
    cubic = dot(gram, gathered).astype(jnp.bfloat16)
    squared = dot_t(cubic, gathered)
    polynomial = (coef_b * gram.astype(jnp.float32) + coef_c * squared).astype(jnp.bfloat16)
    product = dot(polynomial, gathered)
    next_rows = (coef_a * own.astype(jnp.float32) + product).astype(jnp.bfloat16)
    return lax.all_gather(next_rows[None], "mat", axis=0, tiled=True)


def tiles(start, stop):
    return [pl.ds(at, min(TILE, stop - at)) for at in range(start, stop, TILE)]


def starts(blocks):
    return [sum(b.shape[0] for b in blocks[:k]) for k in range(len(blocks) + 1)]


def fetch_blocks(blocks, whole, sems):
    copies = []
    for k, (block, at) in enumerate(zip(blocks, starts(blocks))):
        target = whole.at[pl.ds(at, block.shape[0]), :]
        copies.append(pltpu.make_async_copy(block, target, sems.at[k]))
        copies[k].start()
    return copies


def early_kernel(count, *refs):
    inner, blocks, (gram, cubic, whole, sems) = refs[0], refs[1 : count + 1], refs[count + 1 :]
    left = pl.ds(0, gram.shape[0])

    @pl.when(inner[0] != 0)
    def _():
        copies = fetch_blocks(blocks, whole, sems)
        for at in tiles(0, whole.shape[0]):
            while copies and starts(blocks)[count - len(copies)] < at.start + at.size:
                copies.pop(0).wait()
            gram[:, at] = dot_t(whole[left, :], whole[at, :]).astype(jnp.bfloat16)
        for at in tiles(0, whole.shape[1]):
            cubic[:, at] = dot(gram[...], whole[:, at])


def early_products(inner, rows, blocks):
    count = len(blocks)
    columns = blocks[0].shape[1]
    known = starts(blocks)[-1]
    return pl.pallas_call(
        functools.partial(early_kernel, count),
        out_shape=(
            jax.ShapeDtypeStruct((2 * rows, known), jnp.bfloat16),
            jax.ShapeDtypeStruct((2 * rows, columns), jnp.float32),
        ),
        in_specs=[pl.BlockSpec(memory_space=pltpu.SMEM)]
        + [pl.BlockSpec(memory_space=pltpu.HBM)] * count,
        out_specs=(pl.BlockSpec(memory_space=pltpu.VMEM),) * 2,
        scratch_shapes=[
            pltpu.VMEM((known, columns), jnp.bfloat16),
            pltpu.SemaphoreType.DMA((count,)),
        ],
        compiler_params=pltpu.CompilerParams(vmem_limit_bytes=VMEM_LIMIT),
        cost_estimate=pl.CostEstimate(
            flops=rows * known, bytes_accessed=2 * rows, transcendentals=0
        ),
    )(inner, *blocks)


def late_kernel(early_count, count, own, *refs):
    inner, refs = refs[0], refs[1:]
    blocks, gram_in, cubic_in, refs = refs[:count], refs[count], refs[count + 1], refs[count + 2 :]
    if own:
        outer_poly, out, out_more, outer_more, whole, gram, cubic_sum, cubic, poly, sems = refs
    else:
        out, poly, whole, gram, cubic_sum, cubic, sems = refs
    rows, total = gram.shape
    columns = blocks[0].shape[1]
    begin = starts(blocks)
    known = begin[early_count]
    first = rows if own else 0
    mine = pl.ds(first, rows)
    late = pl.ds(known, total - known)
    mine_poly = pl.ds(first, rows)

    @pl.when(inner[0] != 0)
    def _():
        copies = {}

        def fetch(name, source, target):
            copies[name] = pltpu.make_async_copy(source, target, sems.at[len(copies)])
            copies[name].start()

        def fetch_block(k):
            fetch(k, blocks[k], whole.at[pl.ds(begin[k], blocks[k].shape[0]), :])

        needed = [k for k in range(early_count) if first <= begin[k] < first + rows]
        others = [k for k in range(early_count) if k not in needed]
        for k in needed + list(range(early_count, count)):
            fetch_block(k)
        fetch("gram", gram_in.at[mine, :], gram.at[:, pl.ds(0, known)])
        fetch("cubic", cubic_in.at[mine, :], cubic_sum)
        for k in others:
            fetch_block(k)
        if own:
            fetch("poly", outer_poly, poly.at[pl.ds(0, rows), :])

        for k in needed + list(range(early_count, count)):
            copies[k].wait()
        copies["gram"].wait()
        gram[:, late] = dot_t(whole[mine, :], whole[late, :]).astype(jnp.bfloat16)
        copies["cubic"].wait()
        for at in tiles(0, columns):
            add = dot(gram[:, late], whole[late, at])
            cubic[:, at] = (cubic_sum[:, at] + add).astype(jnp.bfloat16)

        for k in others:
            copies[k].wait()
        for at in tiles(0, total):
            squared = dot_t(cubic[...], whole[at, :])
            poly[mine_poly, at] = (
                coef_b * gram[:, at].astype(jnp.float32) + coef_c * squared
            ).astype(jnp.bfloat16)

        def new(which, at):
            product = dot(poly[which, :], whole[:, at])
            base = whole[which, at].astype(jnp.float32)
            return (coef_a * base + product).astype(jnp.bfloat16)

        half = out.shape[1]
        out[...] = new(mine, pl.ds(0, half))
        if own:
            copies["poly"].wait()
            both = new(pl.ds(0, 2 * rows), pl.ds(half, columns - half))
            outer_more[...] = both[:rows]
            out_more[...] = both[rows:]


def late_products(inner, rows, early, late, gram, cubic, outer_poly=None):
    blocks = early + late
    count = len(blocks)
    columns = blocks[0].shape[1]
    total = starts(blocks)[-1]
    own = outer_poly is not None
    half = jax.ShapeDtypeStruct((rows, columns // 2), jnp.bfloat16)
    poly = jax.ShapeDtypeStruct((rows, total), jnp.bfloat16)
    out_shape = (half,) * 3 if own else (half, poly)
    more = [gram, cubic] + ([outer_poly] if own else [])
    scratch = [
        pltpu.VMEM((total, columns), jnp.bfloat16),
        pltpu.VMEM((rows, total), jnp.bfloat16),
        pltpu.VMEM((rows, columns), jnp.float32),
        pltpu.VMEM((rows, columns), jnp.bfloat16),
    ]
    if own:
        scratch.append(pltpu.VMEM((2 * rows, total), jnp.bfloat16))
    return pl.pallas_call(
        functools.partial(late_kernel, len(early), count, own),
        out_shape=out_shape,
        in_specs=[pl.BlockSpec(memory_space=pltpu.SMEM)]
        + [pl.BlockSpec(memory_space=pltpu.HBM)] * count
        + [pl.BlockSpec(memory_space=pl.ANY)] * len(more),
        out_specs=tuple(pl.BlockSpec(memory_space=pltpu.VMEM) for _ in out_shape),
        scratch_shapes=scratch + [pltpu.SemaphoreType.DMA((count + len(more),))],
        compiler_params=pltpu.CompilerParams(vmem_limit_bytes=VMEM_LIMIT),
        cost_estimate=pl.CostEstimate(
            flops=5 * rows * total * columns, bytes_accessed=2 * total * columns, transcendentals=0
        ),
    )(inner, *blocks, *more)


def line_shards(iterate):
    own = iterate[0]
    rows, columns = own.shape
    place = lax.axis_index("shard") // 2
    outer = (place == 0) | (place == 3)
    mat = lax.axis_index("mat")

    inner = jnp.where(outer, 0, 1).astype(jnp.int32)[None]
    tie = lax.optimization_barrier

    other_core = [(2, 3), (3, 2), (4, 5), (5, 4)]
    inwards = [(0, 2), (1, 3), (6, 4), (7, 5)]
    outwards = [(b, a) for a, b in inwards]
    middle = [(2, 4), (3, 5), (4, 2), (5, 3)]
    across_middle = [(0, 4), (1, 5), (6, 2), (7, 3)]
    along_x = [(m, m ^ 1) for m in range(4)]
    along_y = [(m, m ^ 2) for m in range(4)]

    def move(name, block, axis, pairs):
        with jax.named_scope(name):
            return lax.ppermute(block, axis, pairs)

    def swap(name, block):
        return move("swap_" + name, block, "shard", other_core)

    inner_rows = move("middle", own, "shard", middle)
    outer_rows = move("rows_in", own, "shard", inwards)
    cut = rows * 13 // 20
    far_rows = [
        move("rows_far", part, "shard", across_middle) for part in (own[:cut], own[cut:])
    ]

    def kept(block):
        return pltpu.with_memory_space_constraint(block, pltpu.HBM)

    early = [outer_rows, kept(own), kept(swap("own", own)), inner_rows]
    for block, at in ((outer_rows, rows // 2), (inner_rows, rows * 11 // 20)):
        early += [swap("rows", part) for part in (block[:at], block[at:])]
    early[-1] = kept(early[-1])
    gram, cubic = early_products(inner, rows, early)
    far_rows[0], gram, cubic = tie((far_rows[0], gram, cubic))
    swapped = swap("far", far_rows[0])
    late = far_rows + [swapped, swap("far_last", far_rows[1])]
    outer_first, outer_poly = late_products(inner, rows, early, late, gram, cubic)
    own_first, own_second, outer_second = late_products(
        inner, rows, early, late, gram, cubic, outer_poly
    )
    for_outer, for_own = (outer_first, outer_second), (own_first, own_second)

    result = jnp.zeros((4, rows, columns), jnp.bfloat16)

    def place_in(result, flip, at, part):
        return lax.dynamic_update_slice(result, part[None], (mat ^ flip, 0, at))

    width, corner = columns // 2, [None, None]
    for k in (1, 0):
        returned = move("rows_out", for_outer[k], "shard", outwards)
        mine = tie(jnp.where(outer, returned, for_own[k]))
        by_x = move("along_x", mine, "mat", along_x)
        by_y = move("along_y", mine, "mat", along_y)
        by_x, by_y = tie((by_x, by_y))
        corner[k] = (by_x, by_y)[k]
        for flip, part in enumerate((mine, by_x, by_y)):
            result = place_in(result, flip, k * width, part)
    corner[0] = move("across_y", corner[0], "mat", along_y)
    corner[1] = move("across_x", corner[1], "mat", along_x)
    result = place_in(result, 3, 0, jnp.concatenate(corner, axis=1))
    return result


def solution(mesh):
    if (mesh.shape["mat"], mesh.shape["shard"]) == (4, 8):
        shards = line_shards
    else:
        shards = general_shards
    return jax.shard_map(
        shards,
        mesh=mesh,
        in_specs=(P("mat", "shard", None),),
        out_specs=P(None, "shard", None),
        check_vma=False,
    )
```

```python
import functools

import jax
import jax.numpy as jnp
from jax import lax
from jax.experimental import pallas as pl
from jax.experimental.pallas import tpu as pltpu
from jax.sharding import PartitionSpec as P

coef_a = 3.4445
coef_b = -4.775
coef_c = 2.0315

TILE = 512
VMEM_LIMIT = 30 * 1024 * 1024


def dot_t(left, right):
    return lax.dot_general(
        left, right, (((1,), (1,)), ((), ())), preferred_element_type=jnp.float32
    )


def dot(left, right):
    return jnp.dot(left, right, preferred_element_type=jnp.float32)


def general_shards(iterate):
    own = iterate[0]
    gathered = lax.all_gather(own, "shard", axis=0, tiled=True)
    gram = dot_t(own, gathered).astype(jnp.bfloat16)
    cubic = dot(gram, gathered).astype(jnp.bfloat16)
    squared = dot_t(cubic, gathered)
    polynomial = (coef_b * gram.astype(jnp.float32) + coef_c * squared).astype(jnp.bfloat16)
    product = dot(polynomial, gathered)
    next_rows = (coef_a * own.astype(jnp.float32) + product).astype(jnp.bfloat16)
    return lax.all_gather(next_rows[None], "mat", axis=0, tiled=True)


def tiles(start, stop):
    return [pl.ds(at, min(TILE, stop - at)) for at in range(start, stop, TILE)]


def starts(blocks):
    return [sum(b.shape[0] for b in blocks[:k]) for k in range(len(blocks) + 1)]


def fetch_blocks(blocks, whole, sems):
    copies = []
    for k, (block, at) in enumerate(zip(blocks, starts(blocks))):
        target = whole.at[pl.ds(at, block.shape[0]), :]
        copies.append(pltpu.make_async_copy(block, target, sems.at[k]))
        copies[k].start()
    return copies


def early_kernel(count, *refs):
    inner, blocks, (gram, cubic, whole, sems) = refs[0], refs[1 : count + 1], refs[count + 1 :]
    left = pl.ds(0, gram.shape[0])

    @pl.when(inner[0] != 0)
    def _():
        copies = fetch_blocks(blocks, whole, sems)
        for at in tiles(0, whole.shape[0]):
            while copies and starts(blocks)[count - len(copies)] < at.start + at.size:
                copies.pop(0).wait()
            gram[:, at] = dot_t(whole[left, :], whole[at, :]).astype(jnp.bfloat16)
        for at in tiles(0, whole.shape[1]):
            cubic[:, at] = dot(gram[...], whole[:, at])


def early_products(inner, rows, blocks):
    count = len(blocks)
    columns = blocks[0].shape[1]
    known = starts(blocks)[-1]
    return pl.pallas_call(
        functools.partial(early_kernel, count),
        out_shape=(
            jax.ShapeDtypeStruct((2 * rows, known), jnp.bfloat16),
            jax.ShapeDtypeStruct((2 * rows, columns), jnp.float32),
        ),
        in_specs=[pl.BlockSpec(memory_space=pltpu.SMEM)]
        + [pl.BlockSpec(memory_space=pltpu.HBM)] * count,
        out_specs=(pl.BlockSpec(memory_space=pltpu.VMEM),) * 2,
        scratch_shapes=[
            pltpu.VMEM((known, columns), jnp.bfloat16),
            pltpu.SemaphoreType.DMA((count,)),
        ],
        compiler_params=pltpu.CompilerParams(vmem_limit_bytes=VMEM_LIMIT),
        cost_estimate=pl.CostEstimate(
            flops=rows * known, bytes_accessed=2 * rows, transcendentals=0
        ),
    )(inner, *blocks)


def late_kernel(early_count, count, own, *refs):
    inner, refs = refs[0], refs[1:]
    blocks, gram_in, cubic_in, refs = refs[:count], refs[count], refs[count + 1], refs[count + 2 :]
    if own:
        outer_poly, out, out_more, outer_more, whole, gram, cubic_sum, cubic, poly, sems = refs
    else:
        out, poly, whole, gram, cubic_sum, cubic, sems = refs
    rows, total = gram.shape
    columns = blocks[0].shape[1]
    begin = starts(blocks)
    known = begin[early_count]
    first = rows if own else 0
    mine = pl.ds(first, rows)
    late = pl.ds(known, total - known)
    mine_poly = pl.ds(first, rows)

    @pl.when(inner[0] != 0)
    def _():
        copies = {}

        def fetch(name, source, target):
            copies[name] = pltpu.make_async_copy(source, target, sems.at[len(copies)])
            copies[name].start()

        def fetch_block(k):
            fetch(k, blocks[k], whole.at[pl.ds(begin[k], blocks[k].shape[0]), :])

        needed = [k for k in range(early_count) if first <= begin[k] < first + rows]
        others = [k for k in range(early_count) if k not in needed]
        for k in needed + list(range(early_count, count)):
            fetch_block(k)
        fetch("gram", gram_in.at[mine, :], gram.at[:, pl.ds(0, known)])
        fetch("cubic", cubic_in.at[mine, :], cubic_sum)
        for k in others:
            fetch_block(k)
        if own:
            fetch("poly", outer_poly, poly.at[pl.ds(0, rows), :])

        for k in needed + list(range(early_count, count)):
            copies[k].wait()
        copies["gram"].wait()
        gram[:, late] = dot_t(whole[mine, :], whole[late, :]).astype(jnp.bfloat16)
        copies["cubic"].wait()
        for at in tiles(0, columns):
            add = dot(gram[:, late], whole[late, at])
            cubic[:, at] = (cubic_sum[:, at] + add).astype(jnp.bfloat16)

        for k in others:
            copies[k].wait()
        for at in tiles(0, total):
            squared = dot_t(cubic[...], whole[at, :])
            poly[mine_poly, at] = (
                coef_b * gram[:, at].astype(jnp.float32) + coef_c * squared
            ).astype(jnp.bfloat16)

        def new(which, at):
            product = dot(poly[which, :], whole[:, at])
            base = whole[which, at].astype(jnp.float32)
            return (coef_a * base + product).astype(jnp.bfloat16)

        half = out.shape[1]
        out[...] = new(mine, pl.ds(0, half))
        if own:
            copies["poly"].wait()
            both = new(pl.ds(0, 2 * rows), pl.ds(half, columns - half))
            outer_more[...] = both[:rows]
            out_more[...] = both[rows:]


def late_products(inner, rows, early, late, gram, cubic, outer_poly=None):
    blocks = early + late
    count = len(blocks)
    columns = blocks[0].shape[1]
    total = starts(blocks)[-1]
    own = outer_poly is not None
    half = jax.ShapeDtypeStruct((rows, columns // 2), jnp.bfloat16)
    poly = jax.ShapeDtypeStruct((rows, total), jnp.bfloat16)
    out_shape = (half,) * 3 if own else (half, poly)
    more = [gram, cubic] + ([outer_poly] if own else [])
    scratch = [
        pltpu.VMEM((total, columns), jnp.bfloat16),
        pltpu.VMEM((rows, total), jnp.bfloat16),
        pltpu.VMEM((rows, columns), jnp.float32),
        pltpu.VMEM((rows, columns), jnp.bfloat16),
    ]
    if own:
        scratch.append(pltpu.VMEM((2 * rows, total), jnp.bfloat16))
    return pl.pallas_call(
        functools.partial(late_kernel, len(early), count, own),
        out_shape=out_shape,
        in_specs=[pl.BlockSpec(memory_space=pltpu.SMEM)]
        + [pl.BlockSpec(memory_space=pltpu.HBM)] * count
        + [pl.BlockSpec(memory_space=pl.ANY)] * len(more),
        out_specs=tuple(pl.BlockSpec(memory_space=pltpu.VMEM) for _ in out_shape),
        scratch_shapes=scratch + [pltpu.SemaphoreType.DMA((count + len(more),))],
        compiler_params=pltpu.CompilerParams(vmem_limit_bytes=VMEM_LIMIT),
        cost_estimate=pl.CostEstimate(
            flops=5 * rows * total * columns, bytes_accessed=2 * total * columns, transcendentals=0
        ),
    )(inner, *blocks, *more)


def line_shards(iterate):
    own = iterate[0]
    rows, columns = own.shape
    place = lax.axis_index("shard") // 2
    outer = (place == 0) | (place == 3)
    mat = lax.axis_index("mat")

    inner = jnp.where(outer, 0, 1).astype(jnp.int32)[None]
    tie = lax.optimization_barrier

    other_core = [(2, 3), (3, 2), (4, 5), (5, 4)]
    inwards = [(0, 2), (1, 3), (6, 4), (7, 5)]
    outwards = [(b, a) for a, b in inwards]
    middle = [(2, 4), (3, 5), (4, 2), (5, 3)]
    across_middle = [(0, 4), (1, 5), (6, 2), (7, 3)]
    along_x = [(m, m ^ 1) for m in range(4)]
    along_y = [(m, m ^ 2) for m in range(4)]

    def move(name, block, axis, pairs):
        with jax.named_scope(name):
            return lax.ppermute(block, axis, pairs)

    def swap(name, block):
        return move("swap_" + name, block, "shard", other_core)

    inner_rows = move("middle", own, "shard", middle)
    outer_rows = move("rows_in", own, "shard", inwards)
    cut = rows * 13 // 20
    far_rows = [
        move("rows_far", part, "shard", across_middle) for part in (own[:cut], own[cut:])
    ]

    def kept(block):
        return pltpu.with_memory_space_constraint(block, pltpu.HBM)

    early = [outer_rows, kept(own), kept(swap("own", own)), inner_rows]
    for block, at in ((outer_rows, rows // 2), (inner_rows, rows * 11 // 20)):
        early += [swap("rows", part) for part in (block[:at], block[at:])]
    early[-1] = kept(early[-1])
    gram, cubic = early_products(inner, rows, early)
    far_rows[0], gram, cubic = tie((far_rows[0], gram, cubic))
    swapped = swap("far", far_rows[0])
    late = far_rows + [swapped, swap("far_last", far_rows[1])]
    outer_first, outer_poly = late_products(inner, rows, early, late, gram, cubic)
    own_first, own_second, outer_second = late_products(
        inner, rows, early, late, gram, cubic, outer_poly
    )
    for_outer, for_own = (outer_first, outer_second), (own_first, own_second)

    result = jnp.zeros((4, rows, columns), jnp.bfloat16)

    def place_in(result, flip, at, part):
        return lax.dynamic_update_slice(result, part[None], (mat ^ flip, 0, at))

    width, corner = columns // 2, [None, None]
    for k in (1, 0):
        returned = move("rows_out", for_outer[k], "shard", outwards)
        mine = tie(jnp.where(outer, returned, for_own[k]))
        by_x = move("along_x", mine, "mat", along_x)
        by_y = move("along_y", mine, "mat", along_y)
        by_x, by_y = tie((by_x, by_y))
        corner[k] = (by_x, by_y)[k]
        for flip, part in enumerate((mine, by_x, by_y)):
            result = place_in(result, flip, k * width, part)
    corner = tie(corner)
    corner[0] = move("across_y", corner[0], "mat", along_y)
    corner[1] = move("across_x", corner[1], "mat", along_x)
    result = place_in(result, 3, 0, jnp.concatenate(corner, axis=1))
    return result


def solution(mesh):
    if (mesh.shape["mat"], mesh.shape["shard"]) == (4, 8):
        shards = line_shards
    else:
        shards = general_shards
    return jax.shard_map(
        shards,
        mesh=mesh,
        in_specs=(P("mat", "shard", None),),
        out_specs=P(None, "shard", None),
        check_vma=False,
    )
```

```python
import functools

import jax
import jax.numpy as jnp
from jax import lax
from jax.experimental import pallas as pl
from jax.experimental.pallas import tpu as pltpu
from jax.sharding import PartitionSpec as P

coef_a = 3.4445
coef_b = -4.775
coef_c = 2.0315

TILE = 512
VMEM_LIMIT = 30 * 1024 * 1024


def dot_t(left, right):
    return lax.dot_general(
        left, right, (((1,), (1,)), ((), ())), preferred_element_type=jnp.float32
    )


def dot(left, right):
    return jnp.dot(left, right, preferred_element_type=jnp.float32)


def general_shards(iterate):
    own = iterate[0]
    gathered = lax.all_gather(own, "shard", axis=0, tiled=True)
    gram = dot_t(own, gathered).astype(jnp.bfloat16)
    cubic = dot(gram, gathered).astype(jnp.bfloat16)
    squared = dot_t(cubic, gathered)
    polynomial = (coef_b * gram.astype(jnp.float32) + coef_c * squared).astype(jnp.bfloat16)
    product = dot(polynomial, gathered)
    next_rows = (coef_a * own.astype(jnp.float32) + product).astype(jnp.bfloat16)
    return lax.all_gather(next_rows[None], "mat", axis=0, tiled=True)


def tiles(start, stop):
    return [pl.ds(at, min(TILE, stop - at)) for at in range(start, stop, TILE)]


def starts(blocks):
    return [sum(b.shape[0] for b in blocks[:k]) for k in range(len(blocks) + 1)]


def fetch_blocks(blocks, whole, sems):
    copies = []
    for k, (block, at) in enumerate(zip(blocks, starts(blocks))):
        target = whole.at[pl.ds(at, block.shape[0]), :]
        copies.append(pltpu.make_async_copy(block, target, sems.at[k]))
        copies[k].start()
    return copies


def early_kernel(count, *refs):
    inner, blocks, (gram, cubic, whole, sems) = refs[0], refs[1 : count + 1], refs[count + 1 :]
    left = pl.ds(0, gram.shape[0])

    @pl.when(inner[0] != 0)
    def _():
        copies = fetch_blocks(blocks, whole, sems)
        for at in tiles(0, whole.shape[0]):
            while copies and starts(blocks)[count - len(copies)] < at.start + at.size:
                copies.pop(0).wait()
            gram[:, at] = dot_t(whole[left, :], whole[at, :]).astype(jnp.bfloat16)
        for at in tiles(0, whole.shape[1]):
            cubic[:, at] = dot(gram[...], whole[:, at])


def early_products(inner, rows, blocks):
    count = len(blocks)
    columns = blocks[0].shape[1]
    known = starts(blocks)[-1]
    return pl.pallas_call(
        functools.partial(early_kernel, count),
        out_shape=(
            jax.ShapeDtypeStruct((2 * rows, known), jnp.bfloat16),
            jax.ShapeDtypeStruct((2 * rows, columns), jnp.float32),
        ),
        in_specs=[pl.BlockSpec(memory_space=pltpu.SMEM)]
        + [pl.BlockSpec(memory_space=pltpu.HBM)] * count,
        out_specs=(pl.BlockSpec(memory_space=pltpu.VMEM),) * 2,
        scratch_shapes=[
            pltpu.VMEM((known, columns), jnp.bfloat16),
            pltpu.SemaphoreType.DMA((count,)),
        ],
        compiler_params=pltpu.CompilerParams(vmem_limit_bytes=VMEM_LIMIT),
        cost_estimate=pl.CostEstimate(
            flops=rows * known, bytes_accessed=2 * rows, transcendentals=0
        ),
    )(inner, *blocks)


def late_kernel(early_count, count, own, *refs):
    inner, refs = refs[0], refs[1:]
    blocks, gram_in, cubic_in, refs = refs[:count], refs[count], refs[count + 1], refs[count + 2 :]
    if own:
        outer_poly, out, out_more, outer_more, whole, gram, cubic_sum, cubic, poly, sems = refs
    else:
        out, poly, whole, gram, cubic_sum, cubic, sems = refs
    rows, total = gram.shape
    columns = blocks[0].shape[1]
    begin = starts(blocks)
    known = begin[early_count]
    first = rows if own else 0
    mine = pl.ds(first, rows)
    late = pl.ds(known, total - known)
    mine_poly = pl.ds(first, rows)

    @pl.when(inner[0] != 0)
    def _():
        copies = {}

        def fetch(name, source, target):
            copies[name] = pltpu.make_async_copy(source, target, sems.at[len(copies)])
            copies[name].start()

        def fetch_block(k):
            fetch(k, blocks[k], whole.at[pl.ds(begin[k], blocks[k].shape[0]), :])

        needed = [k for k in range(early_count) if first <= begin[k] < first + rows]
        others = [k for k in range(early_count) if k not in needed]
        for k in needed + list(range(early_count, count)):
            fetch_block(k)
        fetch("gram", gram_in.at[mine, :], gram.at[:, pl.ds(0, known)])
        fetch("cubic", cubic_in.at[mine, :], cubic_sum)
        for k in others:
            fetch_block(k)
        if own:
            fetch("poly", outer_poly, poly.at[pl.ds(0, rows), :])

        for k in needed + list(range(early_count, count)):
            copies[k].wait()
        copies["gram"].wait()
        gram[:, late] = dot_t(whole[mine, :], whole[late, :]).astype(jnp.bfloat16)
        copies["cubic"].wait()
        for at in tiles(0, columns):
            add = dot(gram[:, late], whole[late, at])
            cubic[:, at] = (cubic_sum[:, at] + add).astype(jnp.bfloat16)

        for k in others:
            copies[k].wait()
        for at in tiles(0, total):
            squared = dot_t(cubic[...], whole[at, :])
            poly[mine_poly, at] = (
                coef_b * gram[:, at].astype(jnp.float32) + coef_c * squared
            ).astype(jnp.bfloat16)

        def new(which, at):
            product = dot(poly[which, :], whole[:, at])
            base = whole[which, at].astype(jnp.float32)
            return (coef_a * base + product).astype(jnp.bfloat16)

        half = out.shape[1]
        out[...] = new(mine, pl.ds(0, half))
        if own:
            copies["poly"].wait()
            both = new(pl.ds(0, 2 * rows), pl.ds(half, columns - half))
            outer_more[...] = both[:rows]
            out_more[...] = both[rows:]


def late_products(inner, rows, early, late, gram, cubic, outer_poly=None):
    blocks = early + late
    count = len(blocks)
    columns = blocks[0].shape[1]
    total = starts(blocks)[-1]
    own = outer_poly is not None
    half = jax.ShapeDtypeStruct((rows, columns // 2), jnp.bfloat16)
    poly = jax.ShapeDtypeStruct((rows, total), jnp.bfloat16)
    out_shape = (half,) * 3 if own else (half, poly)
    more = [gram, cubic] + ([outer_poly] if own else [])
    scratch = [
        pltpu.VMEM((total, columns), jnp.bfloat16),
        pltpu.VMEM((rows, total), jnp.bfloat16),
        pltpu.VMEM((rows, columns), jnp.float32),
        pltpu.VMEM((rows, columns), jnp.bfloat16),
    ]
    if own:
        scratch.append(pltpu.VMEM((2 * rows, total), jnp.bfloat16))
    return pl.pallas_call(
        functools.partial(late_kernel, len(early), count, own),
        out_shape=out_shape,
        in_specs=[pl.BlockSpec(memory_space=pltpu.SMEM)]
        + [pl.BlockSpec(memory_space=pltpu.HBM)] * count
        + [pl.BlockSpec(memory_space=pl.ANY)] * len(more),
        out_specs=tuple(pl.BlockSpec(memory_space=pltpu.VMEM) for _ in out_shape),
        scratch_shapes=scratch + [pltpu.SemaphoreType.DMA((count + len(more),))],
        compiler_params=pltpu.CompilerParams(vmem_limit_bytes=VMEM_LIMIT),
        cost_estimate=pl.CostEstimate(
            flops=5 * rows * total * columns, bytes_accessed=2 * total * columns, transcendentals=0
        ),
    )(inner, *blocks, *more)


def line_shards(iterate):
    own = iterate[0]
    rows, columns = own.shape
    place = lax.axis_index("shard") // 2
    outer = (place == 0) | (place == 3)
    mat = lax.axis_index("mat")

    inner = jnp.where(outer, 0, 1).astype(jnp.int32)[None]
    tie = lax.optimization_barrier

    other_core = [(2, 3), (3, 2), (4, 5), (5, 4)]
    inwards = [(0, 2), (1, 3), (6, 4), (7, 5)]
    outwards = [(b, a) for a, b in inwards]
    middle = [(2, 4), (3, 5), (4, 2), (5, 3)]
    across_middle = [(0, 4), (1, 5), (6, 2), (7, 3)]
    along_x = [(m, m ^ 1) for m in range(4)]
    along_y = [(m, m ^ 2) for m in range(4)]

    def move(name, block, axis, pairs):
        with jax.named_scope(name):
            return lax.ppermute(block, axis, pairs)

    def swap(name, block):
        return move("swap_" + name, block, "shard", other_core)

    inner_rows = move("middle", own, "shard", middle)
    outer_rows = move("rows_in", own, "shard", inwards)
    cut = rows * 13 // 20
    far_rows = [
        move("rows_far", part, "shard", across_middle) for part in (own[:cut], own[cut:])
    ]

    def kept(block):
        return pltpu.with_memory_space_constraint(block, pltpu.HBM)

    early = [outer_rows, kept(own), kept(swap("own", own)), inner_rows]
    for block, at in ((outer_rows, rows // 2), (inner_rows, rows * 11 // 20)):
        early += [swap("rows", part) for part in (block[:at], block[at:])]
    early[-1] = kept(early[-1])
    gram, cubic = early_products(inner, rows, early)
    far_rows[0], gram, cubic = tie((far_rows[0], gram, cubic))
    swapped = swap("far", far_rows[0])
    late = far_rows + [swapped, swap("far_last", far_rows[1])]
    outer_first, outer_poly = late_products(inner, rows, early, late, gram, cubic)
    own_first, own_second, outer_second = late_products(
        inner, rows, early, late, gram, cubic, outer_poly
    )
    for_outer, for_own = (outer_first, outer_second), (own_first, own_second)

    result = jnp.zeros((4, rows, columns), jnp.bfloat16)

    def place_in(result, flip, at, part):
        return lax.dynamic_update_slice(result, part[None], (mat ^ flip, 0, at))

    width, corner = columns // 2, [None, None]
    for k in (1, 0):
        returned = move("rows_out", for_outer[k], "shard", outwards)
        mine = tie(jnp.where(outer, returned, for_own[k]))
        by_x = move("along_x", mine, "mat", along_x)
        by_y = move("along_y", mine, "mat", along_y)
        by_x, by_y = tie((by_x, by_y))
        corner[k] = (by_y, by_x)[k]
        for flip, part in enumerate((mine, by_x, by_y)):
            result = place_in(result, flip, k * width, part)
    corner = tie(corner)
    corner[0] = move("across_x", corner[0], "mat", along_x)
    corner[1] = move("across_y", corner[1], "mat", along_y)
    result = place_in(result, 3, 0, jnp.concatenate(corner, axis=1))
    return result


def solution(mesh):
    if (mesh.shape["mat"], mesh.shape["shard"]) == (4, 8):
        shards = line_shards
    else:
        shards = general_shards
    return jax.shard_map(
        shards,
        mesh=mesh,
        in_specs=(P("mat", "shard", None),),
        out_specs=P(None, "shard", None),
        check_vma=False,
    )
```

```python
import functools

import jax
import jax.numpy as jnp
from jax import lax
from jax.experimental import pallas as pl
from jax.experimental.pallas import tpu as pltpu
from jax.sharding import PartitionSpec as P

coef_a = 3.4445
coef_b = -4.775
coef_c = 2.0315

TILE = 512
VMEM_LIMIT = 30 * 1024 * 1024


def dot_t(left, right):
    return lax.dot_general(
        left, right, (((1,), (1,)), ((), ())), preferred_element_type=jnp.float32
    )


def dot(left, right):
    return jnp.dot(left, right, preferred_element_type=jnp.float32)


def general_shards(iterate):
    own = iterate[0]
    gathered = lax.all_gather(own, "shard", axis=0, tiled=True)
    gram = dot_t(own, gathered).astype(jnp.bfloat16)
    cubic = dot(gram, gathered).astype(jnp.bfloat16)
    squared = dot_t(cubic, gathered)
    polynomial = (coef_b * gram.astype(jnp.float32) + coef_c * squared).astype(jnp.bfloat16)
    product = dot(polynomial, gathered)
    next_rows = (coef_a * own.astype(jnp.float32) + product).astype(jnp.bfloat16)
    return lax.all_gather(next_rows[None], "mat", axis=0, tiled=True)


def tiles(start, stop):
    return [pl.ds(at, min(TILE, stop - at)) for at in range(start, stop, TILE)]


def starts(blocks):
    return [sum(b.shape[0] for b in blocks[:k]) for k in range(len(blocks) + 1)]


def fetch_blocks(blocks, whole, sems):
    copies = []
    for k, (block, at) in enumerate(zip(blocks, starts(blocks))):
        target = whole.at[pl.ds(at, block.shape[0]), :]
        copies.append(pltpu.make_async_copy(block, target, sems.at[k]))
        copies[k].start()
    return copies


def early_kernel(count, *refs):
    inner, blocks, (gram, cubic, whole, sems) = refs[0], refs[1 : count + 1], refs[count + 1 :]
    left = pl.ds(0, gram.shape[0])

    @pl.when(inner[0] != 0)
    def _():
        copies = fetch_blocks(blocks, whole, sems)
        for at in tiles(0, whole.shape[0]):
            while copies and starts(blocks)[count - len(copies)] < at.start + at.size:
                copies.pop(0).wait()
            gram[:, at] = dot_t(whole[left, :], whole[at, :]).astype(jnp.bfloat16)
        for at in tiles(0, whole.shape[1]):
            cubic[:, at] = dot(gram[...], whole[:, at])


def early_products(inner, rows, blocks):
    count = len(blocks)
    columns = blocks[0].shape[1]
    known = starts(blocks)[-1]
    return pl.pallas_call(
        functools.partial(early_kernel, count),
        out_shape=(
            jax.ShapeDtypeStruct((2 * rows, known), jnp.bfloat16),
            jax.ShapeDtypeStruct((2 * rows, columns), jnp.float32),
        ),
        in_specs=[pl.BlockSpec(memory_space=pltpu.SMEM)]
        + [pl.BlockSpec(memory_space=pltpu.HBM)] * count,
        out_specs=(pl.BlockSpec(memory_space=pltpu.VMEM),) * 2,
        scratch_shapes=[
            pltpu.VMEM((known, columns), jnp.bfloat16),
            pltpu.SemaphoreType.DMA((count,)),
        ],
        compiler_params=pltpu.CompilerParams(vmem_limit_bytes=VMEM_LIMIT),
        cost_estimate=pl.CostEstimate(
            flops=rows * known, bytes_accessed=2 * rows, transcendentals=0
        ),
    )(inner, *blocks)


def late_kernel(early_count, count, own, *refs):
    inner, refs = refs[0], refs[1:]
    blocks, gram_in, cubic_in, refs = refs[:count], refs[count], refs[count + 1], refs[count + 2 :]
    if own:
        outer_poly, out, out_more, outer_more, whole, gram, cubic_sum, cubic, poly, sems = refs
    else:
        out, poly, whole, gram, cubic_sum, cubic, sems = refs
    rows, total = gram.shape
    columns = blocks[0].shape[1]
    begin = starts(blocks)
    known = begin[early_count]
    first = rows if own else 0
    mine = pl.ds(first, rows)
    late = pl.ds(known, total - known)
    mine_poly = pl.ds(first, rows)

    @pl.when(inner[0] != 0)
    def _():
        copies = {}

        def fetch(name, source, target):
            copies[name] = pltpu.make_async_copy(source, target, sems.at[len(copies)])
            copies[name].start()

        def fetch_block(k):
            fetch(k, blocks[k], whole.at[pl.ds(begin[k], blocks[k].shape[0]), :])

        needed = [k for k in range(early_count) if first <= begin[k] < first + rows]
        others = [k for k in range(early_count) if k not in needed]
        for k in needed + list(range(early_count, count)):
            fetch_block(k)
        fetch("gram", gram_in.at[mine, :], gram.at[:, pl.ds(0, known)])
        fetch("cubic", cubic_in.at[mine, :], cubic_sum)
        for k in others:
            fetch_block(k)
        if own:
            fetch("poly", outer_poly, poly.at[pl.ds(0, rows), :])

        for k in needed + list(range(early_count, count)):
            copies[k].wait()
        copies["gram"].wait()
        gram[:, late] = dot_t(whole[mine, :], whole[late, :]).astype(jnp.bfloat16)
        copies["cubic"].wait()
        for at in tiles(0, columns):
            add = dot(gram[:, late], whole[late, at])
            cubic[:, at] = (cubic_sum[:, at] + add).astype(jnp.bfloat16)

        for k in others:
            copies[k].wait()
        for at in tiles(0, total):
            squared = dot_t(cubic[...], whole[at, :])
            poly[mine_poly, at] = (
                coef_b * gram[:, at].astype(jnp.float32) + coef_c * squared
            ).astype(jnp.bfloat16)

        def new(which, at):
            product = dot(poly[which, :], whole[:, at])
            base = whole[which, at].astype(jnp.float32)
            return (coef_a * base + product).astype(jnp.bfloat16)

        half = out.shape[1]
        out[...] = new(mine, pl.ds(0, half))
        if own:
            copies["poly"].wait()
            rest = pl.ds(half, columns - half)
            outer_more[...] = new(pl.ds(0, rows), rest)
            out_more[...] = new(mine, rest)


def late_products(inner, rows, early, late, gram, cubic, outer_poly=None):
    blocks = early + late
    count = len(blocks)
    columns = blocks[0].shape[1]
    total = starts(blocks)[-1]
    own = outer_poly is not None
    half = jax.ShapeDtypeStruct((rows, columns // 2), jnp.bfloat16)
    poly = jax.ShapeDtypeStruct((rows, total), jnp.bfloat16)
    out_shape = (half,) * 3 if own else (half, poly)
    more = [gram, cubic] + ([outer_poly] if own else [])
    scratch = [
        pltpu.VMEM((total, columns), jnp.bfloat16),
        pltpu.VMEM((rows, total), jnp.bfloat16),
        pltpu.VMEM((rows, columns), jnp.float32),
        pltpu.VMEM((rows, columns), jnp.bfloat16),
    ]
    if own:
        scratch.append(pltpu.VMEM((2 * rows, total), jnp.bfloat16))
    return pl.pallas_call(
        functools.partial(late_kernel, len(early), count, own),
        out_shape=out_shape,
        in_specs=[pl.BlockSpec(memory_space=pltpu.SMEM)]
        + [pl.BlockSpec(memory_space=pltpu.HBM)] * count
        + [pl.BlockSpec(memory_space=pl.ANY)] * len(more),
        out_specs=tuple(pl.BlockSpec(memory_space=pltpu.VMEM) for _ in out_shape),
        scratch_shapes=scratch + [pltpu.SemaphoreType.DMA((count + len(more),))],
        compiler_params=pltpu.CompilerParams(vmem_limit_bytes=VMEM_LIMIT),
        cost_estimate=pl.CostEstimate(
            flops=5 * rows * total * columns, bytes_accessed=2 * total * columns, transcendentals=0
        ),
    )(inner, *blocks, *more)


def line_shards(iterate):
    own = iterate[0]
    rows, columns = own.shape
    place = lax.axis_index("shard") // 2
    outer = (place == 0) | (place == 3)
    mat = lax.axis_index("mat")

    inner = jnp.where(outer, 0, 1).astype(jnp.int32)[None]
    tie = lax.optimization_barrier

    other_core = [(2, 3), (3, 2), (4, 5), (5, 4)]
    inwards = [(0, 2), (1, 3), (6, 4), (7, 5)]
    outwards = [(b, a) for a, b in inwards]
    middle = [(2, 4), (3, 5), (4, 2), (5, 3)]
    across_middle = [(0, 4), (1, 5), (6, 2), (7, 3)]
    along_x = [(m, m ^ 1) for m in range(4)]
    along_y = [(m, m ^ 2) for m in range(4)]

    def move(name, block, axis, pairs):
        with jax.named_scope(name):
            return lax.ppermute(block, axis, pairs)

    def swap(name, block):
        return move("swap_" + name, block, "shard", other_core)

    inner_rows = move("middle", own, "shard", middle)
    outer_rows = move("rows_in", own, "shard", inwards)
    cut = rows * 13 // 20
    far_rows = [
        move("rows_far", part, "shard", across_middle) for part in (own[:cut], own[cut:])
    ]

    def kept(block):
        return pltpu.with_memory_space_constraint(block, pltpu.HBM)

    early = [outer_rows, kept(own), kept(swap("own", own)), inner_rows]
    for block, at in ((outer_rows, rows // 2), (inner_rows, rows * 11 // 20)):
        early += [swap("rows", part) for part in (block[:at], block[at:])]
    early[-1] = kept(early[-1])
    gram, cubic = early_products(inner, rows, early)
    far_rows[0], gram, cubic = tie((far_rows[0], gram, cubic))
    swapped = swap("far", far_rows[0])
    late = far_rows + [swapped, swap("far_last", far_rows[1])]
    outer_first, outer_poly = late_products(inner, rows, early, late, gram, cubic)
    own_first, own_second, outer_second = late_products(
        inner, rows, early, late, gram, cubic, outer_poly
    )
    for_outer, for_own = (outer_first, outer_second), (own_first, own_second)

    result = jnp.zeros((4, rows, columns), jnp.bfloat16)

    def place_in(result, flip, at, part):
        return lax.dynamic_update_slice(result, part[None], (mat ^ flip, 0, at))

    width, corner = columns // 2, [None, None]
    for k in (1, 0):
        returned = move("rows_out", for_outer[k], "shard", outwards)
        mine = tie(jnp.where(outer, returned, for_own[k]))
        by_x = move("along_x", mine, "mat", along_x)
        by_y = move("along_y", mine, "mat", along_y)
        by_x, by_y = tie((by_x, by_y))
        corner[k] = (by_y, by_x)[k]
        for flip, part in enumerate((mine, by_x, by_y)):
            result = place_in(result, flip, k * width, part)
    corner = tie(corner)
    corner[0] = move("across_x", corner[0], "mat", along_x)
    corner[1] = move("across_y", corner[1], "mat", along_y)
    result = place_in(result, 3, 0, jnp.concatenate(corner, axis=1))
    return result


def solution(mesh):
    if (mesh.shape["mat"], mesh.shape["shard"]) == (4, 8):
        shards = line_shards
    else:
        shards = general_shards
    return jax.shard_map(
        shards,
        mesh=mesh,
        in_specs=(P("mat", "shard", None),),
        out_specs=P(None, "shard", None),
        check_vma=False,
    )
```

```python
import functools

import jax
import jax.numpy as jnp
from jax import lax
from jax.experimental import pallas as pl
from jax.experimental.pallas import tpu as pltpu
from jax.sharding import PartitionSpec as P

coef_a = 3.4445
coef_b = -4.775
coef_c = 2.0315

TILE = 512
VMEM_LIMIT = 30 * 1024 * 1024


def dot_t(left, right):
    return lax.dot_general(
        left, right, (((1,), (1,)), ((), ())), preferred_element_type=jnp.float32
    )


def dot(left, right):
    return jnp.dot(left, right, preferred_element_type=jnp.float32)


def general_shards(iterate):
    own = iterate[0]
    gathered = lax.all_gather(own, "shard", axis=0, tiled=True)
    gram = dot_t(own, gathered).astype(jnp.bfloat16)
    cubic = dot(gram, gathered).astype(jnp.bfloat16)
    squared = dot_t(cubic, gathered)
    polynomial = (coef_b * gram.astype(jnp.float32) + coef_c * squared).astype(jnp.bfloat16)
    product = dot(polynomial, gathered)
    next_rows = (coef_a * own.astype(jnp.float32) + product).astype(jnp.bfloat16)
    return lax.all_gather(next_rows[None], "mat", axis=0, tiled=True)


def tiles(start, stop):
    return [pl.ds(at, min(TILE, stop - at)) for at in range(start, stop, TILE)]


def starts(blocks):
    return [sum(b.shape[0] for b in blocks[:k]) for k in range(len(blocks) + 1)]


def fetch_blocks(blocks, whole, sems):
    copies = []
    for k, (block, at) in enumerate(zip(blocks, starts(blocks))):
        target = whole.at[pl.ds(at, block.shape[0]), :]
        copies.append(pltpu.make_async_copy(block, target, sems.at[k]))
        copies[k].start()
    return copies


def early_kernel(count, *refs):
    inner, blocks, (gram, cubic, whole, sems) = refs[0], refs[1 : count + 1], refs[count + 1 :]
    left = pl.ds(0, gram.shape[0])

    @pl.when(inner[0] != 0)
    def _():
        copies = fetch_blocks(blocks, whole, sems)
        for at in tiles(0, whole.shape[0]):
            while copies and starts(blocks)[count - len(copies)] < at.start + at.size:
                copies.pop(0).wait()
            gram[:, at] = dot_t(whole[left, :], whole[at, :]).astype(jnp.bfloat16)
        for at in tiles(0, whole.shape[1]):
            cubic[:, at] = dot(gram[...], whole[:, at])


def early_products(inner, rows, blocks):
    count = len(blocks)
    columns = blocks[0].shape[1]
    known = starts(blocks)[-1]
    return pl.pallas_call(
        functools.partial(early_kernel, count),
        out_shape=(
            jax.ShapeDtypeStruct((2 * rows, known), jnp.bfloat16),
            jax.ShapeDtypeStruct((2 * rows, columns), jnp.float32),
        ),
        in_specs=[pl.BlockSpec(memory_space=pltpu.SMEM)]
        + [pl.BlockSpec(memory_space=pltpu.HBM)] * count,
        out_specs=(pl.BlockSpec(memory_space=pltpu.VMEM),) * 2,
        scratch_shapes=[
            pltpu.VMEM((known, columns), jnp.bfloat16),
            pltpu.SemaphoreType.DMA((count,)),
        ],
        compiler_params=pltpu.CompilerParams(vmem_limit_bytes=VMEM_LIMIT),
        cost_estimate=pl.CostEstimate(
            flops=rows * known, bytes_accessed=2 * rows, transcendentals=0
        ),
    )(inner, *blocks)


def late_kernel(early_count, count, own, *refs):
    inner, refs = refs[0], refs[1:]
    blocks, gram_in, cubic_in, refs = refs[:count], refs[count], refs[count + 1], refs[count + 2 :]
    if own:
        outer_poly, out, out_more, outer_more, whole, gram, cubic_sum, cubic, poly, sems = refs
    else:
        out, poly, whole, gram, cubic_sum, cubic, sems = refs
    rows, total = gram.shape
    columns = blocks[0].shape[1]
    begin = starts(blocks)
    known = begin[early_count]
    first = rows if own else 0
    mine = pl.ds(first, rows)
    late = pl.ds(known, total - known)
    mine_poly = pl.ds(first, rows)

    @pl.when(inner[0] != 0)
    def _():
        copies = {}

        def fetch(name, source, target):
            copies[name] = pltpu.make_async_copy(source, target, sems.at[len(copies)])
            copies[name].start()

        def fetch_block(k):
            fetch(k, blocks[k], whole.at[pl.ds(begin[k], blocks[k].shape[0]), :])

        needed = [k for k in range(early_count) if first <= begin[k] < first + rows]
        others = [k for k in range(early_count) if k not in needed]
        for k in needed + list(range(early_count, count)):
            fetch_block(k)
        fetch("gram", gram_in.at[mine, :], gram.at[:, pl.ds(0, known)])
        fetch("cubic", cubic_in.at[mine, :], cubic_sum)
        for k in others:
            fetch_block(k)
        if own:
            fetch("poly", outer_poly, poly.at[pl.ds(0, rows), :])

        for k in needed + list(range(early_count, count)):
            copies[k].wait()
        copies["gram"].wait()
        gram[:, late] = dot_t(whole[mine, :], whole[late, :]).astype(jnp.bfloat16)
        copies["cubic"].wait()
        for at in tiles(0, columns):
            add = dot(gram[:, late], whole[late, at])
            cubic[:, at] = (cubic_sum[:, at] + add).astype(jnp.bfloat16)

        for k in others:
            copies[k].wait()
        for at in tiles(0, total):
            squared = dot_t(cubic[...], whole[at, :])
            poly[mine_poly, at] = (
                coef_b * gram[:, at].astype(jnp.float32) + coef_c * squared
            ).astype(jnp.bfloat16)

        def new(which, at):
            product = dot(poly[which, :], whole[:, at])
            base = whole[which, at].astype(jnp.float32)
            return (coef_a * base + product).astype(jnp.bfloat16)

        half = out.shape[1]
        out[...] = new(mine, pl.ds(0, half))
        if own:
            copies["poly"].wait()
            rest = pl.ds(half, columns - half)
            outer_more[...] = new(pl.ds(0, rows), rest)
            out_more[...] = new(mine, rest)


def late_products(inner, rows, early, late, gram, cubic, outer_poly=None):
    blocks = early + late
    count = len(blocks)
    columns = blocks[0].shape[1]
    total = starts(blocks)[-1]
    own = outer_poly is not None
    half = jax.ShapeDtypeStruct((rows, columns // 2), jnp.bfloat16)
    poly = jax.ShapeDtypeStruct((rows, total), jnp.bfloat16)
    out_shape = (half,) * 3 if own else (half, poly)
    more = [gram, cubic] + ([outer_poly] if own else [])
    scratch = [
        pltpu.VMEM((total, columns), jnp.bfloat16),
        pltpu.VMEM((rows, total), jnp.bfloat16),
        pltpu.VMEM((rows, columns), jnp.float32),
        pltpu.VMEM((rows, columns), jnp.bfloat16),
    ]
    if own:
        scratch.append(pltpu.VMEM((2 * rows, total), jnp.bfloat16))
    return pl.pallas_call(
        functools.partial(late_kernel, len(early), count, own),
        out_shape=out_shape,
        in_specs=[pl.BlockSpec(memory_space=pltpu.SMEM)]
        + [pl.BlockSpec(memory_space=pltpu.HBM)] * count
        + [pl.BlockSpec(memory_space=pl.ANY)] * len(more),
        out_specs=tuple(pl.BlockSpec(memory_space=pltpu.VMEM) for _ in out_shape),
        scratch_shapes=scratch + [pltpu.SemaphoreType.DMA((count + len(more),))],
        compiler_params=pltpu.CompilerParams(vmem_limit_bytes=VMEM_LIMIT),
        cost_estimate=pl.CostEstimate(
            flops=5 * rows * total * columns, bytes_accessed=2 * total * columns, transcendentals=0
        ),
    )(inner, *blocks, *more)


def line_shards(iterate):
    own = iterate[0]
    rows, columns = own.shape
    place = lax.axis_index("shard") // 2
    outer = (place == 0) | (place == 3)
    mat = lax.axis_index("mat")

    inner = jnp.where(outer, 0, 1).astype(jnp.int32)[None]
    tie = lax.optimization_barrier

    other_core = [(2, 3), (3, 2), (4, 5), (5, 4)]
    inwards = [(0, 2), (1, 3), (6, 4), (7, 5)]
    outwards = [(b, a) for a, b in inwards]
    middle = [(2, 4), (3, 5), (4, 2), (5, 3)]
    across_middle = [(0, 4), (1, 5), (6, 2), (7, 3)]
    along_x = [(m, m ^ 1) for m in range(4)]
    along_y = [(m, m ^ 2) for m in range(4)]

    def move(name, block, axis, pairs):
        with jax.named_scope(name):
            return lax.ppermute(block, axis, pairs)

    def swap(name, block):
        return move("swap_" + name, block, "shard", other_core)

    inner_rows = move("middle", own, "shard", middle)
    outer_rows = move("rows_in", own, "shard", inwards)
    cut = rows * 13 // 20
    far_rows = [
        move("rows_far", part, "shard", across_middle) for part in (own[:cut], own[cut:])
    ]

    def kept(block):
        return pltpu.with_memory_space_constraint(block, pltpu.HBM)

    early = [outer_rows, kept(own), kept(swap("own", own)), inner_rows]
    for block, at in ((outer_rows, rows * 11 // 20), (inner_rows, rows // 2)):
        early += [swap("rows", part) for part in (block[:at], block[at:])]
    early[-1] = kept(early[-1])
    gram, cubic = early_products(inner, rows, early)
    far_rows[0], gram, cubic = tie((far_rows[0], gram, cubic))
    swapped = swap("far", far_rows[0])
    late = far_rows + [swapped, swap("far_last", far_rows[1])]
    outer_first, outer_poly = late_products(inner, rows, early, late, gram, cubic)
    own_first, own_second, outer_second = late_products(
        inner, rows, early, late, gram, cubic, outer_poly
    )
    for_outer, for_own = (outer_first, outer_second), (own_first, own_second)

    result = jnp.zeros((4, rows, columns), jnp.bfloat16)

    def place_in(result, flip, at, part):
        return lax.dynamic_update_slice(result, part[None], (mat ^ flip, 0, at))

    width, corner = columns // 2, [None, None]
    for k in (1, 0):
        returned = move("rows_out", for_outer[k], "shard", outwards)
        mine = tie(jnp.where(outer, returned, for_own[k]))
        by_x = move("along_x", mine, "mat", along_x)
        by_y = move("along_y", mine, "mat", along_y)
        by_x, by_y = tie((by_x, by_y))
        corner[k] = (by_y, by_x)[k]
        for flip, part in enumerate((mine, by_x, by_y)):
            result = place_in(result, flip, k * width, part)
    corner = tie(corner)
    corner[0] = move("across_x", corner[0], "mat", along_x)
    corner[1] = move("across_y", corner[1], "mat", along_y)
    result = place_in(result, 3, 0, jnp.concatenate(corner, axis=1))
    return result


def solution(mesh):
    if (mesh.shape["mat"], mesh.shape["shard"]) == (4, 8):
        shards = line_shards
    else:
        shards = general_shards
    return jax.shard_map(
        shards,
        mesh=mesh,
        in_specs=(P("mat", "shard", None),),
        out_specs=P(None, "shard", None),
        check_vma=False,
    )
```
